32 devices in a mesh: dp: 8 (over z, y), head: 4 (over x, core).
Axes of the slice: x: 2, y: 2, z: 4, core: 2. Of those that a mesh axis runs over, the one named last changes fastest.
Arguments:
- tokens: bfloat16 [18432, 768], P(('dp', 'head')), may hold values from -6 to 6
- w_qkv: bfloat16 [3, 768, 768], P(None, None, 'head'), may hold values from -0.21875 to 0.21875
- b_qv: bfloat16 [2, 768], P(None, 'head'), may hold values from -1.796875 to 1.796875
- w_out: bfloat16 [768, 768], P('head'), may hold values from -0.875 to 0.875
- b_out: bfloat16 [768], replicated, may hold values from -1.796875 to 1.796875
- gain_one: bfloat16 [768], replicated, may hold values from 0.5 to 1.5
- shift_one: bfloat16 [768], replicated, may hold values from -1.796875 to 1.796875
- w_in: bfloat16 [768, 3072], replicated, may hold values from -0.21875 to 0.21875
- b_in: bfloat16 [3072], replicated, may hold values from -1.796875 to 1.796875
- w_down: bfloat16 [3072, 768], replicated, may hold values from -0.109375 to 0.109375
- b_down: bfloat16 [768], replicated, may hold values from -1.796875 to 1.796875
- gain_two: bfloat16 [768], replicated, may hold values from 0.5 to 1.5
- shift_two: bfloat16 [768], replicated, may hold values from -1.796875 to 1.796875
- w_term: bfloat16 [768], replicated, may hold values from -0.21875 to 0.21875
- b_term: bfloat16 [1], replicated, may hold values from -3 to 3
- pass_len: int32 [32], P('dp'), may hold values from 40 to 512, as said below
- query_len: int32 [64], P('dp'), may hold values from 8 to 32, as said below
- grad_out: bfloat16 [18432, 768], P(('dp', 'head')), may hold values from -6 to 6
- grad_term: float32 [18432], P(('dp', 'head')), may hold values from -6 to 6
Outputs:
- out: bfloat16 [18432, 768], P(('dp', 'head'))
- term: float32 [18432], P(('dp', 'head'))
- grad_tokens: bfloat16 [18432, 768], P(('dp', 'head'))
- grad_w_qkv: float32 [3, 768, 768], P(None, None, 'head')
- grad_b_qv: float32 [2, 768], P(None, 'head')
- grad_w_out: float32 [768, 768], P('head')
- grad_b_out: float32 [768], replicated
- grad_gain_one: float32 [768], replicated
- grad_shift_one: float32 [768], replicated
- grad_w_in: float32 [768, 3072], P(None, ('dp', 'head'))
- grad_b_in: float32 [3072], replicated
- grad_w_down: float32 [3072, 768], P(('dp', 'head'))
- grad_b_down: float32 [768], replicated
- grad_gain_two: float32 [768], replicated
- grad_shift_two: float32 [768], replicated
- grad_w_term: float32 [768], replicated
- grad_b_term: float32 [1], replicated
The draws below stay inside these ranges and needn't reach their ends.
Inputs may be any that keep to these rules, and one draw needn't show every extreme that they name: `pass_len`: among the passages of each index of dp, one drawn from the seed has length exactly 512. `query_len`: among the queries of each index of dp, one drawn from the seed has length exactly 32.
All inputs are finite; a program needn't handle non-finite values.
Results may differ from the reference program's by a relative error of at most 0.014.
The reference program's roundings to bfloat16 on the way count: a program that leaves them out, or rounds other values in their place, can miss the bound.
Values may be sent and summed in bfloat16 or wider, within the bound.
No kernel may reach another device: no remote copies, remote signals or barrier semaphores. Data moves between devices by JAX's collectives and lax.ppermute only.
A program may use at most 192 MiB of HBM per device.

```python
import math
import jax
import jax.numpy as jnp
from jax import lax

D = 768
HEADS = 12
HEAD_DIM = 64
FF = 3072
PLEN = 512
QLEN = 32
PMIN = 40
QMIN = 8
PASS_DEV = 4
QRY_DEV = 8
E = 768
GROUP = 2304
TOKENS = 18432
N_DP = 8


def full_rows(key, groups, per_group, lowest, highest):
    values = jax.random.randint(key, (groups, per_group), lowest, highest + 1)
    chosen = jax.random.randint(jax.random.fold_in(key, 7), (groups, 1), 0, per_group)
    columns = jnp.arange(per_group, dtype=jnp.int32)[None, :]
    return jnp.where(columns == chosen, highest, values).reshape(-1).astype(jnp.int32)


def draw_pass_len(key, part):
    key = jax.random.fold_in(key, 11)
    return full_rows(key, N_DP, PASS_DEV, PMIN, PLEN)


def draw_query_len(key, part):
    key = jax.random.fold_in(key, 23)
    return full_rows(key, N_DP, QRY_DEV, QMIN, QLEN)


def raised(array, key, source, target, blocks, factor):
    owner, partner = [(jnp.arange(array.shape[axis_at]) // (array.shape[axis_at] // blocks)).reshape([-1 if axis == axis_at else 1 for axis in range(array.ndim)]) for axis_at in (source, target)]
    chosen = jax.random.permutation(key, blocks)[partner]
    strong = (owner == chosen) | (owner == (partner + blocks // 2) % blocks)
    return jnp.where(strong, factor * array, array)


def shard_levels(key, dims, shards, least, high):
    def one(position, blocks):
        heights = jax.random.uniform(jax.random.fold_in(jax.random.fold_in(key, 6), position), (blocks,), jnp.float32, least / len(shards), high / len(shards))
        return jnp.repeat(jnp.exp(heights), dims[position] // blocks).reshape((-1,) + (1,) * (len(dims) - position - 1))

    loudness = one(*shards[0])
    for cut in shards[1:]:
        loudness = loudness * one(*cut)
    return loudness


def bell_draw(rng, extent, scale, bound, cuts=(), kind=jnp.bfloat16):
    array = scale * jax.random.normal(rng, extent, jnp.float32)
    if cuts:
        array = array * shard_levels(rng, extent, cuts, -0.22, 0.18)
    return jnp.clip(array, -bound, bound).astype(kind)


def heavy_noise(key, shape, scale, reach, shards, heavy, kind=jnp.bfloat16):
    drawn = scale * jax.random.normal(key, shape, jnp.float32)
    if shards:
        drawn = drawn * shard_levels(key, shape, shards, -0.22, 0.18)
    return jnp.clip(raised(drawn, jax.random.fold_in(key, 3), *heavy), -reach, reach).astype(kind)


def setup_inputs(seed: int = 0) -> dict:
    key_of = jax.random.split(jax.random.key(seed), 20)
    tokens = bell_draw(key_of[0], (TOKENS, D), 1.0, 6.0, ((0, 32),))
    w_qkv = bell_draw(key_of[1], (3, D, E), D ** -0.5, 0.21875, ((2, 4),))
    b_qv = bell_draw(key_of[2], (2, E), 0.3, 1.796875, ((1, 4),))
    w_out = bell_draw(key_of[3], (E, D), (E // 16) ** -0.5, 0.875, ((0, 4),))
    b_out = bell_draw(key_of[4], (D,), 0.3, 1.796875)
    gain_one = jnp.clip(1.0 + 0.1 * jax.random.normal(key_of[5], (D,), jnp.float32), 0.5, 1.5).astype(jnp.bfloat16)
    shift_one = bell_draw(key_of[6], (D,), 0.3, 1.796875)
    w_in = bell_draw(key_of[7], (D, FF), D ** -0.5, 0.21875)
    b_in = bell_draw(key_of[8], (FF,), 0.3, 1.796875)
    w_down = bell_draw(key_of[9], (FF, D), FF ** -0.5, 0.109375)
    b_down = bell_draw(key_of[10], (D,), 0.3, 1.796875)
    gain_two = jnp.clip(1.0 + 0.1 * jax.random.normal(key_of[11], (D,), jnp.float32), 0.5, 1.5).astype(jnp.bfloat16)
    shift_two = bell_draw(key_of[12], (D,), 0.3, 1.796875)
    w_term = bell_draw(key_of[13], (D,), D ** -0.5, 0.21875)
    b_term = bell_draw(key_of[14], (1,), 1.0, 3.0)
    pass_len = draw_pass_len(jax.random.fold_in(key_of[19], 71), 0)
    query_len = draw_query_len(jax.random.fold_in(key_of[19], 71), 0)
    grad_out = heavy_noise(key_of[17], (TOKENS, D), 1.0, 6.0, ((0, 32),), (0, 1, 32, 2.75))
    grad_term = bell_draw(key_of[18], (TOKENS,), 1.0, 6.0, ((0, 32),), jnp.float32)
    return {"tokens": tokens, "w_qkv": w_qkv, "b_qv": b_qv, "w_out": w_out, "b_out": b_out, "gain_one": gain_one, "shift_one": shift_one, "w_in": w_in, "b_in": b_in, "w_down": w_down, "b_down": b_down, "gain_two": gain_two, "shift_two": shift_two, "w_term": w_term, "b_term": b_term, "pass_len": pass_len, "query_len": query_len, "grad_out": grad_out, "grad_term": grad_term}


@jax.custom_vjp
def low(v):
    return lax.optimization_barrier(v.astype(jnp.bfloat16)).astype(jnp.float32)

@jax.custom_vjp
def low_back(v):
    return v

def low_keep(v):
    return (low(v), None)

def low_pass(kept, grad):
    return (grad,)

def back_keep(v):
    return (v, None)

def back_low(kept, grad):
    return (low(grad),)
low.defvjp(low_keep, low_pass)
low_back.defvjp(back_keep, back_low)

def product(left, right):
    return jnp.dot(left, right, precision=lax.Precision.HIGHEST, preferred_element_type=jnp.float32)

def normalize(hidden, gain, shift):
    center = hidden - lax.optimization_barrier(jnp.mean(hidden, -1, keepdims=True))
    spread = lax.optimization_barrier(jnp.mean(center * center, -1, keepdims=True))
    return center * lax.rsqrt(spread + 1e-06) * gain + shift

def attend(query, keys, values, lengths):
    scores = jnp.einsum('sqhd,skhd->shqk', query, keys, precision=lax.Precision.HIGHEST) * (1.0 / math.sqrt(HEAD_DIM))
    scores = low_back(scores)
    valid = jnp.arange(keys.shape[1], dtype=jnp.int32)[None, :] < lengths[:, None]
    scores = jnp.where(valid[:, None, None, :], scores, -1000000000.0)
    shares = low(jax.nn.softmax(scores, axis=-1))
    mixed = jnp.einsum('shqk,skhd->sqhd', shares, values, precision=lax.Precision.HIGHEST)
    return low_back(low(mixed))

def group_layer(rows, params, pass_group, query_group):
    w_qkv, b_qv, w_out, b_out, gain_one, shift_one, w_in, b_in, w_down, b_down, gain_two, shift_two, w_term, b_term = params
    query = low_back(low(product(rows, w_qkv[0]) + b_qv[0]))
    keys = low_back(low(product(rows, w_qkv[1])))
    values = low_back(low(product(rows, w_qkv[2]) + b_qv[1]))
    split = PASS_DEV * PLEN

    def long_heads(block):
        return block[:split].reshape(PASS_DEV, PLEN, HEADS, HEAD_DIM)

    def short_heads(block):
        return block[split:].reshape(QRY_DEV, QLEN, HEADS, HEAD_DIM)
    long_part = attend(long_heads(query), long_heads(keys), long_heads(values), pass_group)
    short_part = attend(short_heads(query), short_heads(keys), short_heads(values), query_group)
    context = jnp.concatenate([long_part.reshape(split, E), short_part.reshape(QRY_DEV * QLEN, E)], 0)
    attention = low_back(product(context, w_out)) + b_out
    first = normalize(rows + attention, gain_one, shift_one)
    inner = low_back(product(low(first), w_in)) + b_in
    active = low(jax.nn.gelu(inner))
    second = normalize(first + low_back(product(active, w_down)) + b_down, gain_two, shift_two)
    term = jax.nn.softplus(product(second, w_term) + b_term[0])
    return (second, term)

def reference(tokens, w_qkv, b_qv, w_out, b_out, gain_one, shift_one, w_in, b_in, w_down, b_down, gain_two, shift_two, w_term, b_term, pass_len, query_len, grad_out, grad_term):
    params = tuple((member.astype(jnp.float32) for member in (w_qkv, b_qv, w_out, b_out, gain_one, shift_one, w_in, b_in, w_down, b_down, gain_two, shift_two, w_term, b_term)))
    rows = tokens.astype(jnp.float32).reshape(N_DP, GROUP, D)
    pass_groups = pass_len.reshape(N_DP, PASS_DEV)
    query_groups = query_len.reshape(N_DP, QRY_DEV)

    def forward(all_rows, weights):

        def step(carry, item):
            block, pass_group, query_group = item
            return (carry, jax.checkpoint(group_layer)(block, weights, pass_group, query_group))
        carry, results = lax.scan(step, jnp.zeros((), jnp.float32), (all_rows, pass_groups, query_groups))
        return results
    (second, term), pullback = jax.vjp(forward, rows, params)
    grad_rows, grads = pullback((grad_out.astype(jnp.float32).reshape(N_DP, GROUP, D), grad_term.reshape(N_DP, GROUP)))
    return (second.reshape(TOKENS, D).astype(jnp.bfloat16), term.reshape(TOKENS), grad_rows.reshape(TOKENS, D).astype(jnp.bfloat16), grads[0], grads[1], grads[2], grads[3], grads[4], grads[5], grads[6], grads[7], grads[8], grads[9], grads[10], grads[11], grads[12], grads[13])
```

```python
import math

import jax
import jax.numpy as jnp
from jax import lax
from jax.sharding import PartitionSpec as P

HEAD_DIM = 64
PLEN = 512
QLEN = 32
F32 = jnp.float32
BF16 = jnp.bfloat16


def swap(array, axis, bit):
    size = lax.axis_size(axis)
    return lax.ppermute(array, axis, [(at, at ^ bit) for at in range(size)])


def bits_of(size):
    return [1 << at for at in range(size.bit_length() - 1)]


def align(rows, extra):
    heads = lax.axis_size("head")
    me = lax.axis_index("head")
    count = rows.shape[0]
    last = heads - 1
    moved = extra * last
    payload = jnp.where(me == last, rows[count - moved - extra : count - extra], rows[count - moved :])
    received = lax.ppermute(payload, "head", [(at, (at + 1) % heads) for at in range(heads)])
    passage = lax.dynamic_slice_in_dim(
        jnp.concatenate([received, rows], 0), moved - extra * me, count - extra, 0
    )
    query = jnp.where(me == 0, received[:extra], rows[count - extra :])
    for target in range(1, last):
        begin = count - (heads - target) * extra
        sent = lax.ppermute(rows[begin : begin + extra], "head", [(last, target)])
        query = jnp.where(me == target, sent, query)
    return jnp.concatenate([passage, query], 0)


def unalign(rows, extra):
    heads = lax.axis_size("head")
    me = lax.axis_index("head")
    count = rows.shape[0]
    last = heads - 1
    moved = extra * last
    query = rows[count - extra :]
    payload = jnp.where(
        me == 0, jnp.concatenate([query, rows[: moved - extra]], 0), rows[:moved]
    )
    received = lax.ppermute(payload, "head", [((at + 1) % heads, at) for at in range(heads)])
    queries = [received[:extra]]
    for source in range(1, last):
        queries.append(lax.ppermute(query, "head", [(source, last)]))
    queries.append(query)
    tail = jnp.where(
        me == last,
        jnp.concatenate(queries, 0),
        jnp.concatenate([received, query], 0),
    )
    return lax.dynamic_slice_in_dim(
        jnp.concatenate([rows[: count - extra], tail], 0), extra * me, count, 0
    )


def split_three(values):
    high = lax.reduce_precision(values, 8, 7)
    rest = values - high
    middle = lax.reduce_precision(rest, 8, 7)
    return [part.astype(BF16) for part in (high, middle, rest - middle)]


def with_column(rows, values):
    parts = jnp.stack(split_three(values), 1)
    return jnp.concatenate([rows, jnp.pad(parts, ((0, 0), (0, 125)))], 1)


def column_of(rows, width):
    parts = rows[:, width : width + 3].astype(F32)
    return rows[:, :width], parts[:, 0] + (parts[:, 1] + parts[:, 2])


def scatter_sum(current, order):
    axes = dict(order)
    remaining = [name for name, _ in sorted(order, key=lambda item: item[1][2])]
    for name, (axis, bit, _) in order:
        at = remaining.index(name)
        keep = lax.index_in_dim(current, 0, at, keepdims=False)
        send = lax.index_in_dim(current, 1, at, keepdims=False).astype(BF16)
        current = keep + swap(send, axis, bit).astype(F32)
        remaining.remove(name)
    return current


def relative(array, axis, bit, at):
    mine = (lax.axis_index(axis) & bit) != 0
    return jnp.where(mine, jnp.flip(array, at), array)


def attention_scores(query, keys, valid):
    scores = jnp.einsum("qhd,khd->hqk", query, keys, preferred_element_type=F32) * (
        1.0 / math.sqrt(HEAD_DIM)
    )
    return jnp.where(valid[None], scores, -1000000000.0)


def attend(query, keys, values, valid):
    scores = attention_scores(query, keys, valid)
    row_max = jnp.max(scores, -1, keepdims=True)
    exponent = jnp.exp(scores - row_max)
    total = jnp.sum(exponent, -1, keepdims=True)
    shares = (exponent / total).astype(BF16)
    mixed = jnp.einsum("hqk,khd->qhd", shares, values, preferred_element_type=F32).astype(BF16)
    return mixed, row_max + jnp.log(total)


def attend_back(query, keys, values, valid, log_total, grad_mixed):
    scores = attention_scores(query, keys, valid)
    shares = jnp.exp(scores - log_total)
    grad_shares = jnp.einsum("qhd,khd->hqk", grad_mixed, values, preferred_element_type=F32)
    grad_values = jnp.einsum(
        "hqk,qhd->khd", shares.astype(BF16), grad_mixed, preferred_element_type=F32
    ).astype(BF16)
    inner = jnp.sum(shares * grad_shares, -1, keepdims=True)
    grad_scores = (shares * (grad_shares - inner)).astype(BF16)
    scale = 1.0 / math.sqrt(HEAD_DIM)
    grad_query = jnp.einsum("hqk,khd->qhd", grad_scores, keys, preferred_element_type=F32) * scale
    grad_keys = jnp.einsum("hqk,qhd->khd", grad_scores, query, preferred_element_type=F32) * scale
    return grad_query.astype(BF16), grad_keys.astype(BF16), grad_values


def normalize(hidden, gain, shift):
    center = hidden - jnp.mean(hidden, -1, keepdims=True)
    inverse = lax.rsqrt(jnp.mean(center * center, -1, keepdims=True) + 1e-06)
    unit = center * inverse
    return (unit * gain + shift, unit, inverse)


def normalize_back(grad, unit, inverse, gain):
    grad_unit = grad * gain
    return inverse * (
        grad_unit
        - jnp.mean(grad_unit, -1, keepdims=True)
        - unit * jnp.mean(grad_unit * unit, -1, keepdims=True)
    )


def shards(
    tokens, w_qkv, b_qv, w_out, b_out, gain_one, shift_one, w_in, b_in, w_down, b_down,
    gain_two, shift_two, w_term, b_term, pass_len, query_len, grad_out, grad_term,
):
    n_dp, n_head = lax.axis_size("dp"), lax.axis_size("head")
    me = lax.axis_index("head")
    width = tokens.shape[1]
    wide = w_qkv.shape[2]
    hidden = w_in.shape[1]
    extra = query_len.shape[0] * QLEN // n_head
    split = PLEN

    own_pack = jnp.concatenate([w_qkv.transpose(0, 2, 1).reshape(3 * wide, width), w_out], 0)
    rows = align(tokens, extra)
    packs = [own_pack, swap(own_pack, "head", 1)]
    packs.append(swap(own_pack, "head", 2))
    packs.append(swap(packs[2], "head", 1))
    bias = jnp.concatenate([b_qv, jnp.zeros_like(b_qv)], 0).reshape(1, -1)
    all_bias = lax.all_to_all(
        jnp.tile(b_qv.reshape(1, 2, wide), (n_head, 1, 1)), "head", 0, 0, tiled=True
    )
    length = lax.dynamic_index_in_dim(pass_len, me, 0, keepdims=False)
    each = query_len.shape[0] // n_head
    lengths = lax.dynamic_slice_in_dim(query_len, me * each, each, 0)
    long_valid = jnp.broadcast_to(
        jnp.arange(PLEN, dtype=jnp.int32)[None, :] < length, (PLEN, PLEN)
    )
    place = jnp.arange(extra, dtype=jnp.int32)
    short_valid = (place[:, None] // QLEN == place[None, :] // QLEN) & (
        place[None, :] % QLEN < lengths[place // QLEN][None, :]
    )
    grads_in = align(with_column(grad_out, grad_term), extra)

    saved = []
    attention = b_out.astype(F32)[None, :]
    for part in range(n_head):
        pack = packs[part]
        owner_bias = lax.dynamic_index_in_dim(all_bias, me ^ part, 0, keepdims=False).astype(F32)
        both = jnp.einsum("td,ed->te", rows, pack[: 3 * wide], preferred_element_type=F32)
        query = (both[:, :wide] + owner_bias[0]).astype(BF16).reshape(-1, wide // HEAD_DIM, HEAD_DIM)
        keys = both[:, wide : 2 * wide].astype(BF16).reshape(-1, wide // HEAD_DIM, HEAD_DIM)
        values = (both[:, 2 * wide :] + owner_bias[1]).astype(BF16).reshape(
            -1, wide // HEAD_DIM, HEAD_DIM
        )
        long_mixed, long_total = attend(query[:split], keys[:split], values[:split], long_valid)
        short_mixed, short_total = attend(query[split:], keys[split:], values[split:], short_valid)
        mixed = jnp.concatenate([long_mixed, short_mixed], 0).reshape(-1, wide)
        attention = attention + jnp.dot(mixed, pack[3 * wide :], preferred_element_type=F32)
        saved.append((query, keys, values, mixed, long_total, short_total))

    gain_first = gain_one.astype(F32)
    gain_second = gain_two.astype(F32)
    residual = rows.astype(F32) + attention
    first, first_unit, first_inverse = normalize(residual, gain_first, shift_one.astype(F32))
    first_low = first.astype(BF16)
    inner = jnp.dot(first_low, w_in, preferred_element_type=F32) + b_in.astype(F32)
    active, gelu_back = jax.vjp(jax.nn.gelu, inner)
    active_low = active.astype(BF16)
    second_in = (
        first + jnp.dot(active_low, w_down, preferred_element_type=F32) + b_down.astype(F32)
    )
    second, second_unit, second_inverse = normalize(second_in, gain_second, shift_two.astype(F32))
    term_weight = w_term.astype(F32)
    logit = jnp.sum(second * term_weight[None, :], -1) + b_term.astype(F32)[0]
    term = jax.nn.softplus(logit)
    rows_out = unalign(with_column(second.astype(BF16), term), extra)
    out, term = column_of(rows_out, width)

    grad_second, grad_weight = column_of(grads_in, width)
    grad_logit = grad_weight * jax.nn.sigmoid(logit)
    grad_w_term = jnp.sum(grad_logit[:, None] * second, 0)
    grad_b_term = jnp.sum(grad_logit)[None]
    grad_second = grad_second.astype(F32) + grad_logit[:, None] * term_weight[None, :]
    grad_gain_two = jnp.sum(grad_second * second_unit, 0)
    grad_shift_two = jnp.sum(grad_second, 0)
    grad_middle = normalize_back(grad_second, second_unit, second_inverse, gain_second)
    grad_b_down = jnp.sum(grad_middle, 0)
    grad_middle_low = grad_middle.astype(BF16)

    def owned(grad):
        dp_bits = bits_of(n_dp)[::-1]
        shape = [2] * len(dp_bits) + [2, 2]
        current = grad.reshape(*shape, hidden // (n_dp * n_head), width)
        for at, bit in enumerate(dp_bits):
            current = relative(current, "dp", bit, at)
        current = relative(current, "head", 2, len(dp_bits))
        return relative(current, "head", 1, len(dp_bits) + 1)

    stages = {}
    for at, bit in enumerate(bits_of(n_dp)[::-1]):
        stages["dp%d" % bit] = ("dp", bit, at)
    stages["x"] = ("head", 2, len(stages))
    stages["core"] = ("head", 1, len(stages))
    dp_names = ["dp%d" % bit for bit in bits_of(n_dp)]
    order_x = [(name, stages[name]) for name in ["core", "x"] + dp_names]
    order_y = [(name, stages[name]) for name in ["core", dp_names[0], "x"] + dp_names[1:]]

    grad_w_down = jnp.einsum("tf,td->fd", active_low, grad_middle_low, preferred_element_type=F32)
    grad_w_down = scatter_sum(owned(grad_w_down), order_x)
    grad_active = jnp.einsum("td,fd->tf", grad_middle_low, w_down, preferred_element_type=F32)
    grad_inner = gelu_back(grad_active)[0]
    grad_b_in = jnp.sum(grad_inner, 0)
    grad_inner_low = grad_inner.astype(BF16)
    grad_w_in = jnp.einsum("tf,td->fd", grad_inner_low, first_low, preferred_element_type=F32)
    grad_w_in = scatter_sum(owned(grad_w_in), order_y).T
    grad_first = grad_middle + jnp.einsum(
        "tf,df->td", grad_inner_low, w_in, preferred_element_type=F32
    )
    grad_gain_one = jnp.sum(grad_first * first_unit, 0)
    grad_shift_one = jnp.sum(grad_first, 0)
    grad_residual = normalize_back(grad_first, first_unit, first_inverse, gain_first)
    grad_b_out = jnp.sum(grad_residual, 0)
    grad_attention = grad_residual.astype(BF16)

    sums = [
        grad_b_out, grad_gain_one, grad_shift_one, grad_b_in, grad_b_down, grad_gain_two,
        grad_shift_two, grad_w_term, jnp.pad(grad_b_term, (0, 127)),
    ]
    sizes = [member.shape[0] for member in sums]
    vector = jnp.concatenate(sums)
    for axis, bit in [("head", 1), ("head", 2)] + [("dp", bit) for bit in bits_of(n_dp)]:
        vector = vector + swap(vector, axis, bit)
    cuts = [sum(sizes[:at]) for at in range(1, len(sizes))]
    vectors = jnp.split(vector, cuts)

    grad_packs, grad_biases = [None] * n_head, [None] * n_head
    grad_rows = grad_residual
    for part in (3, 2, 1, 0):
        pack = packs[part]
        query, keys, values, mixed, long_total, short_total = saved[part]
        grad_mixed = jnp.einsum(
            "td,ed->te", grad_attention, pack[3 * wide :], preferred_element_type=F32
        ).astype(BF16).reshape(-1, wide // HEAD_DIM, HEAD_DIM)
        long_grads = attend_back(
            query[:split], keys[:split], values[:split], long_valid, long_total, grad_mixed[:split]
        )
        short_grads = attend_back(
            query[split:], keys[split:], values[split:], short_valid, short_total, grad_mixed[split:]
        )
        grads = jnp.concatenate(
            [
                jnp.concatenate([long_grads[at], short_grads[at]], 0).reshape(-1, wide)
                for at in range(3)
            ],
            1,
        )
        grad_biases[part] = jnp.stack(
            [
                jnp.sum(grads[:, :wide], 0, dtype=F32),
                jnp.sum(grads[:, 2 * wide :], 0, dtype=F32),
            ]
        )
        grad_packs[part] = jnp.concatenate(
            [
                jnp.einsum("te,td->ed", grads, rows, preferred_element_type=F32),
                jnp.einsum("te,td->ed", mixed, grad_attention, preferred_element_type=F32),
            ],
            0,
        )
        grad_rows = grad_rows + jnp.dot(grads, pack[: 3 * wide], preferred_element_type=F32)
    grad_tokens = unalign(grad_rows.astype(BF16), extra)

    far = grad_packs[2] + swap(grad_packs[3].astype(BF16), "head", 1).astype(F32)
    near = grad_packs[0] + swap(grad_packs[1].astype(BF16), "head", 1).astype(F32)
    block = near + swap(far.astype(BF16), "head", 2).astype(F32)
    far_bias = grad_biases[2] + swap(grad_biases[3], "head", 1)
    near_bias = grad_biases[0] + swap(grad_biases[1], "head", 1)
    grad_b_qv = near_bias + swap(far_bias, "head", 2)
    for bit in bits_of(n_dp):
        grad_b_qv = grad_b_qv + swap(grad_b_qv, "dp", bit)
    me_dp = lax.axis_index("dp")
    for bit in bits_of(n_dp):
        half = block.shape[0] // 2
        side = ((me_dp & bit) != 0).astype(jnp.int32)
        keep = lax.dynamic_slice_in_dim(block, side * half, half, 0)
        send = lax.dynamic_slice_in_dim(block, (1 - side) * half, half, 0).astype(BF16)
        block = keep + swap(send, "dp", bit).astype(F32)
    block = block.astype(BF16)
    for bit in bits_of(n_dp)[::-1]:
        other = swap(block, "dp", bit)
        mine = (me_dp & bit) != 0
        block = jnp.where(
            mine, jnp.concatenate([other, block], 0), jnp.concatenate([block, other], 0)
        )
    block = block.astype(F32)
    grad_w_qkv = block[: 3 * wide].reshape(3, wide, width).transpose(0, 2, 1)
    grad_w_out = block[3 * wide :]
    return (
        out, term, grad_tokens, grad_w_qkv, grad_b_qv, grad_w_out, vectors[0], vectors[1],
        vectors[2], grad_w_in, vectors[3], grad_w_down, vectors[4], vectors[5], vectors[6],
        vectors[7], vectors[8][:1],
    )


def solution(mesh):
    both = ("dp", "head")
    placed = (
        P(both, None), P(None, None, "head"), P(None, "head"), P("head", None),
        P(), P(), P(), P(), P(), P(), P(), P(), P(), P(), P(),
        P("dp"), P("dp"), P(both, None), P(both),
    )
    return jax.shard_map(
        shards,
        mesh=mesh,
        in_specs=placed,
        out_specs=(
            P(both, None), P(both), P(both, None), P(None, None, "head"), P(None, "head"),
            P("head", None), P(), P(), P(), P(None, both), P(), P(both, None),
            P(), P(), P(), P(), P(),
        ),
        check_vma=False,
    )
```

```python
import functools
import math

import jax
import jax.numpy as jnp
from jax import lax
from jax.experimental import pallas as pl
from jax.experimental.pallas import tpu as pltpu
from jax.sharding import PartitionSpec as P

HEAD_DIM = 64
PLEN = 512
QLEN = 32
F32 = jnp.float32
BF16 = jnp.bfloat16
BLOCK = 384
NN = (((1,), (0,)), ((), ()))
NT = (((1,), (1,)), ((), ()))
TN = (((0,), (0,)), ((), ()))
SCALE = 1.0 / math.sqrt(HEAD_DIM)
LIMIT = 56 * 1024 * 1024


def mm(left, right, dims):
    return lax.dot_general(left, right, dims, preferred_element_type=F32)


def full(array):
    zeros = (0,) * array.ndim
    return pl.BlockSpec(array.shape, lambda *_: zeros)


def whole(shape):
    zeros = (0,) * len(shape)
    return pl.BlockSpec(shape, lambda *_: zeros)


def masks(lengths_ref, extra):
    long_key = lax.broadcasted_iota(jnp.int32, (PLEN, PLEN), 0)
    key = lax.broadcasted_iota(jnp.int32, (extra, extra), 0)
    row = lax.broadcasted_iota(jnp.int32, (extra, extra), 1)
    short = jnp.zeros((extra, extra), jnp.bool_)
    for at in range(extra // QLEN):
        low, high = at * QLEN, (at + 1) * QLEN
        short = short | (
            (key >= low) & (key < low + lengths_ref[1 + at]) & (row >= low) & (row < high)
        )
    return long_key < lengths_ref[0], short


def attend_kernel(lengths_ref, x_ref, pack_ref, qkv_ref, mixed_ref, total_ref):
    wide = mixed_ref.shape[0]
    count = x_ref.shape[0]
    extra = count - PLEN
    ones = jnp.ones((16, count), BF16)
    weight = pack_ref[: 3 * wide, :]
    all_qkv = mm(weight, x_ref[...], NT)
    bias_q = mm(pack_ref[4 * wide :, :wide], ones, TN)
    bias_v = mm(pack_ref[4 * wide :, 256 : 256 + wide], ones, TN)
    qkv_ref[:wide, :] = (all_qkv[:wide] + bias_q).astype(BF16) * BF16(SCALE)
    qkv_ref[wide : 2 * wide, :] = all_qkv[wide : 2 * wide].astype(BF16)
    qkv_ref[2 * wide :, :] = (all_qkv[2 * wide :] + bias_v).astype(BF16)
    total_ref[...] = jnp.zeros_like(total_ref)
    valids = masks(lengths_ref, extra)
    for head in range(wide // HEAD_DIM):
        at = head * HEAD_DIM
        for valid, low, high in ((valids[0], 0, PLEN), (valids[1], PLEN, count)):
            query = qkv_ref[at : at + HEAD_DIM, low:high]
            keys = qkv_ref[wide + at : wide + at + HEAD_DIM, low:high]
            values = qkv_ref[2 * wide + at : 2 * wide + at + HEAD_DIM, low:high]
            scores = jnp.where(valid, mm(keys, query, TN), -1000000000.0)
            top = jnp.max(scores, 0, keepdims=True)
            exponent = jnp.exp(scores - top)
            total = jnp.sum(exponent, 0, keepdims=True)
            shares = (exponent * (1.0 / total)).astype(BF16)
            mixed_ref[at : at + HEAD_DIM, low:high] = mm(values, shares, NN).astype(BF16)
            total_ref[head : head + 1, low:high] = top + jnp.log(total)


def attend(lengths, x, pack, wide):
    count = x.shape[0]
    shapes = [
        jax.ShapeDtypeStruct((3 * wide, count), BF16),
        jax.ShapeDtypeStruct((wide, count), BF16),
        jax.ShapeDtypeStruct((8, count), F32),
    ]
    return pl.pallas_call(
        attend_kernel,
        out_shape=shapes,
        in_specs=[pl.BlockSpec(memory_space=pltpu.SMEM)] + [pl.BlockSpec(memory_space=pltpu.VMEM)] * 2,
        out_specs=[pl.BlockSpec(memory_space=pltpu.VMEM)] * 3,
        compiler_params=pltpu.CompilerParams(vmem_limit_bytes=LIMIT),
        cost_estimate=pl.CostEstimate(flops=1_200_000_000, bytes_accessed=4_000_000, transcendentals=800_000),
        name="attend",
    )(lengths, x, pack)


def attend_back_kernel(
    lengths_ref, x_ref, pack_ref, da_ref, qkv_ref, total_ref, mixed_ref, grad_ref, weight_ref, bias_ref
):
    wide = mixed_ref.shape[0]
    count = x_ref.shape[0]
    extra = count - PLEN
    grad_mixed = mm(pack_ref[3 * wide : 4 * wide, :], da_ref[...], NT).astype(BF16)
    weight_ref[3 * wide : 4 * wide, :] = mm(mixed_ref[...], da_ref[...], NN).astype(weight_ref.dtype)
    valids = masks(lengths_ref, extra)
    for head in range(wide // HEAD_DIM):
        at = head * HEAD_DIM
        for valid, low, high in ((valids[0], 0, PLEN), (valids[1], PLEN, count)):
            query = qkv_ref[at : at + HEAD_DIM, low:high]
            keys = qkv_ref[wide + at : wide + at + HEAD_DIM, low:high]
            values = qkv_ref[2 * wide + at : 2 * wide + at + HEAD_DIM, low:high]
            upper = grad_mixed[at : at + HEAD_DIM, low:high]
            scores = jnp.where(valid, mm(keys, query, TN), -1000000000.0)
            shares = jnp.exp(scores - total_ref[head : head + 1, low:high])
            grad_shares = mm(values, upper, TN)
            inner = jnp.sum(shares * grad_shares, 0, keepdims=True)
            grad_scores = (shares * (grad_shares - inner)).astype(BF16)
            grad_ref[2 * wide + at : 2 * wide + at + HEAD_DIM, low:high] = mm(
                upper, shares.astype(BF16), NT
            ).astype(BF16)
            grad_ref[wide + at : wide + at + HEAD_DIM, low:high] = mm(query, grad_scores, NT).astype(BF16)
            grad_ref[at : at + HEAD_DIM, low:high] = (mm(keys, grad_scores, NN) * SCALE).astype(BF16)
    weight_ref[: 3 * wide, :] = mm(grad_ref[...], x_ref[...], NN).astype(weight_ref.dtype)
    bias_ref[...] = mm(jnp.ones((8, count), BF16), grad_ref[...], NT)


def attend_back(lengths, x, pack, da, qkv, total, mixed, dtype):
    wide, count = mixed.shape
    shapes = [
        jax.ShapeDtypeStruct((3 * wide, count), BF16),
        jax.ShapeDtypeStruct((4 * wide, x.shape[1]), dtype),
        jax.ShapeDtypeStruct((8, 3 * wide), F32),
    ]
    return pl.pallas_call(
        attend_back_kernel,
        out_shape=shapes,
        in_specs=[pl.BlockSpec(memory_space=pltpu.SMEM)] + [pl.BlockSpec(memory_space=pltpu.VMEM)] * 6,
        out_specs=[pl.BlockSpec(memory_space=pltpu.VMEM)] * 3,
        compiler_params=pltpu.CompilerParams(vmem_limit_bytes=LIMIT),
        cost_estimate=pl.CostEstimate(flops=3_000_000_000, bytes_accessed=7_000_000, transcendentals=800_000),
        name="attend_back",
    )(lengths, x, pack, da, qkv, total, mixed)


def rows_kernel(*refs):
    parts = (len(refs) - 2) // 2
    base_ref, out_ref = refs[0], refs[-1]
    total = base_ref[...]
    for part in range(parts):
        total = total + mm(refs[1 + part][...], refs[1 + parts + part][...], TN)
    out_ref[...] = total.astype(BF16)


def rows_back(base, grads, packs):
    wide = grads[0].shape[0]
    specs = [full(base)] + [full(g) for g in grads]
    specs += [pl.BlockSpec((wide, p.shape[1]), lambda *_: (0, 0)) for p in packs]
    return pl.pallas_call(
        rows_kernel,
        grid=(1,),
        out_shape=jax.ShapeDtypeStruct(base.shape, BF16),
        in_specs=specs,
        out_specs=full(base),
        compiler_params=pltpu.CompilerParams(vmem_limit_bytes=LIMIT),
        cost_estimate=pl.CostEstimate(flops=2_000_000_000, bytes_accessed=9_000_000, transcendentals=0),
        name="rows_back",
    )(base, *grads, *packs)


def normed(hidden):
    center = hidden - jnp.mean(hidden, -1, keepdims=True)
    inverse = lax.rsqrt(jnp.mean(center * center, -1, keepdims=True) + 1e-06)
    return center * inverse, inverse


def norm_back(grad, unit, inverse, gain):
    grad_unit = grad * gain
    return inverse * (
        grad_unit
        - jnp.mean(grad_unit, -1, keepdims=True)
        - unit * jnp.mean(grad_unit * unit, -1, keepdims=True)
    )


def column_sum(values):
    return jnp.sum(values, 0, keepdims=True)


def forward_kernel(parts, *refs):
    x_ref, params_ref, grads_ref, bias_ref, w_in_ref, w_down_ref = refs[:6]
    mixed_refs = refs[6 : 6 + parts]
    out_refs = refs[6 + parts : 6 + 2 * parts]
    r1_ref, a1_ref, g_ref, slope_ref, out_ref, db_ref, dr2_ref, vec_ref = refs[6 + 2 * parts : -2]
    first_ref, sum_ref = refs[-2:]
    step, steps = pl.program_id(0), pl.num_programs(0)
    width = x_ref.shape[1]

    def param(at):
        return params_ref[at : at + 1, :].astype(F32)

    @pl.when(step == 0)
    def _():
        total = x_ref[...].astype(F32) + param(0)
        for part in range(parts):
            total = total + mm(mixed_refs[part][...], out_refs[part][...], TN)
        r1_ref[...] = total
        unit, _ = normed(total)
        first = unit * param(1) + param(2)
        first_ref[...] = first
        a1_ref[...] = first.astype(BF16)
        sum_ref[...] = jnp.zeros_like(sum_ref)

    inner = mm(a1_ref[...], w_in_ref[...], NN) + bias_ref[...].astype(F32)
    square = inner * inner
    factor = math.sqrt(2.0 / math.pi)
    tanh = jnp.tanh(factor * (inner + 0.044715 * (square * inner)))
    half = 0.5 * (1.0 + tanh)
    active = (inner * half).astype(BF16)
    g_ref[...] = active
    slope_ref[...] = half + (0.5 * factor) * inner * (1.0 - tanh * tanh) * (1.0 + (3 * 0.044715) * square)
    sum_ref[...] += mm(active, w_down_ref[...], NN)

    @pl.when(step == steps - 1)
    def _():
        unit, inverse = normed(first_ref[...] + sum_ref[...] + param(3))
        gain = param(4)
        second = unit * gain + param(5)
        weight = param(6)
        logit = jnp.sum(second * weight, -1, keepdims=True) + params_ref[7:8, 0:1].astype(F32)
        term = jnp.maximum(logit, 0.0) + jnp.log1p(jnp.exp(-jnp.abs(logit)))
        sigmoid = 1.0 / (1.0 + jnp.exp(-logit))
        lane = lax.broadcasted_iota(jnp.int32, (term.shape[0], 128), 1)
        high = term.astype(BF16).astype(F32)
        middle = (term - high).astype(BF16).astype(F32)
        rest = term - high - middle
        tail = jnp.where(lane == 0, high, jnp.where(lane == 1, middle, jnp.where(lane == 2, rest, 0.0)))
        out_ref[:, :width] = second.astype(BF16)
        out_ref[:, width:] = tail.astype(BF16)
        grad_term = jnp.sum(grads_ref[:, width:].astype(F32), -1, keepdims=True)
        grad_logit = grad_term * sigmoid
        grad = grads_ref[:, :width].astype(F32) + grad_logit * weight
        back = norm_back(grad, unit, inverse, gain)
        db_ref[...] = back.astype(BF16)
        dr2_ref[...] = back
        vec_ref[...] = jnp.zeros_like(vec_ref)
        vec_ref[0:1, :] = column_sum(grad * unit)
        vec_ref[1:2, :] = column_sum(grad)
        vec_ref[2:3, :] = column_sum(back)
        vec_ref[3:4, :] = column_sum(grad_logit * second)
        vec_ref[4:5, :] = jnp.broadcast_to(column_sum(grad_logit), (1, width))


def forward(x, params, grads, b_in, w_in, w_down, mixed, packs):
    count, width = x.shape
    hidden = w_in.shape[1]
    wide = mixed[0].shape[0]
    specs = [
        full(x), full(params), full(grads),
        pl.BlockSpec((1, BLOCK), lambda j: (0, j)),
        pl.BlockSpec((width, BLOCK), lambda j: (0, j)),
        pl.BlockSpec((BLOCK, width), lambda j: (j, 0)),
    ]
    specs += [full(m) for m in mixed]
    specs += [pl.BlockSpec((wide, width), lambda j: (3, 0)) for _ in packs]
    shapes = [
        ((count, width), F32), ((count, width), BF16), ((count, hidden), BF16), ((count, hidden), F32),
        ((count, width + 128), BF16), ((count, width), BF16), ((count, width), F32), ((8, width), F32),
    ]
    out_specs = [whole(s) for s, _ in shapes]
    for at in (2, 3):
        out_specs[at] = pl.BlockSpec((count, BLOCK), lambda j: (0, j))
    return pl.pallas_call(
        functools.partial(forward_kernel, len(mixed)),
        grid=(hidden // BLOCK,),
        out_shape=[jax.ShapeDtypeStruct(s, d) for s, d in shapes],
        in_specs=specs,
        out_specs=out_specs,
        scratch_shapes=[pltpu.VMEM((count, width), F32), pltpu.VMEM((count, width), F32)],
        compiler_params=pltpu.CompilerParams(vmem_limit_bytes=LIMIT),
        cost_estimate=pl.CostEstimate(flops=6_200_000_000, bytes_accessed=30_000_000, transcendentals=2_000_000),
        name="forward",
    )(x, params, grads, b_in, w_in, w_down, *mixed, *packs)


def put_owned(me_ref, tile_ref, send_ref, keep_ref):
    block = send_ref.shape[2]
    for far in (0, 1):
        mine = me_ref[1] ^ (2 * far)
        keep_ref[far, 0] = tile_ref[pl.ds(pl.multiple_of(mine * block, block), block), :]
        send_ref[far, 0] = tile_ref[pl.ds(pl.multiple_of((mine ^ 1) * block, block), block), :].astype(BF16)


def down_kernel(owners, me_ref, g_ref, db_ref, *refs):
    tile = mm(g_ref[...], db_ref[...], TN)
    if owners:
        refs[2][...] = tile
        put_owned(me_ref, refs[2], refs[0], refs[1])
    else:
        refs[0][...] = tile


def owner_outputs(owners, hidden, width):
    if not owners:
        return [((hidden, width), F32)], [pl.BlockSpec((BLOCK, width), lambda j, me: (j, 0))], []
    n_dp = hidden // BLOCK
    shape = (2, n_dp, BLOCK // 4, width)
    spec = pl.BlockSpec((2, 1, BLOCK // 4, width), lambda j, me: (0, j, 0, 0))
    return [(shape, BF16), (shape, F32)], [spec, spec], [pltpu.VMEM((BLOCK, width), F32)]


def down_back(owners, me, g, db):
    count, hidden = g.shape
    width = db.shape[1]
    shapes, out_specs, scratch = owner_outputs(owners, hidden, width)
    return pl.pallas_call(
        functools.partial(down_kernel, owners),
        out_shape=[jax.ShapeDtypeStruct(s, d) for s, d in shapes],
        grid_spec=pltpu.PrefetchScalarGridSpec(
            num_scalar_prefetch=1,
            grid=(hidden // BLOCK,),
            in_specs=[pl.BlockSpec((count, BLOCK), lambda j, me: (0, me[0] ^ j)), full(db)],
            out_specs=out_specs,
            scratch_shapes=scratch,
        ),
        compiler_params=pltpu.CompilerParams(vmem_limit_bytes=LIMIT),
        cost_estimate=pl.CostEstimate(flops=2_700_000_000, bytes_accessed=12_000_000, transcendentals=0),
        name="down_back",
    )(me, g, db)


def backward_kernel(
    owners, me_ref, db_ref, slope_ref, w_down_ref, w_in_ref, a1_ref, r1_ref, dr2_ref, params_ref, vec_ref,
    dr1_ref, da_ref, out_vec_ref, b_in_ref, *refs
):
    step, steps = pl.program_id(0), pl.num_programs(0)
    sum_ref = refs[-1]

    @pl.when(step == 0)
    def _():
        sum_ref[...] = dr2_ref[...]

    grad_inner = mm(db_ref[...], w_down_ref[...], NT) * slope_ref[...]
    b_in_ref[pl.ds(me_ref[0] ^ step, 1), :] = column_sum(grad_inner)
    low = grad_inner.astype(BF16)
    sum_ref[...] += mm(low, w_in_ref[...], NT)
    tile = mm(low, a1_ref[...], TN)
    if owners:
        refs[2][...] = tile
        put_owned(me_ref, refs[2], refs[0], refs[1])
    else:
        refs[0][...] = tile

    @pl.when(step == steps - 1)
    def _():
        grad = sum_ref[...]
        unit, inverse = normed(r1_ref[...])
        back = norm_back(grad, unit, inverse, params_ref[1:2, :].astype(F32))
        dr1_ref[...] = back
        da_ref[...] = back.astype(BF16)
        out_vec_ref[:8, :] = vec_ref[...]
        out_vec_ref[8:, :] = jnp.zeros_like(vec_ref)
        out_vec_ref[8:9, :] = column_sum(grad * unit)
        out_vec_ref[9:10, :] = column_sum(grad)
        out_vec_ref[10:11, :] = column_sum(back)


def backward(owners, me, db, slope, w_down, w_in, a1, r1, dr2, params, vec):
    count, width = db.shape
    hidden = w_in.shape[1]
    shapes, out_specs, scratch = owner_outputs(owners, hidden, width)
    steps = hidden // BLOCK
    firsts = [((count, width), F32), ((count, width), BF16), ((16, width), F32), ((steps, BLOCK), F32)]
    return pl.pallas_call(
        functools.partial(backward_kernel, owners),
        out_shape=[jax.ShapeDtypeStruct(s, d) for s, d in firsts + shapes],
        grid_spec=pltpu.PrefetchScalarGridSpec(
            num_scalar_prefetch=1,
            grid=(steps,),
            in_specs=[
                full(db),
                pl.BlockSpec((count, BLOCK), lambda j, me: (0, me[0] ^ j)),
                pl.BlockSpec((BLOCK, width), lambda j, me: (me[0] ^ j, 0)),
                pl.BlockSpec((width, BLOCK), lambda j, me: (0, me[0] ^ j)),
                full(a1), full(r1), full(dr2), full(params), full(vec),
            ],
            out_specs=[whole(s) for s, _ in firsts] + out_specs,
            scratch_shapes=scratch + [pltpu.VMEM((count, width), F32)],
        ),
        compiler_params=pltpu.CompilerParams(vmem_limit_bytes=LIMIT),
        cost_estimate=pl.CostEstimate(flops=8_200_000_000, bytes_accessed=40_000_000, transcendentals=0),
        name="backward",
    )(me, db, slope, w_down, w_in, a1, r1, dr2, params, vec)


def swap(array, axis, bit):
    size = lax.axis_size(axis)
    return lax.ppermute(array, axis, [(at, at ^ bit) for at in range(size)])


def bits_of(size):
    return [1 << at for at in range(size.bit_length() - 1)]


def align(rows, extra):
    heads = lax.axis_size("head")
    me = lax.axis_index("head")
    count = rows.shape[0]
    last = heads - 1
    moved = extra * last
    payload = jnp.where(me == last, rows[count - moved - extra : count - extra], rows[count - moved :])
    received = lax.ppermute(payload, "head", [(at, (at + 1) % heads) for at in range(heads)])
    passage = lax.dynamic_slice_in_dim(
        jnp.concatenate([received, rows], 0), moved - extra * me, count - extra, 0
    )
    query = jnp.where(me == 0, received[:extra], rows[count - extra :])
    for target in range(1, last):
        begin = count - (heads - target) * extra
        sent = lax.ppermute(rows[begin : begin + extra], "head", [(last, target)])
        query = jnp.where(me == target, sent, query)
    return jnp.concatenate([passage, query], 0)


def unalign(rows, extra):
    heads = lax.axis_size("head")
    me = lax.axis_index("head")
    count = rows.shape[0]
    last = heads - 1
    moved = extra * last
    query = rows[count - extra :]
    payload = jnp.where(
        me == 0, jnp.concatenate([query, rows[: moved - extra]], 0), rows[:moved]
    )
    received = lax.ppermute(payload, "head", [((at + 1) % heads, at) for at in range(heads)])
    queries = [received[:extra]]
    for source in range(1, last):
        queries.append(lax.ppermute(query, "head", [(source, last)]))
    queries.append(query)
    tail = jnp.where(
        me == last,
        jnp.concatenate(queries, 0),
        jnp.concatenate([received, query], 0),
    )
    return lax.dynamic_slice_in_dim(
        jnp.concatenate([rows[: count - extra], tail], 0), extra * me, count, 0
    )


def with_column(rows, values):
    high = lax.reduce_precision(values, 8, 7)
    rest = values - high
    middle = lax.reduce_precision(rest, 8, 7)
    parts = jnp.stack([high, middle, rest - middle], 1).astype(BF16)
    return jnp.concatenate([rows, jnp.pad(parts, ((0, 0), (0, 125)))], 1)


def column_of(rows, width):
    parts = rows[:, width : width + 3].astype(F32)
    return rows[:, :width], parts[:, 0] + (parts[:, 1] + parts[:, 2])


def scatter_sum(keep, send, order, n_dp):
    shape = keep.shape[2:]
    names = ["x"] + ["dp%d" % bit for bit in bits_of(n_dp)[::-1]]
    current = keep.reshape([2] * len(names) + list(shape))
    received = swap(send, "head", 1).reshape(current.shape)
    for name in order:
        at = names.index(name)
        axis, bit = ("head", 2) if name == "x" else ("dp", int(name[2:]))

        def side(array, which):
            return lax.index_in_dim(array, which, at, keepdims=False)

        away = (side(current, 1) + side(received, 1).astype(F32)).astype(BF16)
        current = side(current, 0) + side(received, 0).astype(F32)
        received = swap(away, axis, bit)
        names.pop(at)
    return current + received.astype(F32)


def shards(
    tokens, w_qkv, b_qv, w_out, b_out, gain_one, shift_one, w_in, b_in, w_down, b_down,
    gain_two, shift_two, w_term, b_term, pass_len, query_len, grad_out, grad_term,
):
    n_dp, n_head = lax.axis_size("dp"), lax.axis_size("head")
    me, me_dp = lax.axis_index("head"), lax.axis_index("dp")
    width = tokens.shape[1]
    wide = w_qkv.shape[2]
    hidden = w_in.shape[1]
    extra = query_len.shape[0] * QLEN // n_head
    owners = n_head == 4 and hidden // n_dp == BLOCK

    bias = jnp.pad(
        jnp.concatenate([b_qv[0], jnp.zeros((256 - wide,), BF16), b_qv[1]])[None],
        ((0, 15), (0, width - 256 - wide)),
    )
    own_pack = jnp.concatenate([w_qkv.transpose(0, 2, 1).reshape(3 * wide, width), w_out, bias], 0)
    rows = align(tokens, extra)
    packs = [own_pack, swap(own_pack, "head", 1)]
    packs.append(swap(own_pack, "head", 2))
    packs.append(swap(packs[2], "head", 1))
    each = query_len.shape[0] // n_head
    lengths = jnp.concatenate(
        [lax.dynamic_slice_in_dim(pass_len, me, 1, 0), lax.dynamic_slice_in_dim(query_len, me * each, each, 0)]
    )
    grads_in = align(with_column(grad_out, grad_term), extra)
    params = jnp.stack(
        [b_out, gain_one, shift_one, b_down, gain_two, shift_two, w_term, jnp.pad(b_term, (0, width - 1))]
        + [jnp.zeros((width,), BF16)] * 8
    )
    place = jnp.stack([me_dp if owners else jnp.zeros_like(me_dp), me]).astype(jnp.int32)

    saved = [attend(lengths, rows, pack, wide) for pack in packs]
    r1, a1, active, slope, out_rows, db, dr2, vec = forward(
        rows, params, grads_in, b_in[None], w_in, w_down, [m for _, m, _ in saved], packs
    )
    out, term = column_of(unalign(out_rows, extra), width)

    first = ["dp%d" % bit for bit in bits_of(n_dp)]
    down = down_back(owners, place, active, db)
    db, *down = lax.optimization_barrier((db, *down))
    dr1, da, vec, grad_b_in, *inner = backward(
        owners, place, db, slope, w_down, w_in, a1, r1, dr2, params, vec
    )
    if owners:
        grad_w_down = scatter_sum(down[1], down[0], ["x"] + first, n_dp)
        grad_w_in = scatter_sum(inner[1], inner[0], first[:1] + ["x"] + first[1:], n_dp)
    else:
        both = ("dp", "head")
        grad_w_down = lax.psum_scatter(down[0], both, scatter_dimension=0, tiled=True)
        grad_w_in = lax.psum_scatter(inner[0], both, scatter_dimension=0, tiled=True)
    grad_w_in = grad_w_in.T

    vector = jnp.concatenate([vec, grad_b_in.reshape(-1, width)], 0)
    for axis, bit in [("head", 1), ("head", 2)] + [("dp", bit) for bit in bits_of(n_dp)]:
        vector = vector + swap(vector, axis, bit)
    grad_b_in = vector[16:].reshape(-1)

    grads, weights, biases = [None] * n_head, [None] * n_head, [None] * n_head
    for part in (3, 2, 1, 0):
        qkv, mixed, total = saved[part]
        grads[part], weights[part], biases[part] = attend_back(
            lengths, rows, packs[part], da, qkv, total, mixed, BF16 if part % 2 else F32
        )
    grad_rows = rows_back(dr1, grads, packs)
    grad_tokens = unalign(grad_rows, extra)

    far = weights[2] + swap(weights[3], "head", 1).astype(F32)
    near = weights[0] + swap(weights[1], "head", 1).astype(F32)
    block = near + swap(far.astype(BF16), "head", 2).astype(F32)
    far_bias = biases[2] + swap(biases[3], "head", 1)
    near_bias = biases[0] + swap(biases[1], "head", 1)
    bias_sum = near_bias + swap(far_bias, "head", 2)
    for bit in bits_of(n_dp):
        bias_sum = bias_sum + swap(bias_sum, "dp", bit)
    grad_b_qv = jnp.stack([bias_sum[0, :wide], bias_sum[0, 2 * wide :]])
    for bit in bits_of(n_dp):
        half = block.shape[0] // 2
        side = ((me_dp & bit) != 0).astype(jnp.int32)
        keep = lax.dynamic_slice_in_dim(block, side * half, half, 0)
        send = lax.dynamic_slice_in_dim(block, (1 - side) * half, half, 0).astype(BF16)
        block = keep + swap(send, "dp", bit).astype(F32)
    block = block.astype(BF16)
    for bit in bits_of(n_dp)[::-1]:
        other = swap(block, "dp", bit)
        mine = (me_dp & bit) != 0
        block = jnp.where(
            mine, jnp.concatenate([other, block], 0), jnp.concatenate([block, other], 0)
        )
    block = block.astype(F32)
    grad_w_qkv = block[: 3 * wide].reshape(3, wide, width).transpose(0, 2, 1)
    grad_w_out = block[3 * wide :]
    return (
        out, term, grad_tokens, grad_w_qkv, grad_b_qv, grad_w_out, vector[10], vector[8],
        vector[9], grad_w_in, grad_b_in, grad_w_down, vector[2], vector[0], vector[1],
        vector[3], vector[4, :1],
    )


def solution(mesh):
    both = ("dp", "head")
    placed = (
        P(both, None), P(None, None, "head"), P(None, "head"), P("head", None),
        P(), P(), P(), P(), P(), P(), P(), P(), P(), P(), P(),
        P("dp"), P("dp"), P(both, None), P(both),
    )
    return jax.shard_map(
        shards,
        mesh=mesh,
        in_specs=placed,
        out_specs=(
            P(both, None), P(both), P(both, None), P(None, None, "head"), P(None, "head"),
            P("head", None), P(), P(), P(), P(None, both), P(), P(both, None),
            P(), P(), P(), P(), P(),
        ),
        check_vma=False,
    )
```

```python
import functools
import math

import jax
import jax.numpy as jnp
import numpy as np
from jax import lax
from jax.experimental import pallas as pl
from jax.experimental.pallas import tpu as pltpu
from jax.sharding import PartitionSpec as P

HEAD_DIM = 64
PLEN = 512
QLEN = 32
F32 = jnp.float32
BF16 = jnp.bfloat16
NN = (((1,), (0,)), ((), ()))
NT = (((1,), (1,)), ((), ()))
TN = (((0,), (0,)), ((), ()))
SCALE = 1.0 / math.sqrt(HEAD_DIM)
MIB = 1024 * 1024
SMEM = pl.BlockSpec(memory_space=pltpu.SMEM)
VMEM = pl.BlockSpec(memory_space=pltpu.VMEM)


def mm(left, right, dims):
    return lax.dot_general(left, right, dims, preferred_element_type=F32)


def whole(shape):
    zeros = (0,) * len(shape)
    return pl.BlockSpec(shape, lambda *_: zeros)


def call(kernel, name, outs, flops, mib, grid=None, in_specs=None, out_specs=None, scratch=(), scalars=0):
    options = dict(
        out_shape=[jax.ShapeDtypeStruct(shape, dtype) for shape, dtype in outs],
        compiler_params=pltpu.CompilerParams(vmem_limit_bytes=44 * MIB),
        cost_estimate=pl.CostEstimate(flops=flops * 100, bytes_accessed=flops // 5, transcendentals=0),
        name=name,
    )
    if grid is None:
        return pl.pallas_call(
            kernel, in_specs=in_specs, out_specs=[VMEM] * len(outs), scratch_shapes=list(scratch), **options
        )
    spec = pltpu.PrefetchScalarGridSpec(
        num_scalar_prefetch=scalars, grid=grid, in_specs=in_specs, out_specs=out_specs,
        scratch_shapes=list(scratch),
    )
    return pl.pallas_call(kernel, grid_spec=spec, **options)


def masks(lengths_ref, extra):
    long_key = lax.broadcasted_iota(jnp.int32, (PLEN, PLEN), 0)
    key = lax.broadcasted_iota(jnp.int32, (extra, extra), 0)
    row = lax.broadcasted_iota(jnp.int32, (extra, extra), 1)
    short = jnp.zeros((extra, extra), jnp.bool_)
    for at in range(extra // QLEN):
        low, high = at * QLEN, (at + 1) * QLEN
        short = short | (
            (key >= low) & (key < low + lengths_ref[2 + at]) & (row >= low) & (row < high)
        )
    return long_key < lengths_ref[1], short


def attend_kernel(lengths_ref, x_ref, *refs):
    pack_refs, (qkv_ref, mixed_ref, total_ref) = refs[:-3], refs[-3:]
    wide = mixed_ref.shape[1]
    count = x_ref.shape[0]
    ones = jnp.ones((16, count), BF16)
    order = lengths_ref[0]
    valids = masks(lengths_ref, count - PLEN)
    total_ref[...] = jnp.zeros_like(total_ref)
    for at, pack_ref in enumerate(pack_refs):
        for member in range(3):
            piece = pack_ref[member ^ order]
            part = mm(piece[:wide], x_ref[...], NT)
            if member != 1:
                part = part + mm(piece[wide:, :wide], ones, TN)
            part = part.astype(BF16)
            qkv_ref[at, member * wide : (member + 1) * wide, :] = part * BF16(SCALE) if member == 0 else part
        for head in range(wide // HEAD_DIM):
            row = head * HEAD_DIM
            for valid, low, high in ((valids[0], 0, PLEN), (valids[1], PLEN, count)):
                query = qkv_ref[at, row : row + HEAD_DIM, low:high]
                keys = qkv_ref[at, wide + row : wide + row + HEAD_DIM, low:high]
                values = qkv_ref[at, 2 * wide + row : 2 * wide + row + HEAD_DIM, low:high]
                scores = jnp.where(valid, mm(keys, query, TN), -1000000000.0)
                top = jnp.max(scores, 0, keepdims=True)
                exponent = jnp.exp(scores - top)
                total = jnp.sum(exponent, 0, keepdims=True)
                shares = (exponent * (1.0 / total)).astype(BF16)
                mixed_ref[at, row : row + HEAD_DIM, low:high] = mm(values, shares, NN).astype(BF16)
                total_ref[at, head : head + 1, low:high] = top + jnp.log(total)


def attend(lengths, x, packs, wide):
    count = x.shape[0]
    parts = len(packs)
    outs = [((parts, 3 * wide, count), BF16), ((parts, wide, count), BF16), ((parts, 8, count), F32)]
    return call(
        attend_kernel, "attend", outs, 1_200_000_000 * parts, 24, in_specs=[SMEM] + [VMEM] * (1 + parts)
    )(lengths, x, *packs)


def attend_back_kernel(lengths_ref, da_ref, qkv_ref, total_ref, mixed_ref, vec_ref, pack_ref, grad_ref):
    wide = mixed_ref.shape[1]
    count, width = da_ref.shape
    valids = masks(lengths_ref, count - PLEN)
    grad_mixed = mm(pack_ref[3 ^ lengths_ref[0]][:wide], da_ref[...], NT).astype(BF16)
    grad_ref[: 3 * wide, count:] = jnp.zeros((3 * wide, width - count), BF16)
    grad_ref[3 * wide : 4 * wide, :] = mm(mixed_ref[0], da_ref[...], NN).astype(BF16)
    grad_ref[4 * wide :, :] = vec_ref[...].astype(BF16)
    for head in range(wide // HEAD_DIM):
        row = head * HEAD_DIM
        for valid, low, high in ((valids[0], 0, PLEN), (valids[1], PLEN, count)):
            query = qkv_ref[0, row : row + HEAD_DIM, low:high]
            keys = qkv_ref[0, wide + row : wide + row + HEAD_DIM, low:high]
            values = qkv_ref[0, 2 * wide + row : 2 * wide + row + HEAD_DIM, low:high]
            upper = grad_mixed[row : row + HEAD_DIM, low:high]
            scores = jnp.where(valid, mm(keys, query, TN), -1000000000.0)
            shares = jnp.exp(scores - total_ref[0, head : head + 1, low:high])
            grad_shares = mm(values, upper, TN)
            inner = jnp.sum(shares * grad_shares, 0, keepdims=True)
            grad_scores = (shares * (grad_shares - inner)).astype(BF16)
            grad_ref[2 * wide + row : 2 * wide + row + HEAD_DIM, low:high] = mm(
                upper, shares.astype(BF16), NT
            ).astype(BF16)
            grad_ref[wide + row : wide + row + HEAD_DIM, low:high] = mm(query, grad_scores, NT).astype(BF16)
            grad_ref[row : row + HEAD_DIM, low:high] = (mm(keys, grad_scores, NN) * SCALE).astype(BF16)


def attend_back(lengths, da, qkv, total, mixed, vec, pack):
    _, wide, count = mixed.shape
    width = da.shape[1]
    return call(
        attend_back_kernel, "attend_back", [((4 * wide + vec.shape[0], width), BF16)], 2_000_000_000, 24,
        in_specs=[SMEM] + [VMEM] * 6,
    )(lengths, da, qkv, total, mixed, vec, pack)[0]


def head_grads_kernel(x_ref, x_core_ref, own_ref, core_ref, vec_ref, first_ref, second_ref):
    count = x_ref.shape[0]
    sums = vec_ref.shape[0]
    rows = own_ref.shape[0] - sums
    wide = rows // 4
    cut = first_ref.shape[0]
    dtype = second_ref.dtype
    grads = jnp.concatenate([own_ref[: 3 * wide, :count], core_ref[: 3 * wide, :count]], 1)
    tokens = jnp.concatenate([x_ref[...], x_core_ref[...]], 0)
    first_ref[...] = mm(grads[:cut], tokens, NN).astype(first_ref.dtype)
    second_ref[: 3 * wide - cut, :] = mm(grads[cut:], tokens, NN).astype(dtype)
    second_ref[3 * wide - cut : rows - cut, :] = (
        own_ref[3 * wide : rows].astype(F32) + core_ref[3 * wide : rows].astype(F32)
    ).astype(dtype)
    second_ref[rows - cut :, :] = jnp.zeros((second_ref.shape[0] - rows + cut, second_ref.shape[1]), dtype)
    ones = jnp.ones((16, grads.shape[1]), BF16)
    second_ref[rows - cut : rows - cut + 16, : 3 * wide] = mm(ones, grads, NT).astype(dtype)
    second_ref[rows - cut + 16 : rows - cut + 16 + sums, :] = (
        vec_ref[...] + core_ref[rows:].astype(F32)
    ).astype(dtype)


def head_grads(x, x_core, at_core, own, core, vec, dtype):
    count, width = x.shape
    rows = own.shape[0] - vec.shape[0]
    outs = [((rows // 2, width), dtype), ((rows // 2 + 64, width), F32)]
    return call(
        head_grads_kernel, "head_grads", outs, 1_500_000_000, 24, grid=(1,),
        in_specs=[
            whole(x.shape), pl.BlockSpec((count, width), lambda _: (0, at_core)), whole(own.shape),
            whole(core.shape), whole(vec.shape),
        ],
        out_specs=[whole(shape) for shape, _ in outs],
    )(x, x_core, own, core, vec)


def rows_kernel(orders_ref, base_ref, beside_ref, *refs):
    out_ref = refs[-1]
    parts = (len(refs) - 1) // 2
    width = base_ref.shape[1]
    total = base_ref[...]
    for part in range(parts):
        grad_ref, pack_ref = refs[part], refs[parts + part]
        wide = pack_ref.shape[1] - 16
        for member in range(3):
            piece = pack_ref[member ^ orders_ref[part]]
            total = total + mm(grad_ref[member * wide : (member + 1) * wide, : base_ref.shape[0]], piece[:wide], TN)
    out_ref[:, :width] = total.astype(BF16)
    out_ref[:, width:] = beside_ref[...]


def rows_back(orders, base, beside, grads, packs):
    shape = (base.shape[0], base.shape[1] + beside.shape[1])
    return call(
        rows_kernel, "rows_back", [(shape, BF16)], 2_000_000_000, 32, in_specs=[SMEM] + [VMEM] * (2 + 2 * len(packs)),
    )(orders, base, beside, *grads, *packs)[0]


def normed(hidden):
    center = hidden - jnp.mean(hidden, -1, keepdims=True)
    inverse = lax.rsqrt(jnp.mean(center * center, -1, keepdims=True) + 1e-06)
    return center * inverse, inverse


def norm_back(grad, unit, inverse, gain):
    grad_unit = grad * gain
    return inverse * (
        grad_unit
        - jnp.mean(grad_unit, -1, keepdims=True)
        - unit * jnp.mean(grad_unit * unit, -1, keepdims=True)
    )


def column_sum(values):
    return jnp.sum(values, 0, keepdims=True)


def put_halves(values, block, core, mine_ref, other_ref):
    if values.shape[1] < 2 * block:
        mine_ref[...] = values
        return
    sides = [
        jnp.concatenate(
            [values[:, at : at + block] for at in range(side * block, values.shape[1], 2 * block)], 1
        )
        for side in (0, 1)
    ]
    mine_ref[...] = jnp.where(core == 0, sides[0], sides[1])
    other_ref[...] = jnp.where(core == 0, sides[1], sides[0])


def forward_kernel(parts, block, scalars_ref, *refs):
    x_ref, params_ref, grads_ref, bias_ref, w_in_ref, w_down_ref = refs[:6]
    mixed_refs = refs[6 : 6 + parts]
    out_refs = refs[6 + parts : 6 + 2 * parts]
    r1_ref, a1_ref, mine_ref, pass_ref, slope_ref, out_ref, db_ref, dr2_ref, vec_ref = refs[6 + 2 * parts : -2]
    first_ref, sum_ref = refs[-2:]
    half_width = pass_ref.shape[1] - 3 * x_ref.shape[1]
    step, steps = pl.program_id(0), pl.num_programs(0)
    width = x_ref.shape[1]

    def param(at):
        return params_ref[at : at + 1, :].astype(F32)

    @pl.when(step == 0)
    def _():
        total = x_ref[...].astype(F32) + param(0)
        for part in range(parts):
            total = total + mm(mixed_refs[part][0], out_refs[part][0], TN)
        r1_ref[...] = total
        unit, _ = normed(total)
        first = unit * param(1) + param(2)
        first_ref[...] = first
        a1_ref[...] = first.astype(BF16)
        pass_ref[:, half_width + width : half_width + 2 * width] = first.astype(BF16)
        pass_ref[:, half_width + 2 * width :] = x_ref[...]
        sum_ref[...] = jnp.zeros_like(sum_ref)

    inner = mm(a1_ref[...], w_in_ref[...], NN) + bias_ref[...].astype(F32)
    square = inner * inner
    factor = math.sqrt(2.0 / math.pi)
    tanh = jnp.tanh(inner * (factor + (factor * 0.044715) * square))
    half = 0.5 + 0.5 * tanh
    active = (inner * half).astype(BF16)
    share = active.shape[1] // 2
    place = pl.ds(pl.multiple_of(step * share, share), share)
    put_halves(active, block, scalars_ref[parts], mine_ref, pass_ref.at[:, place])
    slope_ref[...] = half + inner * (0.5 - 0.5 * tanh * tanh) * (factor + (3 * factor * 0.044715) * square)
    sum_ref[...] += mm(active, w_down_ref[...], NN)

    @pl.when(step == steps - 1)
    def _():
        unit, inverse = normed(first_ref[...] + sum_ref[...] + param(3))
        gain = param(4)
        second = unit * gain + param(5)
        weight = param(6)
        logit = jnp.sum(second * weight, -1, keepdims=True) + params_ref[7:8, 0:1].astype(F32)
        term = jnp.maximum(logit, 0.0) + jnp.log1p(jnp.exp(-jnp.abs(logit)))
        sigmoid = 1.0 / (1.0 + jnp.exp(-logit))
        lane = lax.broadcasted_iota(jnp.int32, (term.shape[0], 128), 1)
        high = term.astype(BF16).astype(F32)
        middle = (term - high).astype(BF16).astype(F32)
        rest = term - high - middle
        tail = jnp.where(lane == 0, high, jnp.where(lane == 1, middle, jnp.where(lane == 2, rest, 0.0)))
        out_ref[:, :width] = second.astype(BF16)
        out_ref[:, width:] = tail.astype(BF16)
        grad_term = jnp.sum(grads_ref[:, width:].astype(F32), -1, keepdims=True)
        grad_logit = grad_term * sigmoid
        grad = grads_ref[:, :width].astype(F32) + grad_logit * weight
        back = norm_back(grad, unit, inverse, gain)
        db_ref[...] = back.astype(BF16)
        pass_ref[:, half_width : half_width + width] = back.astype(BF16)
        dr2_ref[...] = back
        vec_ref[...] = jnp.zeros_like(vec_ref)
        vec_ref[0:1, :] = column_sum(grad * unit)
        vec_ref[1:2, :] = column_sum(grad)
        vec_ref[2:3, :] = column_sum(back)
        vec_ref[3:4, :] = column_sum(grad_logit * second)
        scalar = jnp.broadcast_to(column_sum(grad_logit), (1, width))
        scaled = jnp.floor(jnp.abs(scalar) * param(8))
        digit = scaled - 2.0 * jnp.floor(0.5 * scaled)
        vec_ref[4:5, :] = jnp.where(scalar < 0, -digit, digit)


def forward(scalars, x, params, grads, b_in, w_in, w_down, mixed, packs, block, chunk):
    count, width = x.shape
    hidden = w_in.shape[1]
    wide = mixed[0].shape[1]
    parts = len(packs)
    specs = [
        whole(x.shape), whole(params.shape), whole(grads.shape),
        pl.BlockSpec((1, chunk), lambda j, o: (0, j)),
        pl.BlockSpec((width, chunk), lambda j, o: (0, j)),
        pl.BlockSpec((chunk, width), lambda j, o: (j, 0)),
    ]
    mixed = [(array, at) for array in mixed for at in range(array.shape[0])]
    specs += [
        pl.BlockSpec((1, wide, count), functools.partial(lambda at, j, o: (at, 0, 0), at)) for _, at in mixed
    ]
    specs += [
        pl.BlockSpec((1, wide, width), functools.partial(lambda part, j, o: (3 ^ o[part], 0, 0), part))
        for part in range(parts)
    ]
    share = 2 if chunk >= 2 * block else 1
    outs = [
        ((count, width), F32), ((count, width), BF16), ((count, hidden // share), BF16),
        ((count, hidden // 2 + 3 * width), BF16), ((count, hidden), F32),
        ((count, width + 128), BF16), ((count, width), BF16), ((count, width), F32), ((8, width), F32),
    ]
    out_specs = [whole(s) for s, _ in outs]
    out_specs[2] = pl.BlockSpec((count, chunk // share), lambda j, o: (0, j))
    out_specs[4] = pl.BlockSpec((count, chunk), lambda j, o: (0, j))
    return call(
        functools.partial(forward_kernel, parts, block), "forward", outs, 6_200_000_000, 48,
        grid=(hidden // chunk,), in_specs=specs, out_specs=out_specs, scalars=1,
        scratch=[pltpu.VMEM((count, width), F32), pltpu.VMEM((count, width), F32)],
    )(scalars, x, params, grads, b_in, w_in, w_down, *[array for array, _ in mixed], *packs)


def backward_kernel(
    block, scalars_ref, db_ref, slope_ref, w_down_ref, w_in_ref, r1_ref, dr2_ref, params_ref, vec_ref,
    dr1_ref, da_ref, out_vec_ref, mine_ref, other_ref, sum_ref
):
    step, steps = pl.program_id(0), pl.num_programs(0)

    @pl.when(step == 0)
    def _():
        sum_ref[...] = dr2_ref[...]
        out_vec_ref[:8, :] = vec_ref[...]
        out_vec_ref[8:, :] = jnp.zeros_like(vec_ref)

    grad_inner = mm(db_ref[...], w_down_ref[...], NT) * slope_ref[...]
    out_vec_ref[pl.ds(11 + step, 1), :] = column_sum(grad_inner)
    low = grad_inner.astype(BF16)
    put_halves(low, block, scalars_ref[0], mine_ref, other_ref)
    sum_ref[...] += mm(low, w_in_ref[...], NT)

    @pl.when(step == steps - 1)
    def _():
        grad = sum_ref[...]
        unit, inverse = normed(r1_ref[...])
        back = norm_back(grad, unit, inverse, params_ref[1:2, :].astype(F32))
        dr1_ref[...] = back
        da_ref[...] = back.astype(BF16)
        out_vec_ref[8:9, :] = column_sum(grad * unit)
        out_vec_ref[9:10, :] = column_sum(grad)
        out_vec_ref[10:11, :] = column_sum(back)


def backward(scalars, db, slope, w_down, w_in, r1, dr2, params, vec, block):
    count, width = db.shape
    hidden = w_in.shape[1]
    chunk = width
    share = 2 if chunk >= 2 * block else 1
    outs = [
        ((count, width), F32), ((count, width), BF16), ((16, width), F32),
        ((count, hidden // share), BF16), ((count, hidden // 2), BF16),
    ]
    out_specs = [whole(s) for s, _ in outs]
    out_specs[3] = pl.BlockSpec((count, chunk // share), lambda j, o: (0, j))
    out_specs[4] = pl.BlockSpec((count, chunk // 2), lambda j, o: (0, j))
    return call(
        functools.partial(backward_kernel, block), "backward", outs, 5_500_000_000, 48, grid=(hidden // chunk,),
        in_specs=[
            whole(db.shape),
            pl.BlockSpec((count, chunk), lambda j, o: (0, j)),
            pl.BlockSpec((chunk, width), lambda j, o: (j, 0)),
            pl.BlockSpec((width, chunk), lambda j, o: (0, j)),
            whole(r1.shape), whole(dr2.shape), whole(params.shape), whole(vec.shape),
        ],
        out_specs=out_specs, scalars=1, scratch=[pltpu.VMEM((count, width), F32)],
    )(scalars, db, slope, w_down, w_in, r1, dr2, params, vec)


def owner_grads_kernel(block, by_z, me_ref, left_ref, left_core_ref, right_ref, right_core_ref, send_ref, keep_ref, tile_ref):
    tile_ref[...] = mm(
        jnp.concatenate([left_ref[...], left_core_ref[...]], 0),
        jnp.concatenate([right_ref[...], right_core_ref[...]], 0),
        TN,
    )
    low = me_ref[0] & 3
    far = me_ref[1] >> 1
    for at in range(4):
        y, z = (at ^ low) & 1, (at ^ low) >> 1
        away, place = (z, y) if by_z else (y, z)
        for x in (0, 1):
            begin = pl.multiple_of(2 * block * at + block * (far ^ x), block)
            rows = tile_ref[pl.ds(begin, block), :]

            @pl.when(away == 1)
            def _():
                send_ref[(x, place, 0) if by_z else (place, x, 0)] = rows.astype(BF16)

            @pl.when(away == 0)
            def _():
                keep_ref[(x, place, 0) if by_z else (place, x, 0)] = rows


def owner_grads(me, left, left_core, right, right_core, at_core, block, by_z):
    count, half = left.shape
    width = right.shape[1]
    n_dp = half // (2 * block)
    chunk = 8 * block
    shape = (2, 2, n_dp // 4, block, width)
    spec = pl.BlockSpec((2, 2, 1, block, width), lambda j, me: (0, 0, j, 0, 0))
    columns = pl.BlockSpec((count, chunk), lambda j, me: (0, j ^ (me[0] >> 2)))
    return call(
        functools.partial(owner_grads_kernel, block, by_z), "owner_grads", [(shape, BF16), (shape, F32)],
        2_700_000_000, 40, grid=(half // chunk,),
        in_specs=[columns, columns, whole(right.shape), pl.BlockSpec((count, width), lambda j, me: (0, at_core))],
        out_specs=[spec, spec], scalars=1, scratch=[pltpu.VMEM((chunk, width), F32)],
    )(me, left, left_core, right, right_core)


def swap(array, axis, bit, name="swap"):
    size = lax.axis_size(axis)
    with jax.named_scope(name + "_" + axis + str(bit)):
        return lax.ppermute(array, axis, [(at, at ^ bit) for at in range(size)])


def bits_of(size):
    return [1 << at for at in range(size.bit_length() - 1)]


def shift(rows, extra):
    heads = lax.axis_size("head")
    me = lax.axis_index("head")
    count = rows.shape[0]
    moved = extra * (heads - 1)
    payload = jnp.where(me == heads - 1, rows[count - moved - extra : count - extra], rows[count - moved :])
    return lax.ppermute(payload, "head", [(at, (at + 1) % heads) for at in range(heads)])


def queries_for(rows, extra, target):
    begin = rows.shape[0] - (lax.axis_size("head") - target) * extra
    return rows[begin : begin + extra]


def aligned(rows, received, sent, extra):
    me = lax.axis_index("head")
    count = rows.shape[0]
    moved = received.shape[0]
    passage = lax.dynamic_slice_in_dim(
        jnp.concatenate([received, rows], 0), moved - extra * me, count - extra, 0
    )
    query = jnp.where(
        me == 0, received[:extra], jnp.where(me == 1, sent[0], jnp.where(me == 2, sent[1], rows[count - extra :]))
    )
    return jnp.concatenate([passage, query], 0)


def align(rows, extra):
    received = shift(rows, extra)
    sent = [
        lax.ppermute(queries_for(rows, extra, target), "head", [(lax.axis_size("head") - 1, target)])
        for target in (1, 2)
    ]
    return aligned(rows, received, sent, extra)


def unalign(rows, extra):
    heads = lax.axis_size("head")
    me = lax.axis_index("head")
    count = rows.shape[0]
    last = heads - 1
    moved = extra * last
    query = rows[count - extra :]
    payload = jnp.where(
        me == 0, jnp.concatenate([query, rows[: moved - extra]], 0), rows[:moved]
    )
    received = lax.ppermute(payload, "head", [((at + 1) % heads, at) for at in range(heads)])
    queries = [received[:extra]]
    for source in range(1, last):
        queries.append(lax.ppermute(query, "head", [(source, last)]))
    queries.append(query)
    tail = jnp.where(
        me == last,
        jnp.concatenate(queries, 0),
        jnp.concatenate([received, query], 0),
    )
    return lax.dynamic_slice_in_dim(
        jnp.concatenate([rows[: count - extra], tail], 0), extra * me, count, 0
    )


def with_column(rows, values):
    high = lax.reduce_precision(values, 8, 7)
    rest = values - high
    middle = lax.reduce_precision(rest, 8, 7)
    parts = jnp.stack([high, middle, rest - middle], 1).astype(BF16)
    return jnp.concatenate([rows, jnp.pad(parts, ((0, 0), (0, 125)))], 1)


def column_of(rows, width):
    parts = rows[:, width : width + 3].astype(F32)
    return rows[:, :width], parts[:, 0] + (parts[:, 1] + parts[:, 2])


def after(value, *others):
    return lax.optimization_barrier((*others, value))[-1]


class Scatter:
    def __init__(self, send, keep, sent, names, label):
        self.names, self.label, self.current = list(names), label, keep
        self.received = self.swap(send, sent)

    def swap(self, away, name):
        axis, bit = ("head", 2) if name == "x" else ("dp", int(name[2:]))
        return swap(away, axis, bit, self.label)

    def step(self, *before):
        name = self.names.pop(0)
        shape = self.current.shape[1:]
        self.received = after(self.received, *before) if before else self.received

        def side(which):
            return self.current[which].reshape(shape) + self.received[which].astype(F32).reshape(shape)

        away = side(1).astype(BF16)
        self.current = side(0)
        self.received = self.swap(away, name)
        return away

    def result(self):
        return self.current + self.received.astype(F32)


class Total:
    def __init__(self, keep, far, steps, label):
        self.label, self.keep, self.far, self.steps = label, keep, far, list(steps)
        self.received, self.kind = None, None
        dp = [name for name in steps if name != "x"]
        self.steps += dp[:-1][::-1]
        self.middle = dp[-1]
        self.backs = len(dp) - 1
        self.me = lax.axis_index("dp")

    def merged(self):
        kind, received = self.kind, self.received
        if kind == "back":
            return jnp.where(
                self.mine,
                jnp.concatenate([received, self.keep], 0),
                jnp.concatenate([self.keep, received], 0),
            )
        if kind == "both":
            rows = self.keep.shape[0]
            self.far = self.far + received[:rows].astype(F32)
            received = received[rows:]
        if kind is not None:
            return self.keep.astype(F32) + received.astype(F32)
        return self.keep

    def step(self, *before):
        name = self.steps.pop(0)
        if before:
            tied = [value for value in (self.keep, self.far, self.received) if value is not None]
            tied = list(lax.optimization_barrier((*before, *tied))[len(before) :])
            self.keep = tied.pop(0)
            if self.far is not None:
                self.far = tied.pop(0)
            if self.received is not None:
                self.received = tied.pop(0)
        block = self.merged()
        if name == "x":
            away, self.far = self.far.astype(BF16), None
            self.keep, self.kind = block, "add"
            self.received = swap(away, "head", 2, self.label)
            return away
        bit = int(name[2:])
        self.mine = (self.me & bit) != 0
        if name == self.middle:
            away = self.keep = block.astype(BF16)
            self.kind = "add"
        elif len(self.steps) < self.backs:
            away = self.keep = block.astype(BF16)
            self.kind = "back"
        else:
            half = block.shape[0] // 2
            side = self.mine.astype(jnp.int32)

            def part(array, which):
                return lax.dynamic_slice_in_dim(array, which * half, half, 0)

            away = part(block, 1 - side).astype(BF16)
            self.keep, self.kind = part(block, side), "add"
            if self.far is not None:
                away = jnp.concatenate([part(self.far, 1 - side).astype(BF16), away], 0)
                self.far, self.kind = part(self.far, side), "both"
        self.received = swap(away, "dp", bit, self.label)
        return away


TAIL = "iabidababtadbabd"


def shards(
    tokens, w_qkv, b_qv, w_out, b_out, gain_one, shift_one, w_in, b_in, w_down, b_down,
    gain_two, shift_two, w_term, b_term, pass_len, query_len, grad_out, grad_term,
):
    n_dp, n_head = lax.axis_size("dp"), lax.axis_size("head")
    me, me_dp = lax.axis_index("head"), lax.axis_index("dp")
    width = tokens.shape[1]
    wide = w_qkv.shape[2]
    hidden = w_in.shape[1]
    extra = query_len.shape[0] * QLEN // n_head
    block = hidden // (n_dp * n_head)
    owners = n_head == 4 and block == 96
    chunk = 768

    bias = jnp.zeros((4, 16, width), BF16).at[0, 0, :wide].set(b_qv[0]).at[2, 0, :wide].set(b_qv[1])
    own = jnp.concatenate([jnp.concatenate([w_qkv.transpose(0, 2, 1), w_out[None]], 0), bias], 1)
    turn = me_dp & 3
    received = shift(tokens, extra)
    grads_in = align(with_column(grad_out, grad_term), extra)
    piece = jnp.concatenate(
        [lax.dynamic_index_in_dim(own, turn, 0, keepdims=False), queries_for(tokens, extra, 1)], 0
    )
    piece = swap(piece, "head", 2, "weights")
    beside = jnp.concatenate([own.reshape(-1, width), queries_for(tokens, extra, 2)], 0)
    beside = swap(beside, "head", 1, "weights")
    second, received = lax.optimization_barrier(
        (lax.dynamic_index_in_dim(own, turn ^ 3, 0, keepdims=False), received)
    )
    last = swap(second, "head", 2, "weights")
    high = own.shape[1]
    rows = aligned(tokens, received, (piece[high:], beside[4 * high :]), extra)
    pieces = [piece[:high], swap(piece[:high], "dp", 1, "weights"), swap(piece[:high], "dp", 2, "weights"), last]
    packs = [own, beside[: 4 * high].reshape(own.shape)]
    each = query_len.shape[0] // n_head
    zero = jnp.zeros((1,), jnp.int32)
    lengths = [
        lax.dynamic_slice_in_dim(pass_len, me, 1, 0), lax.dynamic_slice_in_dim(query_len, me * each, each, 0)
    ]
    near = jnp.concatenate([zero, *lengths])
    distant = jnp.concatenate([turn.astype(jnp.int32)[None], *lengths])
    core = (me & 1).astype(jnp.int32)[None]
    scalars = jnp.concatenate([zero, zero, distant[:1], distant[:1], core])
    digits = np.zeros((width,), np.float32)
    digits[:36] = 2.0 ** (np.arange(36) - 11)
    params = jnp.concatenate(
        [b_out, gain_one, shift_one, b_down, gain_two, shift_two, w_term, b_term]
        + [jnp.zeros((width - 1,), BF16), jnp.asarray(digits, BF16), jnp.zeros((7 * width,), BF16)]
    ).reshape(16, width)
    place = jnp.stack([me_dp, me]).astype(jnp.int32)

    saved = [attend(near, rows, packs[:1], wide)]
    rows_then, grads_in = lax.optimization_barrier((after(rows, saved[0][1]), grads_in))
    saved.append(attend(near, rows_then, packs[1:2], wide))
    pieces = lax.optimization_barrier((saved[1][1], *pieces))[1:]
    packs.append(jnp.stack(pieces))
    packs.append(swap(packs[2], "head", 1, "weights"))
    saved.append(attend(distant, rows, packs[2:3], wide))
    rows_then, packs[3] = lax.optimization_barrier((after(rows, saved[2][1]), packs[3]))
    saved.append(attend(distant, rows_then, packs[3:], wide))
    split = block if owners else hidden
    r1, a1, mine, given, slope, out_rows, db, dr2, vec = forward(
        scalars, rows, params, grads_in, b_in[None], w_in, w_down, [m for _, m, _ in saved], packs, split, chunk
    )
    given_core = swap(given, "head", 1, "given")
    dr1, da, vec, dz_mine, dz_other = backward(core, db, slope, w_down, w_in, r1, dr2, params, vec, split)
    names = ["dp%d" % bit for bit in bits_of(n_dp)]
    at_core = hidden // 2 // width
    if owners:
        dz_core = swap(dz_other, "head", 1, "inner")
        place, given_core = lax.optimization_barrier((after(place, da), given_core))
        send, keep = owner_grads(place, mine, given_core, db, given_core, at_core, block, True)
        down = Scatter(send, keep, names[1], ["x", names[0]] + names[2:], "down")
        place, dz_core = lax.optimization_barrier((after(place, send), dz_core))
        send, keep = owner_grads(place, dz_mine, dz_core, a1, given_core, at_core + 1, block, False)
        inner = Scatter(send, keep, names[0], [names[1], "x"] + names[2:], "inner")
        da = after(da, send)
    else:
        both = ("dp", "head")
        grad_w_down = lax.psum_scatter(mm(mine, db, TN), both, scatter_dimension=0, tiled=True)
        grad_w_in = lax.psum_scatter(mm(dz_mine, a1, TN), both, scatter_dimension=0, tiled=True)

    def back(part, da):
        qkv, mixed, total = saved[part]
        return attend_back(distant if part > 1 else near, da, qkv, total, mixed, vec, packs[part])

    def heads(part, own, core, dtype):
        return head_grads(rows, given_core, at_core + 2, own, core, vec, dtype)

    grads, then = {}, da
    for part in (3, 2, 1, 0):
        grads[part] = back(part, after(da, then))
        then = grads[part]
    if owners:
        down.received = after(down.received, then)
        inner.received = after(inner.received, then)
        sent = lax.optimization_barrier((then, down.received, inner.received, grads[3], grads[1]))
        down.received, inner.received = sent[1:3]
    else:
        sent = lax.optimization_barrier((then, grads[3], grads[1]))
    far_core, near_core = swap(sent[-2], "head", 1, "far"), swap(sent[-1], "head", 1, "near")
    then = sent[0]
    if owners:
        then = inner.step(then)
    far_then, far_core, near_core = lax.optimization_barrier((after(grads[2], then), far_core, near_core))
    far_sum = heads(2, far_then, far_core, BF16)
    near_sum = heads(0, after(grads[0], far_sum[0]), near_core, F32)
    steps = ["dp%d" % bit for bit in bits_of(n_dp)]
    totals = [
        Total(near_sum[0], far_sum[0], ["x"] + steps, "first"),
        Total(near_sum[1], far_sum[1], steps[:1] + ["x"] + steps[1:], "second"),
    ]
    totals[0].step()
    then = totals[1].step()
    combined = rows_back(scalars, after(dr1, then), out_rows, [grads[part] for part in range(n_head)], packs)
    done = [combined]

    def step(one):
        done[:] = [one.step(*done)]

    scatters = {"d": down, "i": inner} if owners else {}
    for item in TAIL:
        if item in "ab":
            total = totals["ab".index(item)]
            if total.steps:
                step(total)
        elif item == "t":
            combined = unalign(after(combined, *done), extra)
        elif item in scatters and scatters[item].names:
            step(scatters[item])
    for total in totals:
        while total.steps:
            step(total)
    for one in scatters.values():
        while one.names:
            step(one)
    if owners:
        grad_w_down, grad_w_in = down.result().reshape(block, width), inner.result().reshape(block, width)
    total = jnp.concatenate([one.merged() for one in totals], 0).astype(F32)
    grad_w_qkv = total[: 3 * wide].reshape(3, wide, width).transpose(0, 2, 1)
    grad_w_out = total[3 * wide : 4 * wide]
    bias_row, sums = total[4 * wide], total[4 * wide + 16 : 4 * wide + 32]
    grad_b_qv = jnp.stack([bias_row[:wide], bias_row[2 * wide : 3 * wide]])
    grad_b_term = jnp.sum(sums[4, :36] * jnp.asarray(2.0 ** (11 - np.arange(36)), F32))[None]
    grad_tokens = combined[:, :width]
    out, term = column_of(combined[:, width:], width)
    return (
        out, term, grad_tokens, grad_w_qkv, grad_b_qv, grad_w_out, sums[10], sums[8],
        sums[9], grad_w_in.T, sums[11:15].reshape(-1), grad_w_down, sums[2], sums[0], sums[1],
        sums[3], grad_b_term,
    )


def solution(mesh):
    both = ("dp", "head")
    placed = (
        P(both, None), P(None, None, "head"), P(None, "head"), P("head", None),
        P(), P(), P(), P(), P(), P(), P(), P(), P(), P(), P(),
        P("dp"), P("dp"), P(both, None), P(both),
    )
    return jax.shard_map(
        shards,
        mesh=mesh,
        in_specs=placed,
        out_specs=(
            P(both, None), P(both), P(both, None), P(None, None, "head"), P(None, "head"),
            P("head", None), P(), P(), P(), P(None, both), P(), P(both, None),
            P(), P(), P(), P(), P(),
        ),
        check_vma=False,
    )
```

```python
import functools
import math

import jax
import jax.numpy as jnp
import numpy as np
from jax import lax
from jax.experimental import pallas as pl
from jax.experimental.pallas import tpu as pltpu
from jax.sharding import PartitionSpec as P

HEAD_DIM = 64
PLEN = 512
QLEN = 32
F32 = jnp.float32
BF16 = jnp.bfloat16
NN = (((1,), (0,)), ((), ()))
NT = (((1,), (1,)), ((), ()))
TN = (((0,), (0,)), ((), ()))
SCALE = 1.0 / math.sqrt(HEAD_DIM)
MIB = 1024 * 1024
CUT = 384
SMEM = pl.BlockSpec(memory_space=pltpu.SMEM)
VMEM = pl.BlockSpec(memory_space=pltpu.VMEM)


def mm(left, right, dims):
    return lax.dot_general(left, right, dims, preferred_element_type=F32)


def whole(shape):
    zeros = (0,) * len(shape)
    return pl.BlockSpec(shape, lambda *_: zeros)


def call(kernel, name, outs, flops, mib, grid=None, in_specs=None, out_specs=None, scratch=(), scalars=0):
    options = dict(
        out_shape=[jax.ShapeDtypeStruct(shape, dtype) for shape, dtype in outs],
        compiler_params=pltpu.CompilerParams(vmem_limit_bytes=mib * MIB),
        cost_estimate=pl.CostEstimate(flops=flops * 100, bytes_accessed=flops // 5, transcendentals=0),
        name=name,
    )
    if grid is None:
        return pl.pallas_call(
            kernel, in_specs=in_specs, out_specs=[VMEM] * len(outs), scratch_shapes=list(scratch), **options
        )
    spec = pltpu.PrefetchScalarGridSpec(
        num_scalar_prefetch=scalars, grid=grid, in_specs=in_specs, out_specs=out_specs,
        scratch_shapes=list(scratch),
    )
    return pl.pallas_call(kernel, grid_spec=spec, **options)


def masks(lengths_ref, extra):
    long_key = lax.broadcasted_iota(jnp.int32, (PLEN, PLEN), 0)
    key = lax.broadcasted_iota(jnp.int32, (extra, extra), 0)
    row = lax.broadcasted_iota(jnp.int32, (extra, extra), 1)
    short = jnp.zeros((extra, extra), jnp.bool_)
    for at in range(extra // QLEN):
        low, high = at * QLEN, (at + 1) * QLEN
        short = short | (
            (key >= low) & (key < low + lengths_ref[lengths_ref[2] + at]) & (row >= low) & (row < high)
        )
    return long_key < lengths_ref[lengths_ref[1]], short


def attend_kernel(lengths_ref, x_ref, *refs):
    pack_refs, (qkv_ref, mixed_ref, total_ref) = refs[:-3], refs[-3:]
    wide = mixed_ref.shape[1]
    pitch = wide + 16
    count = x_ref.shape[0]
    ones = jnp.ones((16, count), BF16)
    order = lengths_ref[0]
    valids = masks(lengths_ref, count - PLEN)
    total_ref[...] = jnp.zeros_like(total_ref)
    for at, pack_ref in enumerate(pack_refs):
        for member in range(3):
            begin = pl.multiple_of((member ^ order) * pitch, pitch)
            part = mm(pack_ref[pl.ds(begin, wide), :], x_ref[...], NT)
            if member != 1:
                part = part + mm(pack_ref[pl.ds(begin + wide, 16), :wide], ones, TN)
            part = part.astype(BF16)
            qkv_ref[at, member * wide : (member + 1) * wide, :] = part * BF16(SCALE) if member == 0 else part
        for head in range(wide // HEAD_DIM):
            row = head * HEAD_DIM
            for valid, low, high in ((valids[0], 0, PLEN), (valids[1], PLEN, count)):
                query = qkv_ref[at, row : row + HEAD_DIM, low:high]
                keys = qkv_ref[at, wide + row : wide + row + HEAD_DIM, low:high]
                values = qkv_ref[at, 2 * wide + row : 2 * wide + row + HEAD_DIM, low:high]
                scores = jnp.where(valid, mm(keys, query, TN), -1000000000.0)
                top = jnp.max(scores, 0, keepdims=True)
                exponent = jnp.exp(scores - top)
                total = jnp.sum(exponent, 0, keepdims=True)
                shares = (exponent * (1.0 / total)).astype(BF16)
                mixed_ref[at, row : row + HEAD_DIM, low:high] = mm(values, shares, NN).astype(BF16)
                total_ref[at, head : head + 1, low:high] = top + jnp.log(total)


def attend(lengths, x, pack, wide):
    count = x.shape[0]
    outs = [((1, 3 * wide, count), BF16), ((1, wide, count), BF16), ((1, 8, count), F32)]
    return call(attend_kernel, "attend", outs, 1_200_000_000, 44, in_specs=[SMEM] + [VMEM] * 2)(lengths, x, pack)


def attend_back_kernel(lengths_ref, da_ref, qkv_ref, total_ref, mixed_ref, vec_ref, pack_ref, grad_ref):
    wide = mixed_ref.shape[1]
    count, width = da_ref.shape
    valids = masks(lengths_ref, count - PLEN)
    begin = pl.multiple_of((3 ^ lengths_ref[0]) * (wide + 16), wide + 16)
    grad_mixed = mm(pack_ref[pl.ds(begin, wide), :], da_ref[...], NT).astype(BF16)
    grad_ref[: 3 * wide, count:] = jnp.zeros((3 * wide, width - count), BF16)
    grad_ref[3 * wide : 4 * wide, :] = mm(mixed_ref[0], da_ref[...], NN).astype(BF16)
    grad_ref[4 * wide :, :] = vec_ref[...].astype(BF16)
    for head in range(wide // HEAD_DIM):
        row = head * HEAD_DIM
        for valid, low, high in ((valids[0], 0, PLEN), (valids[1], PLEN, count)):
            query = qkv_ref[0, row : row + HEAD_DIM, low:high]
            keys = qkv_ref[0, wide + row : wide + row + HEAD_DIM, low:high]
            values = qkv_ref[0, 2 * wide + row : 2 * wide + row + HEAD_DIM, low:high]
            upper = grad_mixed[row : row + HEAD_DIM, low:high]
            scores = jnp.where(valid, mm(keys, query, TN), -1000000000.0)
            shares = jnp.exp(scores - total_ref[0, head : head + 1, low:high])
            grad_shares = mm(values, upper, TN)
            inner = jnp.sum(shares * grad_shares, 0, keepdims=True)
            grad_scores = (shares * (grad_shares - inner)).astype(BF16)
            grad_ref[2 * wide + row : 2 * wide + row + HEAD_DIM, low:high] = mm(
                upper, shares.astype(BF16), NT
            ).astype(BF16)
            grad_ref[wide + row : wide + row + HEAD_DIM, low:high] = mm(query, grad_scores, NT).astype(BF16)
            grad_ref[row : row + HEAD_DIM, low:high] = (mm(keys, grad_scores, NN) * SCALE).astype(BF16)


def attend_back(lengths, da, qkv, total, mixed, vec, pack):
    _, wide, count = mixed.shape
    width = da.shape[1]
    return call(
        attend_back_kernel, "attend_back", [((4 * wide + vec.shape[0], width), BF16)], 2_000_000_000, 44,
        in_specs=[SMEM] + [VMEM] * 6,
    )(lengths, da, qkv, total, mixed, vec, pack)[0]


def head_grads_kernel(x_ref, x_core_ref, own_ref, core_ref, vec_ref, first_ref, second_ref):
    count = x_ref.shape[0]
    sums = vec_ref.shape[0]
    rows = own_ref.shape[0] - sums
    wide = rows // 4
    cut = first_ref.shape[0]
    dtype = second_ref.dtype
    grads = jnp.concatenate([own_ref[: 3 * wide, :count], core_ref[: 3 * wide, :count]], 1)
    tokens = jnp.concatenate([x_ref[...], x_core_ref[...]], 0)
    first_ref[...] = mm(grads[:cut], tokens, NN).astype(first_ref.dtype)
    second_ref[: 3 * wide - cut, :] = mm(grads[cut:], tokens, NN).astype(dtype)
    second_ref[3 * wide - cut : rows - cut, :] = (
        own_ref[3 * wide : rows].astype(F32) + core_ref[3 * wide : rows].astype(F32)
    ).astype(dtype)
    second_ref[rows - cut :, :] = jnp.zeros((second_ref.shape[0] - rows + cut, second_ref.shape[1]), dtype)
    ones = jnp.ones((16, grads.shape[1]), BF16)
    second_ref[rows - cut : rows - cut + 16, : 3 * wide] = mm(ones, grads, NT).astype(dtype)
    second_ref[rows - cut + 16 : rows - cut + 16 + sums, :] = (
        vec_ref[...] + core_ref[rows:].astype(F32)
    ).astype(dtype)


def head_grads(x, x_core, at_core, own, core, vec, dtype):
    count, width = x.shape
    rows = own.shape[0] - vec.shape[0]
    outs = [((CUT, width), F32), ((rows - CUT + 64, width), dtype)]
    return call(
        head_grads_kernel, "head_grads", outs, 1_500_000_000, 44, grid=(1,),
        in_specs=[
            whole(x.shape), pl.BlockSpec((count, width), lambda _: (0, at_core)), whole(own.shape),
            whole(core.shape), whole(vec.shape),
        ],
        out_specs=[whole(shape) for shape, _ in outs],
    )(x, x_core, own, core, vec)


def rows_kernel(wide, orders_ref, base_ref, beside_ref, *refs):
    out_ref = refs[-1]
    parts = (len(refs) - 1) // 2
    width = base_ref.shape[1]
    total = base_ref[...]
    for part in range(parts):
        grad_ref, pack_ref = refs[part], refs[parts + part]
        high = wide + 16
        for member in range(3):
            begin = pl.multiple_of((member ^ orders_ref[part]) * high, high)
            grad = grad_ref[member * wide : (member + 1) * wide, : base_ref.shape[0]]
            total = total + mm(grad, pack_ref[pl.ds(begin, wide), :], TN)
    out_ref[:, :width] = total.astype(BF16)
    out_ref[:, width:] = beside_ref[...]


def rows_back(orders, base, beside, grads, packs):
    shape = (base.shape[0], base.shape[1] + beside.shape[1])
    return call(
        functools.partial(rows_kernel, grads[0].shape[0] // 4 // 16 * 16), "rows_back", [(shape, BF16)], 2_000_000_000, 44, in_specs=[SMEM] + [VMEM] * (2 + 2 * len(packs)),
    )(orders, base, beside, *grads, *packs)[0]


def normed(hidden):
    center = hidden - jnp.mean(hidden, -1, keepdims=True)
    inverse = lax.rsqrt(jnp.mean(center * center, -1, keepdims=True) + 1e-06)
    return center * inverse, inverse


def norm_back(grad, unit, inverse, gain):
    grad_unit = grad * gain
    return inverse * (
        grad_unit
        - jnp.mean(grad_unit, -1, keepdims=True)
        - unit * jnp.mean(grad_unit * unit, -1, keepdims=True)
    )


def column_sum(values):
    return jnp.sum(values, 0, keepdims=True)


def put_halves(values, block, core, mine_ref, other_ref):
    if values.shape[1] < 2 * block:
        mine_ref[...] = values
        return
    sides = [
        jnp.concatenate(
            [values[:, at : at + block] for at in range(side * block, values.shape[1], 2 * block)], 1
        )
        for side in (0, 1)
    ]
    mine_ref[...] = jnp.where(core == 0, sides[0], sides[1])
    other_ref[...] = jnp.where(core == 0, sides[1], sides[0])


def forward_kernel(parts, block, scalars_ref, *refs):
    x_ref, params_ref, grads_ref, bias_ref, w_in_ref, w_down_ref = refs[:6]
    mixed_refs = refs[6 : 6 + parts]
    out_refs = refs[6 + parts : 6 + 2 * parts]
    r1_ref, a1_ref, mine_ref, pass_ref, slope_ref, out_ref, db_ref, dr2_ref, vec_ref = refs[6 + 2 * parts : -2]
    first_ref, sum_ref = refs[-2:]
    half_width = pass_ref.shape[1] - 3 * x_ref.shape[1]
    step, steps = pl.program_id(0), pl.num_programs(0)
    width = x_ref.shape[1]

    def param(at):
        return params_ref[at : at + 1, :].astype(F32)

    @pl.when(step == 0)
    def _():
        total = x_ref[...].astype(F32) + param(0)
        for part in range(parts):
            total = total + mm(mixed_refs[part][0], out_refs[part][...], TN)
        r1_ref[...] = total
        unit, _ = normed(total)
        first = unit * param(1) + param(2)
        first_ref[...] = first
        a1_ref[...] = first.astype(BF16)
        pass_ref[:, half_width + width : half_width + 2 * width] = first.astype(BF16)
        pass_ref[:, half_width + 2 * width :] = x_ref[...]
        sum_ref[...] = jnp.zeros_like(sum_ref)

    inner = mm(a1_ref[...], w_in_ref[...], NN) + bias_ref[...].astype(F32)
    square = inner * inner
    factor = math.sqrt(2.0 / math.pi)
    tanh = jnp.tanh(inner * (factor + (factor * 0.044715) * square))
    half = 0.5 + 0.5 * tanh
    active = (inner * half).astype(BF16)
    share = active.shape[1] // 2
    place = pl.ds(pl.multiple_of(step * share, share), share)
    put_halves(active, block, scalars_ref[parts], mine_ref, pass_ref.at[:, place])
    slope_ref[...] = half + inner * (0.5 - 0.5 * tanh * tanh) * (factor + (3 * factor * 0.044715) * square)
    sum_ref[...] += mm(active, w_down_ref[...], NN)

    @pl.when(step == steps - 1)
    def _():
        unit, inverse = normed(first_ref[...] + sum_ref[...] + param(3))
        gain = param(4)
        second = unit * gain + param(5)
        weight = param(6)
        logit = jnp.sum(second * weight, -1, keepdims=True) + params_ref[7:8, 0:1].astype(F32)
        term = jnp.maximum(logit, 0.0) + jnp.log1p(jnp.exp(-jnp.abs(logit)))
        sigmoid = 1.0 / (1.0 + jnp.exp(-logit))
        lane = lax.broadcasted_iota(jnp.int32, (term.shape[0], 128), 1)
        high = term.astype(BF16).astype(F32)
        middle = (term - high).astype(BF16).astype(F32)
        rest = term - high - middle
        tail = jnp.where(lane == 0, high, jnp.where(lane == 1, middle, jnp.where(lane == 2, rest, 0.0)))
        out_ref[:, :width] = second.astype(BF16)
        out_ref[:, width:] = tail.astype(BF16)
        grad_term = jnp.sum(grads_ref[:, width:].astype(F32), -1, keepdims=True)
        grad_logit = grad_term * sigmoid
        grad = grads_ref[:, :width].astype(F32) + grad_logit * weight
        back = norm_back(grad, unit, inverse, gain)
        db_ref[...] = back.astype(BF16)
        pass_ref[:, half_width : half_width + width] = back.astype(BF16)
        dr2_ref[...] = back
        vec_ref[...] = jnp.zeros_like(vec_ref)
        vec_ref[0:1, :] = column_sum(grad * unit)
        vec_ref[1:2, :] = column_sum(grad)
        vec_ref[2:3, :] = column_sum(back)
        vec_ref[3:4, :] = column_sum(grad_logit * second)
        scalar = jnp.broadcast_to(column_sum(grad_logit), (1, width))
        scaled = jnp.floor(jnp.abs(scalar) * param(8))
        digit = scaled - 2.0 * jnp.floor(0.5 * scaled)
        vec_ref[4:5, :] = jnp.where(scalar < 0, -digit, digit)


def forward(scalars, x, params, grads, b_in, w_in, w_down, mixed, packs, block, chunk):
    count, width = x.shape
    hidden = w_in.shape[1]
    wide = mixed[0].shape[1]
    parts = len(packs)
    specs = [
        whole(x.shape), whole(params.shape), whole(grads.shape),
        pl.BlockSpec((1, chunk), lambda j, o: (0, j)),
        pl.BlockSpec((width, chunk), lambda j, o: (0, j)),
        pl.BlockSpec((chunk, width), lambda j, o: (j, 0)),
    ]
    mixed = [(array, at) for array in mixed for at in range(array.shape[0])]
    specs += [
        pl.BlockSpec((1, wide, count), functools.partial(lambda at, j, o: (at, 0, 0), at)) for _, at in mixed
    ]
    specs += [
        pl.BlockSpec(
            (pl.Element(wide), pl.Element(width)),
            functools.partial(lambda part, j, o: ((3 ^ o[part]) * (wide + 16), 0), part),
        )
        for part in range(parts)
    ]
    share = 2 if chunk >= 2 * block else 1
    outs = [
        ((count, width), F32), ((count, width), BF16), ((count, hidden // share), BF16),
        ((count, hidden // 2 + 3 * width), BF16), ((count, hidden), F32),
        ((count, width + 128), BF16), ((count, width), BF16), ((count, width), F32), ((8, width), F32),
    ]
    out_specs = [whole(s) for s, _ in outs]
    out_specs[2] = pl.BlockSpec((count, chunk // share), lambda j, o: (0, j))
    out_specs[4] = pl.BlockSpec((count, chunk), lambda j, o: (0, j))
    return call(
        functools.partial(forward_kernel, parts, block), "forward", outs, 6_200_000_000, 44,
        grid=(hidden // chunk,), in_specs=specs, out_specs=out_specs, scalars=1,
        scratch=[pltpu.VMEM((count, width), F32), pltpu.VMEM((count, width), F32)],
    )(scalars, x, params, grads, b_in, w_in, w_down, *[array for array, _ in mixed], *packs)


def backward_kernel(
    block, scalars_ref, db_ref, slope_ref, w_down_ref, w_in_ref, r1_ref, dr2_ref, params_ref, vec_ref,
    dr1_ref, da_ref, out_vec_ref, mine_ref, other_ref, sum_ref
):
    step, steps = pl.program_id(0), pl.num_programs(0)

    @pl.when(step == 0)
    def _():
        sum_ref[...] = dr2_ref[...]
        out_vec_ref[:8, :] = vec_ref[...]
        out_vec_ref[8:, :] = jnp.zeros_like(vec_ref)

    grad_inner = mm(db_ref[...], w_down_ref[...], NT) * slope_ref[...]
    out_vec_ref[pl.ds(11 + step, 1), :] = column_sum(grad_inner)
    low = grad_inner.astype(BF16)
    put_halves(low, block, scalars_ref[0], mine_ref, other_ref)
    sum_ref[...] += mm(low, w_in_ref[...], NT)

    @pl.when(step == steps - 1)
    def _():
        grad = sum_ref[...]
        unit, inverse = normed(r1_ref[...])
        back = norm_back(grad, unit, inverse, params_ref[1:2, :].astype(F32))
        dr1_ref[...] = back
        da_ref[...] = back.astype(BF16)
        out_vec_ref[8:9, :] = column_sum(grad * unit)
        out_vec_ref[9:10, :] = column_sum(grad)
        out_vec_ref[10:11, :] = column_sum(back)


def backward(scalars, db, slope, w_down, w_in, r1, dr2, params, vec, block):
    count, width = db.shape
    hidden = w_in.shape[1]
    chunk = width
    share = 2 if chunk >= 2 * block else 1
    outs = [
        ((count, width), F32), ((count, width), BF16), ((16, width), F32),
        ((count, hidden // share), BF16), ((count, hidden // 2), BF16),
    ]
    out_specs = [whole(s) for s, _ in outs]
    out_specs[3] = pl.BlockSpec((count, chunk // share), lambda j, o: (0, j))
    out_specs[4] = pl.BlockSpec((count, chunk // 2), lambda j, o: (0, j))
    return call(
        functools.partial(backward_kernel, block), "backward", outs, 5_500_000_000, 44, grid=(hidden // chunk,),
        in_specs=[
            whole(db.shape),
            pl.BlockSpec((count, chunk), lambda j, o: (0, j)),
            pl.BlockSpec((chunk, width), lambda j, o: (j, 0)),
            pl.BlockSpec((width, chunk), lambda j, o: (0, j)),
            whole(r1.shape), whole(dr2.shape), whole(params.shape), whole(vec.shape),
        ],
        out_specs=out_specs, scalars=1, scratch=[pltpu.VMEM((count, width), F32)],
    )(scalars, db, slope, w_down, w_in, r1, dr2, params, vec)


def owner_grads_kernel(block, by_z, me_ref, left_ref, left_core_ref, right_ref, right_core_ref, send_ref, keep_ref, tile_ref):
    tile_ref[...] = mm(
        jnp.concatenate([left_ref[...], left_core_ref[...]], 0),
        jnp.concatenate([right_ref[...], right_core_ref[...]], 0),
        TN,
    )
    low = me_ref[0] & 3
    far = me_ref[1] >> 1
    for at in range(4):
        y, z = (at ^ low) & 1, (at ^ low) >> 1
        away, place = (z, y) if by_z else (y, z)
        for x in (0, 1):
            begin = pl.multiple_of(2 * block * at + block * (far ^ x), block)
            rows = tile_ref[pl.ds(begin, block), :]

            @pl.when(away == 1)
            def _():
                send_ref[(x, place, 0) if by_z else (place, x, 0)] = rows.astype(BF16)

            @pl.when(away == 0)
            def _():
                keep_ref[(x, place, 0) if by_z else (place, x, 0)] = rows


def owner_grads(me, left, left_core, right, right_core, at_core, block, by_z):
    count, half = left.shape
    width = right.shape[1]
    n_dp = half // (2 * block)
    chunk = 8 * block
    shape = (2, 2, n_dp // 4, block, width)
    spec = pl.BlockSpec((2, 2, 1, block, width), lambda j, me: (0, 0, j, 0, 0))
    columns = pl.BlockSpec((count, chunk), lambda j, me: (0, j ^ (me[0] >> 2)))
    return call(
        functools.partial(owner_grads_kernel, block, by_z), "owner_grads", [(shape, BF16), (shape, F32)],
        2_700_000_000, 44, grid=(half // chunk,),
        in_specs=[columns, columns, whole(right.shape), pl.BlockSpec((count, width), lambda j, me: (0, at_core))],
        out_specs=[spec, spec], scalars=1, scratch=[pltpu.VMEM((chunk, width), F32)],
    )(me, left, left_core, right, right_core)


def place_kernel(extra, me_ref, rows_ref, near_ref, *refs):
    query_refs, (grads_ref, out_ref, term_ref, all_ref) = refs[:-4], refs[-4:]
    count, width = grads_ref.shape
    passage = count - extra
    moved = near_ref.shape[0]
    all_ref[:passage, :] = rows_ref[:passage, :]
    all_ref[passage + moved :, :] = rows_ref[passage:, :]

    @pl.when(me_ref[1] == moved // extra)
    def _():
        all_ref[passage : passage + extra, :] = near_ref[:extra, :]
        for at, query_ref in enumerate(query_refs):
            begin = passage + extra * (at + 1)
            all_ref[begin : begin + extra, :] = query_ref[...]

    @pl.when(me_ref[1] != moved // extra)
    def _():
        all_ref[passage : passage + moved, :] = near_ref[...]

    rows = pl.ds(pl.multiple_of(me_ref[1] * extra, extra), count)
    grads_ref[...] = all_ref[rows, :width]
    out_ref[...] = all_ref[rows, width : 2 * width]
    term_ref[...] = mm(jnp.ones((8, 128), BF16), all_ref[rows, 2 * width :], NT)


def place_rows(me, rows, sent, extra, width):
    count = rows.shape[0]
    outs = [((count, width), BF16), ((count, width), BF16), ((8, count), F32)]
    return call(
        functools.partial(place_kernel, extra), "place_rows", outs, 1_000_000, 24,
        in_specs=[SMEM] + [VMEM] * (1 + len(sent)),
        scratch=[pltpu.VMEM((count + sent[0].shape[0], rows.shape[1]), BF16)],
    )(me, rows, *sent)


def swap(array, axis, bit, name="swap"):
    size = lax.axis_size(axis)
    with jax.named_scope(name + "_" + axis + str(bit)):
        return lax.ppermute(array, axis, [(at, at ^ bit) for at in range(size)])


def bits_of(size):
    return [1 << at for at in range(size.bit_length() - 1)]


def shift(rows, extra):
    heads = lax.axis_size("head")
    me = lax.axis_index("head")
    count = rows.shape[0]
    moved = extra * (heads - 1)
    begin = count - moved - jnp.where(me == heads - 1, extra, 0)
    return lax.dynamic_slice_in_dim(rows, begin, moved, 0)


def forth(payload):
    heads = lax.axis_size("head")
    return lax.ppermute(payload, "head", [(at, (at + 1) % heads) for at in range(heads)])


def queries_for(rows, extra, target):
    begin = rows.shape[0] - (lax.axis_size("head") - target) * extra
    return rows[begin : begin + extra]


def aligned(rows, received, sent, extra):
    me = lax.axis_index("head")
    count = rows.shape[0]
    moved = received.shape[0]
    passage = lax.dynamic_slice_in_dim(
        jnp.concatenate([received, rows], 0), moved - extra * me, count - extra, 0
    )
    query = jnp.where(
        me == 0, received[:extra], jnp.where(me == 1, sent[0], jnp.where(me == 2, sent[1], rows[count - extra :]))
    )
    return jnp.concatenate([passage, query], 0)


def back_payloads(rows, extra):
    moved = extra * (lax.axis_size("head") - 1)
    query = rows[rows.shape[0] - extra :]
    payload = jnp.where(
        lax.axis_index("head") == 0, jnp.concatenate([query, rows[: moved - extra]], 0), rows[:moved]
    )
    return payload, query


def send_back(payload, query):
    heads = lax.axis_size("head")
    return [lax.ppermute(payload, "head", [((at + 1) % heads, at) for at in range(heads)])] + [
        lax.ppermute(query, "head", [(source, heads - 1)]) for source in range(1, heads - 1)
    ]


def with_column(rows, values):
    high = lax.reduce_precision(values, 8, 7)
    rest = values - high
    middle = lax.reduce_precision(rest, 8, 7)
    parts = jnp.stack([high, middle, rest - middle], 1).astype(BF16)
    return jnp.concatenate([rows, jnp.pad(parts, ((0, 0), (0, 125)))], 1)


def after(value, *others):
    return lax.optimization_barrier((*others, value))[-1]


class Scatter:
    def __init__(self, send, keep, sent, names, label):
        self.names, self.label, self.current, self.away = list(names), label, keep, None
        self.received = self.swap(send, sent)

    def swap(self, away, name):
        axis, bit = ("head", 2) if name == "x" else ("dp", int(name[2:]))
        return swap(away, axis, bit, self.label)

    def prepare(self, *before):
        shape = self.current.shape[1:]
        self.received = after(self.received, *before) if before else self.received

        def side(which):
            return self.current[which].reshape(shape) + self.received[which].astype(F32).reshape(shape)

        self.away = side(1).astype(BF16)
        self.current = side(0)
        return self.away

    def step(self, *before):
        if self.away is None:
            self.prepare(*before)
        away = after(self.away, *before) if before else self.away
        self.received, self.away = self.swap(away, self.names.pop(0)), None
        return away

    def result(self):
        return self.current + self.received.astype(F32)


class Total:
    def __init__(self, keep, far, steps, label):
        self.label, self.keep, self.far, self.steps = label, keep, far, list(steps)
        self.received, self.kind = None, None
        dp = [name for name in steps if name != "x"]
        self.steps += dp[:-1][::-1]
        self.middle = dp[-1]
        self.backs = len(dp) - 1
        self.me = lax.axis_index("dp")

    def merged(self):
        kind, received = self.kind, self.received
        if kind == "back":
            return jnp.where(
                self.mine,
                jnp.concatenate([received, self.keep], 0),
                jnp.concatenate([self.keep, received], 0),
            )
        if kind == "both":
            rows = self.keep.shape[0]
            self.far = self.far + received[:rows].astype(F32)
            received = received[rows:]
        if kind is not None:
            return self.keep.astype(F32) + received.astype(F32)
        return self.keep

    def step(self, *before):
        name = self.steps.pop(0)
        if before:
            tied = [value for value in (self.keep, self.far, self.received) if value is not None]
            tied = list(lax.optimization_barrier((*before, *tied))[len(before) :])
            self.keep = tied.pop(0)
            if self.far is not None:
                self.far = tied.pop(0)
            if self.received is not None:
                self.received = tied.pop(0)
        block = self.merged()
        if name == "x":
            away, self.far = self.far.astype(BF16), None
            self.keep, self.kind = block, "add"
            self.received = swap(away, "head", 2, self.label)
            return away
        bit = int(name[2:])
        self.mine = (self.me & bit) != 0
        if name == self.middle:
            away = self.keep = block.astype(BF16)
            self.kind = "add"
        elif len(self.steps) < self.backs:
            away = self.keep = block.astype(BF16)
            self.kind = "back"
        else:
            half = block.shape[0] // 2
            side = self.mine.astype(jnp.int32)

            def part(array, which):
                return lax.dynamic_slice_in_dim(array, which * half, half, 0)

            away = part(block, 1 - side).astype(BF16)
            self.keep, self.kind = part(block, side), "add"
            if self.far is not None:
                away = jnp.concatenate([part(self.far, 1 - side).astype(BF16), away], 0)
                self.far, self.kind = part(self.far, side), "both"
        self.received = swap(away, "dp", bit, self.label)
        return away


TAIL = "ipabdiababadbdiabtu"


def shards(
    tokens, w_qkv, b_qv, w_out, b_out, gain_one, shift_one, w_in, b_in, w_down, b_down,
    gain_two, shift_two, w_term, b_term, pass_len, query_len, grad_out, grad_term,
):
    n_dp, n_head = lax.axis_size("dp"), lax.axis_size("head")
    me, me_dp = lax.axis_index("head"), lax.axis_index("dp")
    width = tokens.shape[1]
    wide = w_qkv.shape[2]
    hidden = w_in.shape[1]
    extra = query_len.shape[0] * QLEN // n_head
    block = hidden // (n_dp * n_head)
    owners = n_head == 4 and block == 96
    chunk = 768

    shifted = shift(tokens, extra)
    weights = after(w_qkv, shifted)
    bias = jnp.zeros((4, 16, width), BF16).at[0, 0, :wide].set(b_qv[0]).at[2, 0, :wide].set(b_qv[1])
    own = jnp.concatenate([jnp.concatenate([weights.transpose(0, 2, 1), w_out[None]], 0), bias], 1)
    high = own.shape[1]
    turn = me_dp & 3
    received = forth(shifted)
    query = lax.ppermute(queries_for(tokens, extra, 1), "head", [(n_head - 1, 1)])
    pieces = [swap(lax.dynamic_index_in_dim(own, turn, 0, keepdims=False), "head", 2, "weights")]
    own = own.reshape(-1, width)
    beside = jnp.concatenate([own, queries_for(tokens, extra, 2)], 0)
    second = lax.dynamic_slice_in_dim(after(own, beside), (turn ^ 3) * high, high, 0)
    beside = swap(beside, "head", 1, "weights")
    last = swap(second, "head", 2, "weights")
    rows = aligned(tokens, received, (query, beside[4 * high :]), extra)
    packs = [own, beside]
    counts = (pass_len.shape[0], query_len.shape[0])
    near = jnp.concatenate(
        [
            jnp.stack([jnp.zeros_like(me), 3 + me, 3 + counts[0] + me * (counts[1] // n_head)]).astype(jnp.int32),
            pass_len, query_len,
        ]
    )
    distant = jnp.concatenate([turn.astype(jnp.int32)[None], near[1:]])
    core = (me & 1).astype(jnp.int32)[None]
    scalars = jnp.concatenate([jnp.zeros((2,), jnp.int32), distant[:1], distant[:1], core])
    digits = np.zeros((width,), np.float32)
    digits[:36] = 2.0 ** (np.arange(36) - 11)
    params = jnp.concatenate(
        [b_out, gain_one, shift_one, b_down, gain_two, shift_two, w_term, b_term]
        + [jnp.zeros((width - 1,), BF16), jnp.asarray(digits, BF16), jnp.zeros((7 * width,), BF16)]
    ).reshape(16, width)
    place = jnp.stack([me_dp, me]).astype(jnp.int32)

    saved = [attend(near, rows, packs[0], wide)]
    pieces = [after(pieces[0], saved[0][1])]
    pieces += [swap(pieces[0], "dp", 1, "weights"), swap(pieces[0], "dp", 2, "weights"), last]
    rows_then, packs[1] = lax.optimization_barrier((after(rows, saved[0][1]), packs[1]))
    saved.append(attend(near, rows_then, packs[1], wide))
    pieces = lax.optimization_barrier((saved[1][1], *pieces))[1:]
    packs.append(jnp.concatenate(pieces, 0))
    packs.append(swap(packs[2], "head", 1, "weights"))
    with_terms = with_column(after(grad_out, saved[0][1]), grad_term)
    with_terms = after(with_terms, saved[1][1])
    given = [forth(shift(with_terms, extra))] + [
        lax.ppermute(queries_for(with_terms, extra, target), "head", [(n_head - 1, target)]) for target in (1, 2)
    ]
    saved.append(attend(distant, rows, packs[2], wide))
    rows_then, packs[3] = lax.optimization_barrier((after(rows, saved[2][1]), packs[3]))
    saved.append(attend(distant, rows_then, packs[3], wide))
    given = lax.optimization_barrier((saved[3][1], *given))[1:]
    grads_in = aligned(with_terms, given[0], given[1:], extra)
    split = block if owners else hidden
    r1, a1, mine, given, slope, out_rows, db, dr2, vec = forward(
        scalars, rows, params, grads_in, b_in[None], w_in, w_down, [m for _, m, _ in saved], packs, split, chunk
    )
    given_core = swap(given, "head", 1, "given")
    dr1, da, vec, dz_mine, dz_other = backward(core, db, slope, w_down, w_in, r1, dr2, params, vec, split)
    names = ["dp%d" % bit for bit in bits_of(n_dp)]
    at_core = hidden // 2 // width
    if owners:
        dz_core = swap(dz_other, "head", 1, "inner")
        place, given_core = lax.optimization_barrier((after(place, da), given_core))
        send, keep = owner_grads(place, mine, given_core, db, given_core, at_core, block, True)
        down = Scatter(send, keep, names[1], ["x", names[0]] + names[2:], "down")
        place, dz_core = lax.optimization_barrier((after(place, send), dz_core))
        send, keep = owner_grads(place, dz_mine, dz_core, a1, given_core, at_core + 1, block, False)
        inner = Scatter(send, keep, names[0], [names[1], "x"] + names[2:], "inner")
        da = after(da, send)
    else:
        both = ("dp", "head")
        grad_w_down = lax.psum_scatter(mm(mine, db, TN), both, scatter_dimension=0, tiled=True)
        grad_w_in = lax.psum_scatter(mm(dz_mine, a1, TN), both, scatter_dimension=0, tiled=True)

    def back(part, da):
        qkv, mixed, total = saved[part]
        return attend_back(distant if part > 1 else near, da, qkv, total, mixed, vec, packs[part])

    def heads(part, own, core, dtype):
        return head_grads(rows, given_core, at_core + 2, own, core, vec, dtype)

    grads, then = {}, da
    for part in (3, 2, 1, 0):
        grads[part] = back(part, after(da, then))
        then = grads[part]
    far_core, near_core = swap(grads[3], "head", 1, "far"), swap(grads[1], "head", 1, "near")
    combined = rows_back(scalars, after(dr1, then), out_rows, [grads[part] for part in range(n_head)], packs)
    far_then = after(grads[2], combined)
    if owners:
        far_then, down.received = lax.optimization_barrier((far_then, down.received))
        far_then, inner.received = lax.optimization_barrier((far_then, inner.received))
    far_then, far_core, near_core = lax.optimization_barrier((far_then, far_core, near_core))
    far_sum = heads(2, far_then, far_core, BF16)
    near_sum = heads(0, after(grads[0], far_sum[1]), near_core, F32)
    steps = ["dp%d" % bit for bit in bits_of(n_dp)]
    totals = [
        Total(near_sum[1], far_sum[1], ["x"] + steps, "first"),
        Total(near_sum[0], far_sum[0], steps[:1] + ["x"] + steps[1:], "second"),
    ]
    totals[0].step()
    then = totals[1].step()
    done = [then]

    def step(one):
        done[:] = [one.step(*done)]

    scatters = {"d": down, "i": inner} if owners else {}
    for item in TAIL:
        if item in "ab":
            total = totals["ab".index(item)]
            if total.steps:
                step(total)
        elif item == "t":
            shifted = send_back(*lax.optimization_barrier((*done, *payloads))[len(done) :])
        elif item == "p":
            payloads = back_payloads(after(combined, *done), extra)
        elif item == "w":
            shifted = lax.optimization_barrier((*done, *shifted))[len(done) :]
            done[:] = shifted[1:2]
        elif item in "ej":
            one = scatters.get("di"["ej".index(item)])
            if one and one.names:
                done[:] = [one.prepare(*done)]
        elif item == "u":
            shifted[0] = after(shifted[0], *done)
            shifted = lax.optimization_barrier(tuple(shifted))
            grad_tokens, out, term = place_rows(place, combined, shifted, extra, width)
        elif item in scatters and scatters[item].names:
            step(scatters[item])
    for total in totals:
        while total.steps:
            step(total)
    for one in scatters.values():
        while one.names:
            step(one)
    if owners:
        grad_w_down, grad_w_in = down.result().reshape(block, width), inner.result().reshape(block, width)
    total = jnp.concatenate([one.merged() for one in totals[::-1]], 0).astype(F32)
    grad_w_qkv = total[: 3 * wide].reshape(3, wide, width).transpose(0, 2, 1)
    grad_w_out = total[3 * wide : 4 * wide]
    bias_row, sums = total[4 * wide], total[4 * wide + 16 : 4 * wide + 32]
    grad_b_qv = jnp.stack([bias_row[:wide], bias_row[2 * wide : 3 * wide]])
    grad_b_term = jnp.sum(sums[4, :36] * jnp.asarray(2.0 ** (11 - np.arange(36)), F32))[None]
    return (
        out, term[0], grad_tokens, grad_w_qkv, grad_b_qv, grad_w_out, sums[10], sums[8],
        sums[9], grad_w_in.T, sums[11:15].reshape(-1), grad_w_down, sums[2], sums[0], sums[1],
        sums[3], grad_b_term,
    )


def solution(mesh):
    both = ("dp", "head")
    placed = (
        P(both, None), P(None, None, "head"), P(None, "head"), P("head", None),
        P(), P(), P(), P(), P(), P(), P(), P(), P(), P(), P(),
        P("dp"), P("dp"), P(both, None), P(both),
    )
    return jax.shard_map(
        shards,
        mesh=mesh,
        in_specs=placed,
        out_specs=(
            P(both, None), P(both), P(both, None), P(None, None, "head"), P(None, "head"),
            P("head", None), P(), P(), P(), P(None, both), P(), P(both, None),
            P(), P(), P(), P(), P(),
        ),
        check_vma=False,
    )
```

```python
import functools
import math

import jax
import jax.numpy as jnp
import numpy as np
from jax import lax
from jax.experimental import pallas as pl
from jax.experimental.pallas import tpu as pltpu
from jax.sharding import PartitionSpec as P

HEAD_DIM = 64
PLEN = 512
QLEN = 32
F32 = jnp.float32
BF16 = jnp.bfloat16
NN = (((1,), (0,)), ((), ()))
NT = (((1,), (1,)), ((), ()))
TN = (((0,), (0,)), ((), ()))
SCALE = 1.0 / math.sqrt(HEAD_DIM)
MIB = 1024 * 1024
CUT = 384
SMEM = pl.BlockSpec(memory_space=pltpu.SMEM)
VMEM = pl.BlockSpec(memory_space=pltpu.VMEM)


def mm(left, right, dims):
    return lax.dot_general(left, right, dims, preferred_element_type=F32)


def whole(shape):
    zeros = (0,) * len(shape)
    return pl.BlockSpec(shape, lambda *_: zeros)


def call(kernel, name, outs, flops, mib, grid=None, in_specs=None, out_specs=None, scratch=(), scalars=0):
    options = dict(
        out_shape=[jax.ShapeDtypeStruct(shape, dtype) for shape, dtype in outs],
        compiler_params=pltpu.CompilerParams(vmem_limit_bytes=mib * MIB),
        cost_estimate=pl.CostEstimate(flops=flops * 100, bytes_accessed=flops // 5, transcendentals=0),
        name=name,
    )
    if grid is None:
        return pl.pallas_call(
            kernel, in_specs=in_specs, out_specs=[VMEM] * len(outs), scratch_shapes=list(scratch), **options
        )
    spec = pltpu.PrefetchScalarGridSpec(
        num_scalar_prefetch=scalars, grid=grid, in_specs=in_specs, out_specs=out_specs,
        scratch_shapes=list(scratch),
    )
    return pl.pallas_call(kernel, grid_spec=spec, **options)


def masks(lengths_ref, extra):
    long_key = lax.broadcasted_iota(jnp.int32, (PLEN, PLEN), 0)
    key = lax.broadcasted_iota(jnp.int32, (extra, extra), 0)
    row = lax.broadcasted_iota(jnp.int32, (extra, extra), 1)
    short = jnp.zeros((extra, extra), jnp.bool_)
    for at in range(extra // QLEN):
        low, high = at * QLEN, (at + 1) * QLEN
        short = short | (
            (key >= low) & (key < low + lengths_ref[lengths_ref[2] + at]) & (row >= low) & (row < high)
        )
    return long_key < lengths_ref[lengths_ref[1]], short


def attend_kernel(lengths_ref, x_ref, *refs):
    pack_refs, (qkv_ref, mixed_ref, total_ref) = refs[:-3], refs[-3:]
    wide = mixed_ref.shape[1]
    pitch = wide + 16
    count = x_ref.shape[0]
    ones = jnp.ones((16, count), BF16)
    order = lengths_ref[0]
    valids = masks(lengths_ref, count - PLEN)
    total_ref[...] = jnp.zeros_like(total_ref)
    for at, pack_ref in enumerate(pack_refs):
        for member in range(3):
            begin = pl.multiple_of((member ^ order) * pitch, pitch)
            part = mm(pack_ref[pl.ds(begin, wide), :], x_ref[...], NT)
            if member != 1:
                part = part + mm(pack_ref[pl.ds(begin + wide, 16), :wide], ones, TN)
            part = part.astype(BF16)
            qkv_ref[at, member * wide : (member + 1) * wide, :] = part * BF16(SCALE) if member == 0 else part
        for head in range(wide // HEAD_DIM):
            row = head * HEAD_DIM
            for valid, low, high in ((valids[0], 0, PLEN), (valids[1], PLEN, count)):
                query = qkv_ref[at, row : row + HEAD_DIM, low:high]
                keys = qkv_ref[at, wide + row : wide + row + HEAD_DIM, low:high]
                values = qkv_ref[at, 2 * wide + row : 2 * wide + row + HEAD_DIM, low:high]
                scores = jnp.where(valid, mm(keys, query, TN), -1000000000.0)
                top = jnp.max(scores, 0, keepdims=True)
                exponent = jnp.exp(scores - top)
                total = jnp.sum(exponent, 0, keepdims=True)
                shares = (exponent * (1.0 / total)).astype(BF16)
                mixed_ref[at, row : row + HEAD_DIM, low:high] = mm(values, shares, NN).astype(BF16)
                total_ref[at, head : head + 1, low:high] = top + jnp.log(total)


def attend(lengths, x, pack, wide):
    count = x.shape[0]
    outs = [((1, 3 * wide, count), BF16), ((1, wide, count), BF16), ((1, 8, count), F32)]
    return call(attend_kernel, "attend", outs, 1_200_000_000, 44, in_specs=[SMEM] + [VMEM] * 2)(lengths, x, pack)


def attend_back_kernel(lengths_ref, da_ref, qkv_ref, total_ref, mixed_ref, vec_ref, pack_ref, grad_ref):
    wide = mixed_ref.shape[1]
    count, width = da_ref.shape
    valids = masks(lengths_ref, count - PLEN)
    begin = pl.multiple_of((3 ^ lengths_ref[0]) * (wide + 16), wide + 16)
    grad_mixed = mm(pack_ref[pl.ds(begin, wide), :], da_ref[...], NT).astype(BF16)
    grad_ref[: 3 * wide, count:] = jnp.zeros((3 * wide, width - count), BF16)
    grad_ref[3 * wide : 4 * wide, :] = mm(mixed_ref[0], da_ref[...], NN).astype(BF16)
    grad_ref[4 * wide :, :] = vec_ref[...].astype(BF16)
    for head in range(wide // HEAD_DIM):
        row = head * HEAD_DIM
        for valid, low, high in ((valids[0], 0, PLEN), (valids[1], PLEN, count)):
            query = qkv_ref[0, row : row + HEAD_DIM, low:high]
            keys = qkv_ref[0, wide + row : wide + row + HEAD_DIM, low:high]
            values = qkv_ref[0, 2 * wide + row : 2 * wide + row + HEAD_DIM, low:high]
            upper = grad_mixed[row : row + HEAD_DIM, low:high]
            scores = jnp.where(valid, mm(keys, query, TN), -1000000000.0)
            shares = jnp.exp(scores - total_ref[0, head : head + 1, low:high])
            grad_shares = mm(values, upper, TN)
            inner = jnp.sum(shares * grad_shares, 0, keepdims=True)
            grad_scores = (shares * (grad_shares - inner)).astype(BF16)
            grad_ref[2 * wide + row : 2 * wide + row + HEAD_DIM, low:high] = mm(
                upper, shares.astype(BF16), NT
            ).astype(BF16)
            grad_ref[wide + row : wide + row + HEAD_DIM, low:high] = mm(query, grad_scores, NT).astype(BF16)
            grad_ref[row : row + HEAD_DIM, low:high] = (mm(keys, grad_scores, NN) * SCALE).astype(BF16)


def attend_back(lengths, da, qkv, total, mixed, vec, pack):
    _, wide, count = mixed.shape
    width = da.shape[1]
    return call(
        attend_back_kernel, "attend_back", [((4 * wide + vec.shape[0], width), BF16)], 2_000_000_000, 36,
        in_specs=[SMEM] + [VMEM] * 6,
    )(lengths, da, qkv, total, mixed, vec, pack)[0]


def head_grads_kernel(x_ref, x_core_ref, own_ref, core_ref, vec_ref, first_ref, second_ref):
    count = x_ref.shape[0]
    sums = vec_ref.shape[0]
    rows = own_ref.shape[0] - sums
    wide = rows // 4
    cut = first_ref.shape[0]
    dtype = second_ref.dtype
    grads = jnp.concatenate([own_ref[: 3 * wide, :count], core_ref[: 3 * wide, :count]], 1)
    tokens = jnp.concatenate([x_ref[...], x_core_ref[...]], 0)
    first_ref[...] = mm(grads[:cut], tokens, NN).astype(first_ref.dtype)
    second_ref[: 3 * wide - cut, :] = mm(grads[cut:], tokens, NN).astype(dtype)
    second_ref[3 * wide - cut : rows - cut, :] = (
        own_ref[3 * wide : rows].astype(F32) + core_ref[3 * wide : rows].astype(F32)
    ).astype(dtype)
    second_ref[rows - cut :, :] = jnp.zeros((second_ref.shape[0] - rows + cut, second_ref.shape[1]), dtype)
    ones = jnp.ones((16, grads.shape[1]), BF16)
    second_ref[rows - cut : rows - cut + 16, : 3 * wide] = mm(ones, grads, NT).astype(dtype)
    second_ref[rows - cut + 16 : rows - cut + 16 + sums, :] = (
        vec_ref[...] + core_ref[rows:].astype(F32)
    ).astype(dtype)


def head_grads(x, x_core, at_core, own, core, vec, dtype):
    count, width = x.shape
    rows = own.shape[0] - vec.shape[0]
    outs = [((CUT, width), F32), ((rows - CUT + 64, width), dtype)]
    return call(
        head_grads_kernel, "head_grads", outs, 1_500_000_000, 44, grid=(1,),
        in_specs=[
            whole(x.shape), pl.BlockSpec((count, width), lambda _: (0, at_core)), whole(own.shape),
            whole(core.shape), whole(vec.shape),
        ],
        out_specs=[whole(shape) for shape, _ in outs],
    )(x, x_core, own, core, vec)


def rows_kernel(wide, orders_ref, base_ref, beside_ref, *refs):
    out_ref = refs[-1]
    parts = (len(refs) - 1) // 2
    width = base_ref.shape[1]
    total = base_ref[...]
    for part in range(parts):
        grad_ref, pack_ref = refs[part], refs[parts + part]
        high = wide + 16
        for member in range(3):
            begin = pl.multiple_of((member ^ orders_ref[part]) * high, high)
            grad = grad_ref[member * wide : (member + 1) * wide, : base_ref.shape[0]]
            total = total + mm(grad, pack_ref[pl.ds(begin, wide), :], TN)
    out_ref[:, :width] = total.astype(BF16)
    out_ref[:, width:] = beside_ref[...]


def rows_back(orders, base, beside, grads, packs):
    shape = (base.shape[0], base.shape[1] + beside.shape[1])
    return call(
        functools.partial(rows_kernel, grads[0].shape[0] // 4 // 16 * 16), "rows_back", [(shape, BF16)], 2_000_000_000, 60, in_specs=[SMEM] + [VMEM] * (2 + 2 * len(packs)),
    )(orders, base, beside, *grads, *packs)[0]


def normed(hidden):
    center = hidden - jnp.mean(hidden, -1, keepdims=True)
    inverse = lax.rsqrt(jnp.mean(center * center, -1, keepdims=True) + 1e-06)
    return center * inverse, inverse


def norm_back(grad, unit, inverse, gain):
    grad_unit = grad * gain
    return inverse * (
        grad_unit
        - jnp.mean(grad_unit, -1, keepdims=True)
        - unit * jnp.mean(grad_unit * unit, -1, keepdims=True)
    )


def column_sum(values):
    return jnp.sum(values, 0, keepdims=True)


def put_halves(values, block, core, mine_ref, other_ref):
    if values.shape[1] < 2 * block:
        mine_ref[...] = values
        return
    sides = [
        jnp.concatenate(
            [values[:, at : at + block] for at in range(side * block, values.shape[1], 2 * block)], 1
        )
        for side in (0, 1)
    ]
    mine_ref[...] = jnp.where(core == 0, sides[0], sides[1])
    other_ref[...] = jnp.where(core == 0, sides[1], sides[0])


def forward_kernel(parts, block, scalars_ref, *refs):
    x_ref, params_ref, grads_ref, bias_ref, w_in_ref, w_down_ref = refs[:6]
    mixed_refs = refs[6 : 6 + parts]
    out_refs = refs[6 + parts : 6 + 2 * parts]
    r1_ref, a1_ref, mine_ref, pass_ref, slope_ref, out_ref, db_ref, dr2_ref, vec_ref = refs[6 + 2 * parts : -2]
    first_ref, sum_ref = refs[-2:]
    half_width = pass_ref.shape[1] - 3 * x_ref.shape[1]
    step, steps = pl.program_id(0), pl.num_programs(0)
    width = x_ref.shape[1]

    def param(at):
        return params_ref[at : at + 1, :].astype(F32)

    @pl.when(step == 0)
    def _():
        total = x_ref[...].astype(F32) + param(0)
        for part in range(parts):
            total = total + mm(mixed_refs[part][0], out_refs[part][...], TN)
        r1_ref[...] = total
        unit, _ = normed(total)
        first = unit * param(1) + param(2)
        first_ref[...] = first
        a1_ref[...] = first.astype(BF16)
        pass_ref[:, half_width + width : half_width + 2 * width] = first.astype(BF16)
        pass_ref[:, half_width + 2 * width :] = x_ref[...]
        sum_ref[...] = jnp.zeros_like(sum_ref)

    inner = mm(a1_ref[...], w_in_ref[...], NN) + bias_ref[...].astype(F32)
    square = inner * inner
    factor = math.sqrt(2.0 / math.pi)
    tanh = jnp.tanh(inner * (factor + (factor * 0.044715) * square))
    half = 0.5 + 0.5 * tanh
    active = (inner * half).astype(BF16)
    share = active.shape[1] // 2
    place = pl.ds(pl.multiple_of(step * share, share), share)
    put_halves(active, block, scalars_ref[parts], mine_ref, pass_ref.at[:, place])
    slope_ref[...] = half + inner * (0.5 - 0.5 * tanh * tanh) * (factor + (3 * factor * 0.044715) * square)
    sum_ref[...] += mm(active, w_down_ref[...], NN)

    @pl.when(step == steps - 1)
    def _():
        unit, inverse = normed(first_ref[...] + sum_ref[...] + param(3))
        gain = param(4)
        second = unit * gain + param(5)
        weight = param(6)
        logit = jnp.sum(second * weight, -1, keepdims=True) + params_ref[7:8, 0:1].astype(F32)
        term = jnp.maximum(logit, 0.0) + jnp.log1p(jnp.exp(-jnp.abs(logit)))
        sigmoid = 1.0 / (1.0 + jnp.exp(-logit))
        lane = lax.broadcasted_iota(jnp.int32, (term.shape[0], 128), 1)
        high = term.astype(BF16).astype(F32)
        middle = (term - high).astype(BF16).astype(F32)
        rest = term - high - middle
        tail = jnp.where(lane == 0, high, jnp.where(lane == 1, middle, jnp.where(lane == 2, rest, 0.0)))
        out_ref[:, :width] = second.astype(BF16)
        out_ref[:, width:] = tail.astype(BF16)
        grad_term = jnp.sum(grads_ref[:, width:].astype(F32), -1, keepdims=True)
        grad_logit = grad_term * sigmoid
        grad = grads_ref[:, :width].astype(F32) + grad_logit * weight
        back = norm_back(grad, unit, inverse, gain)
        db_ref[...] = back.astype(BF16)
        pass_ref[:, half_width : half_width + width] = back.astype(BF16)
        dr2_ref[...] = back
        vec_ref[...] = jnp.zeros_like(vec_ref)
        vec_ref[0:1, :] = column_sum(grad * unit)
        vec_ref[1:2, :] = column_sum(grad)
        vec_ref[2:3, :] = column_sum(back)
        vec_ref[3:4, :] = column_sum(grad_logit * second)
        scalar = jnp.broadcast_to(column_sum(grad_logit), (1, width))
        scaled = jnp.floor(jnp.abs(scalar) * param(8))
        digit = scaled - 2.0 * jnp.floor(0.5 * scaled)
        vec_ref[4:5, :] = jnp.where(scalar < 0, -digit, digit)


def forward(scalars, x, params, grads, b_in, w_in, w_down, mixed, packs, block, chunk):
    count, width = x.shape
    hidden = w_in.shape[1]
    wide = mixed[0].shape[1]
    parts = len(packs)
    specs = [
        whole(x.shape), whole(params.shape), whole(grads.shape),
        pl.BlockSpec((1, chunk), lambda j, o: (0, j)),
        pl.BlockSpec((width, chunk), lambda j, o: (0, j)),
        pl.BlockSpec((chunk, width), lambda j, o: (j, 0)),
    ]
    mixed = [(array, at) for array in mixed for at in range(array.shape[0])]
    specs += [
        pl.BlockSpec((1, wide, count), functools.partial(lambda at, j, o: (at, 0, 0), at)) for _, at in mixed
    ]
    specs += [
        pl.BlockSpec(
            (pl.Element(wide), pl.Element(width)),
            functools.partial(lambda part, j, o: ((3 ^ o[part]) * (wide + 16), 0), part),
        )
        for part in range(parts)
    ]
    share = 2 if chunk >= 2 * block else 1
    outs = [
        ((count, width), F32), ((count, width), BF16), ((count, hidden // share), BF16),
        ((count, hidden // 2 + 3 * width), BF16), ((count, hidden), F32),
        ((count, width + 128), BF16), ((count, width), BF16), ((count, width), F32), ((8, width), F32),
    ]
    out_specs = [whole(s) for s, _ in outs]
    out_specs[2] = pl.BlockSpec((count, chunk // share), lambda j, o: (0, j))
    out_specs[4] = pl.BlockSpec((count, chunk), lambda j, o: (0, j))
    return call(
        functools.partial(forward_kernel, parts, block), "forward", outs, 6_200_000_000, 44,
        grid=(hidden // chunk,), in_specs=specs, out_specs=out_specs, scalars=1,
        scratch=[pltpu.VMEM((count, width), F32), pltpu.VMEM((count, width), F32)],
    )(scalars, x, params, grads, b_in, w_in, w_down, *[array for array, _ in mixed], *packs)


def backward_kernel(
    block, scalars_ref, db_ref, slope_ref, w_down_ref, w_in_ref, r1_ref, dr2_ref, params_ref, vec_ref,
    dr1_ref, da_ref, out_vec_ref, mine_ref, other_ref, sum_ref
):
    step, steps = pl.program_id(0), pl.num_programs(0)

    @pl.when(step == 0)
    def _():
        sum_ref[...] = dr2_ref[...]
        out_vec_ref[:8, :] = vec_ref[...]
        out_vec_ref[8:, :] = jnp.zeros_like(vec_ref)

    grad_inner = mm(db_ref[...], w_down_ref[...], NT) * slope_ref[...]
    out_vec_ref[pl.ds(11 + step, 1), :] = column_sum(grad_inner)
    low = grad_inner.astype(BF16)
    put_halves(low, block, scalars_ref[0], mine_ref, other_ref)
    sum_ref[...] += mm(low, w_in_ref[...], NT)

    @pl.when(step == steps - 1)
    def _():
        grad = sum_ref[...]
        unit, inverse = normed(r1_ref[...])
        back = norm_back(grad, unit, inverse, params_ref[1:2, :].astype(F32))
        dr1_ref[...] = back
        da_ref[...] = back.astype(BF16)
        out_vec_ref[8:9, :] = column_sum(grad * unit)
        out_vec_ref[9:10, :] = column_sum(grad)
        out_vec_ref[10:11, :] = column_sum(back)


def backward(scalars, db, slope, w_down, w_in, r1, dr2, params, vec, block):
    count, width = db.shape
    hidden = w_in.shape[1]
    chunk = width
    share = 2 if chunk >= 2 * block else 1
    outs = [
        ((count, width), F32), ((count, width), BF16), ((16, width), F32),
        ((count, hidden // share), BF16), ((count, hidden // 2), BF16),
    ]
    out_specs = [whole(s) for s, _ in outs]
    out_specs[3] = pl.BlockSpec((count, chunk // share), lambda j, o: (0, j))
    out_specs[4] = pl.BlockSpec((count, chunk // 2), lambda j, o: (0, j))
    return call(
        functools.partial(backward_kernel, block), "backward", outs, 5_500_000_000, 44, grid=(hidden // chunk,),
        in_specs=[
            whole(db.shape),
            pl.BlockSpec((count, chunk), lambda j, o: (0, j)),
            pl.BlockSpec((chunk, width), lambda j, o: (j, 0)),
            pl.BlockSpec((width, chunk), lambda j, o: (0, j)),
            whole(r1.shape), whole(dr2.shape), whole(params.shape), whole(vec.shape),
        ],
        out_specs=out_specs, scalars=1, scratch=[pltpu.VMEM((count, width), F32)],
    )(scalars, db, slope, w_down, w_in, r1, dr2, params, vec)


def owner_grads_kernel(block, x_next, me_ref, left_ref, left_core_ref, right_ref, right_core_ref, send_ref, keep_ref, tile_ref):
    tile_ref[...] = mm(
        jnp.concatenate([left_ref[...], left_core_ref[...]], 0),
        jnp.concatenate([right_ref[...], right_core_ref[...]], 0),
        TN,
    )
    low = me_ref[0] & 3
    far = me_ref[1] >> 1
    for at in range(4):
        y, z = (at ^ low) & 1, (at ^ low) >> 1
        for x in (0, 1):
            begin = pl.multiple_of(2 * block * at + block * (far ^ x), block)
            rows = tile_ref[pl.ds(begin, block), :]
            place = (x, y, 0) if x_next else (y, x, 0)

            @pl.when(z == 1)
            def _():
                send_ref[place] = rows.astype(BF16)

            @pl.when(z == 0)
            def _():
                keep_ref[place] = rows


def owner_grads(me, left, left_core, right, right_core, at_core, block, x_next):
    count, half = left.shape
    width = right.shape[1]
    n_dp = half // (2 * block)
    chunk = 8 * block
    shape = (2, 2, n_dp // 4, block, width)
    spec = pl.BlockSpec((2, 2, 1, block, width), lambda j, me: (0, 0, j, 0, 0))
    columns = pl.BlockSpec((count, chunk), lambda j, me: (0, j ^ (me[0] >> 2)))
    return call(
        functools.partial(owner_grads_kernel, block, x_next), "owner_grads", [(shape, BF16), (shape, F32)],
        2_700_000_000, 44, grid=(half // chunk,),
        in_specs=[columns, columns, whole(right.shape), pl.BlockSpec((count, width), lambda j, me: (0, at_core))],
        out_specs=[spec, spec], scalars=1, scratch=[pltpu.VMEM((chunk, width), F32)],
    )(me, left, left_core, right, right_core)


def place_kernel(extra, me_ref, rows_ref, near_ref, *refs):
    query_refs, (grads_ref, out_ref, term_ref, all_ref) = refs[:-4], refs[-4:]
    count, width = grads_ref.shape
    passage = count - extra
    moved = near_ref.shape[0]
    all_ref[:passage, :] = rows_ref[:passage, :]
    all_ref[passage + moved :, :] = rows_ref[passage:, :]

    @pl.when(me_ref[1] == moved // extra)
    def _():
        all_ref[passage : passage + extra, :] = near_ref[:extra, :]
        for at, query_ref in enumerate(query_refs):
            begin = passage + extra * (at + 1)
            all_ref[begin : begin + extra, :] = query_ref[...]

    @pl.when(me_ref[1] != moved // extra)
    def _():
        all_ref[passage : passage + moved, :] = near_ref[...]

    rows = pl.ds(pl.multiple_of(me_ref[1] * extra, extra), count)
    grads_ref[...] = all_ref[rows, :width]
    out_ref[...] = all_ref[rows, width : 2 * width]
    term_ref[...] = mm(jnp.ones((8, 128), BF16), all_ref[rows, 2 * width :], NT)


def place_rows(me, rows, sent, extra, width):
    count = rows.shape[0]
    outs = [((count, width), BF16), ((count, width), BF16), ((8, count), F32)]
    return call(
        functools.partial(place_kernel, extra), "place_rows", outs, 1_000_000, 24,
        in_specs=[SMEM] + [VMEM] * (1 + len(sent)),
        scratch=[pltpu.VMEM((count + sent[0].shape[0], rows.shape[1]), BF16)],
    )(me, rows, *sent)


def swap(array, axis, bit, name="swap"):
    size = lax.axis_size(axis)
    with jax.named_scope(name + "_" + axis + str(bit)):
        return lax.ppermute(array, axis, [(at, at ^ bit) for at in range(size)])


def bits_of(size):
    return [1 << at for at in range(size.bit_length() - 1)]


def shift(rows, extra):
    heads = lax.axis_size("head")
    me = lax.axis_index("head")
    count = rows.shape[0]
    moved = extra * (heads - 1)
    begin = count - moved - jnp.where(me == heads - 1, extra, 0)
    return lax.dynamic_slice_in_dim(rows, begin, moved, 0)


def forth(payload):
    heads = lax.axis_size("head")
    return lax.ppermute(payload, "head", [(at, (at + 1) % heads) for at in range(heads)])


def queries_for(rows, extra, target):
    begin = rows.shape[0] - (lax.axis_size("head") - target) * extra
    return rows[begin : begin + extra]


def aligned(rows, received, sent, extra):
    me = lax.axis_index("head")
    count = rows.shape[0]
    moved = received.shape[0]
    passage = lax.dynamic_slice_in_dim(
        jnp.concatenate([received, rows], 0), moved - extra * me, count - extra, 0
    )
    query = jnp.where(
        me == 0, received[:extra], jnp.where(me == 1, sent[0], jnp.where(me == 2, sent[1], rows[count - extra :]))
    )
    return jnp.concatenate([passage, query], 0)


def back_payloads(rows, extra):
    moved = extra * (lax.axis_size("head") - 1)
    query = rows[rows.shape[0] - extra :]
    payload = jnp.where(
        lax.axis_index("head") == 0, jnp.concatenate([query, rows[: moved - extra]], 0), rows[:moved]
    )
    return payload, query


def send_back(payload):
    heads = lax.axis_size("head")
    return lax.ppermute(payload, "head", [((at + 1) % heads, at) for at in range(heads)])


def with_column(rows, values):
    high = lax.reduce_precision(values, 8, 7)
    rest = values - high
    middle = lax.reduce_precision(rest, 8, 7)
    parts = jnp.stack([high, middle, rest - middle], 1).astype(BF16)
    return jnp.concatenate([rows, jnp.pad(parts, ((0, 0), (0, 125)))], 1)


def after(value, *others):
    return lax.optimization_barrier((*others, value))[-1]


class Scatter:
    def __init__(self, send, keep, sent, names, label):
        self.names, self.label, self.current, self.away = list(names), label, keep, None
        self.received = self.swap(send, sent)

    def swap(self, away, name):
        axis, bit = ("head", 2) if name == "x" else ("dp", int(name[2:]))
        return swap(away, axis, bit, self.label)

    def prepare(self, *before):
        shape = self.current.shape[1:]
        self.received = after(self.received, *before) if before else self.received

        def side(which):
            return self.current[which].reshape(shape) + self.received[which].astype(F32).reshape(shape)

        self.away = side(1).astype(BF16)
        self.current = side(0)
        return self.away

    def step(self, *before):
        if self.away is None:
            self.prepare(*before)
        away = after(self.away, *before) if before else self.away
        self.received, self.away = self.swap(away, self.names.pop(0)), None
        return away

    def result(self):
        return self.current + self.received.astype(F32)


class Total:
    def __init__(self, keep, far, steps, label):
        self.label, self.keep, self.far, self.steps = label, keep, far, list(steps)
        self.received, self.kind = None, None
        dp = [name for name in steps if name != "x"]
        self.steps += dp[:-1][::-1]
        self.middle = dp[-1]
        self.backs = len(dp) - 1
        self.me = lax.axis_index("dp")

    def merged(self):
        kind, received = self.kind, self.received
        if kind == "back":
            return jnp.where(
                self.mine,
                jnp.concatenate([received, self.keep], 0),
                jnp.concatenate([self.keep, received], 0),
            )
        if kind == "both":
            rows = self.keep.shape[0]
            self.far = self.far + received[:rows].astype(F32)
            received = received[rows:]
        if kind is not None:
            return self.keep.astype(F32) + received.astype(F32)
        return self.keep

    def step(self, *before):
        name = self.steps.pop(0)
        if before:
            tied = [value for value in (self.keep, self.far, self.received) if value is not None]
            tied = list(lax.optimization_barrier((*before, *tied))[len(before) :])
            self.keep = tied.pop(0)
            if self.far is not None:
                self.far = tied.pop(0)
            if self.received is not None:
                self.received = tied.pop(0)
        block = self.merged()
        if name == "x":
            away, self.far = self.far.astype(BF16), None
            self.keep, self.kind = block, "add"
            self.received = swap(away, "head", 2, self.label)
            return away
        bit = int(name[2:])
        self.mine = (self.me & bit) != 0
        if name == self.middle:
            away = self.keep = block.astype(BF16)
            self.kind = "add"
        elif len(self.steps) < self.backs:
            away = self.keep = block.astype(BF16)
            self.kind = "back"
        else:
            half = block.shape[0] // 2
            side = self.mine.astype(jnp.int32)

            def part(array, which):
                return lax.dynamic_slice_in_dim(array, which * half, half, 0)

            away = part(block, 1 - side).astype(BF16)
            self.keep, self.kind = part(block, side), "add"
            if self.far is not None:
                away = jnp.concatenate([part(self.far, 1 - side).astype(BF16), away], 0)
                self.far, self.kind = part(self.far, side), "both"
        self.received = swap(away, "dp", bit, self.label)
        return away


TAIL = "abdiababidabpdatbisu"


def shards(
    tokens, w_qkv, b_qv, w_out, b_out, gain_one, shift_one, w_in, b_in, w_down, b_down,
    gain_two, shift_two, w_term, b_term, pass_len, query_len, grad_out, grad_term,
):
    n_dp, n_head = lax.axis_size("dp"), lax.axis_size("head")
    me, me_dp = lax.axis_index("head"), lax.axis_index("dp")
    width = tokens.shape[1]
    wide = w_qkv.shape[2]
    hidden = w_in.shape[1]
    extra = query_len.shape[0] * QLEN // n_head
    block = hidden // (n_dp * n_head)
    owners = n_head == 4 and block == 96
    chunk = 768

    shifted = shift(tokens, extra)
    weights = after(w_qkv, shifted)
    bias = jnp.zeros((4, 16, width), BF16).at[0, 0, :wide].set(b_qv[0]).at[2, 0, :wide].set(b_qv[1])
    own = jnp.concatenate([jnp.concatenate([weights.transpose(0, 2, 1), w_out[None]], 0), bias], 1)
    high = own.shape[1]
    turn = me_dp & 3
    received = forth(shifted)
    query = lax.ppermute(queries_for(tokens, extra, 1), "head", [(n_head - 1, 1)])
    pieces = [swap(lax.dynamic_index_in_dim(own, turn, 0, keepdims=False), "head", 2, "weights")]
    own = own.reshape(-1, width)
    beside = jnp.concatenate([own, queries_for(tokens, extra, 2)], 0)
    second = lax.dynamic_slice_in_dim(after(own, beside), (turn ^ 3) * high, high, 0)
    beside = swap(beside, "head", 1, "weights")
    last = swap(second, "head", 2, "weights")
    rows = aligned(tokens, received, (query, beside[4 * high :]), extra)
    packs = [own, beside]
    counts = (pass_len.shape[0], query_len.shape[0])
    near = jnp.concatenate(
        [
            jnp.stack([jnp.zeros_like(me), 3 + me, 3 + counts[0] + me * (counts[1] // n_head)]).astype(jnp.int32),
            pass_len, query_len,
        ]
    )
    distant = jnp.concatenate([turn.astype(jnp.int32)[None], near[1:]])
    core = (me & 1).astype(jnp.int32)[None]
    scalars = jnp.concatenate([jnp.zeros((2,), jnp.int32), distant[:1], distant[:1], core])
    digits = np.zeros((width,), np.float32)
    digits[:36] = 2.0 ** (np.arange(36) - 11)
    params = jnp.concatenate(
        [b_out, gain_one, shift_one, b_down, gain_two, shift_two, w_term, b_term]
        + [jnp.zeros((width - 1,), BF16), jnp.asarray(digits, BF16), jnp.zeros((7 * width,), BF16)]
    ).reshape(16, width)
    place = jnp.stack([me_dp, me]).astype(jnp.int32)

    saved = [attend(near, rows, packs[0], wide)]
    pieces = [after(pieces[0], saved[0][1])]
    pieces += [swap(pieces[0], "dp", 1, "weights"), swap(pieces[0], "dp", 2, "weights"), last]
    rows_then, packs[1] = lax.optimization_barrier((after(rows, saved[0][1]), packs[1]))
    saved.append(attend(near, rows_then, packs[1], wide))
    pieces = lax.optimization_barrier((saved[1][1], *pieces))[1:]
    packs.append(jnp.concatenate(pieces, 0))
    packs.append(swap(packs[2], "head", 1, "weights"))
    with_terms = with_column(after(grad_out, saved[0][1]), grad_term)
    with_terms = after(with_terms, saved[1][1])
    given = [forth(shift(with_terms, extra))] + [
        lax.ppermute(queries_for(with_terms, extra, target), "head", [(n_head - 1, target)]) for target in (1, 2)
    ]
    saved.append(attend(distant, rows, packs[2], wide))
    rows_then, packs[3] = lax.optimization_barrier((after(rows, saved[2][1]), packs[3]))
    saved.append(attend(distant, rows_then, packs[3], wide))
    given = lax.optimization_barrier((saved[3][1], *given))[1:]
    grads_in = aligned(with_terms, given[0], given[1:], extra)
    split = block if owners else hidden
    r1, a1, mine, given, slope, out_rows, db, dr2, vec = forward(
        scalars, rows, params, grads_in, b_in[None], w_in, w_down, [m for _, m, _ in saved], packs, split, chunk
    )
    given_core = swap(given, "head", 1, "given")
    dr1, da, vec, dz_mine, dz_other = backward(core, db, slope, w_down, w_in, r1, dr2, params, vec, split)
    names = ["dp%d" % bit for bit in bits_of(n_dp)]
    at_core = hidden // 2 // width
    if owners:
        dz_core = swap(dz_other, "head", 1, "inner")
        place, given_core = lax.optimization_barrier((after(place, da), given_core))
        send, keep = owner_grads(place, mine, given_core, db, given_core, at_core, block, True)
        down = Scatter(send, keep, names[1], ["x", names[0]] + names[2:], "down")
        da = after(da, send)
    else:
        both = ("dp", "head")
        grad_w_down = lax.psum_scatter(mm(mine, db, TN), both, scatter_dimension=0, tiled=True)
        grad_w_in = lax.psum_scatter(mm(dz_mine, a1, TN), both, scatter_dimension=0, tiled=True)

    def back(part, da):
        qkv, mixed, total = saved[part]
        return attend_back(distant if part > 1 else near, da, qkv, total, mixed, vec, packs[part])

    def heads(part, own, core, dtype):
        return head_grads(rows, given_core, at_core + 2, own, core, vec, dtype)

    grads, then = {}, da
    for part in (3, 2, 1, 0):
        grads[part] = back(part, after(da, then))
        then = grads[part]
    far_core, near_core = swap(grads[3], "head", 1, "far"), swap(grads[1], "head", 1, "near")
    far_then = grads[2]
    if owners:
        place, dz_core = lax.optimization_barrier((after(place, then), dz_core))
        send, keep = owner_grads(place, dz_mine, dz_core, a1, given_core, at_core + 1, block, False)
        inner = Scatter(send, keep, names[1], [names[0], "x"] + names[2:], "inner")
        far_then, down.received = lax.optimization_barrier((after(far_then, send), down.received))
    far_then, far_core, near_core = lax.optimization_barrier((far_then, far_core, near_core))
    far_sum = heads(2, far_then, far_core, BF16)
    near_sum = heads(0, after(grads[0], far_sum[1]), near_core, F32)
    steps = ["dp%d" % bit for bit in bits_of(n_dp)]
    totals = [
        Total(near_sum[1], far_sum[1], ["x"] + steps, "first"),
        Total(near_sum[0], far_sum[0], steps[:1] + ["x"] + steps[1:], "second"),
    ]
    totals[0].step()
    then = totals[1].step()
    combined = rows_back(scalars, after(dr1, then), out_rows, [grads[part] for part in range(n_head)], packs)
    done = [combined]

    def step(one):
        done[:] = [one.step(*done)]

    scatters = {"d": down, "i": inner} if owners else {}
    for item in TAIL:
        if item in "ab":
            total = totals["ab".index(item)]
            if total.steps:
                step(total)
        elif item == "t":
            payloads = lax.optimization_barrier((*done, *payloads))[len(done) :]
            shifted = [send_back(payloads[0])]
        elif item == "s":
            query = lax.optimization_barrier((*done, payloads[1]))[-1]
            shifted.append(lax.ppermute(query, "head", [(1, n_head - 1)]))
        elif item == "p":
            payloads = back_payloads(after(combined, *done), extra)
        elif item == "w":
            shifted = lax.optimization_barrier((*done, *shifted))[len(done) :]
            done[:] = shifted[1:2]
        elif item in "ej":
            one = scatters.get("di"["ej".index(item)])
            if one and one.names:
                done[:] = [one.prepare(*done)]
        elif item == "u":
            shifted[0] = after(shifted[0], *done)
        elif item in scatters and scatters[item].names:
            step(scatters[item])
    for total in totals:
        while total.steps:
            step(total)
    for one in scatters.values():
        while one.names:
            step(one)
    last = totals[0].merged().astype(F32)
    cut = near_sum[0].shape[0]
    grad_w_out = last[3 * wide - cut : 4 * wide - cut]
    bias_row, sums = last[4 * wide - cut], last[4 * wide - cut + 16 : 4 * wide - cut + 32]
    grad_b_qv = jnp.stack([bias_row[:wide], bias_row[2 * wide : 3 * wide]])
    grad_b_term = jnp.sum(sums[4, :36] * jnp.asarray(2.0 ** (11 - np.arange(36)), F32))[None]
    grad_b_in = sums[11:15].reshape(-1)
    done = [grad_w_out, grad_b_qv, grad_b_term, grad_b_in, sums[10]]
    shifted.append(lax.ppermute(after(payloads[1], grad_w_out), "head", [(2, n_head - 1)]))
    if owners:
        inner.received = after(inner.received, *done)
        grad_w_down, grad_w_in = down.result().reshape(block, width), inner.result().reshape(block, width)
        done = [grad_w_in]
    shifted[0] = after(shifted[0], *done)
    shifted = lax.optimization_barrier(tuple(shifted))
    grad_tokens, out, term = place_rows(place, combined, shifted, extra, width)
    totals[1].received = after(totals[1].received, grad_tokens)
    total = jnp.concatenate([totals[1].merged().astype(F32), last[: 3 * wide - cut]], 0)
    grad_w_qkv = total.reshape(3, wide, width).transpose(0, 2, 1)
    return (
        out, term[0], grad_tokens, grad_w_qkv, grad_b_qv, grad_w_out, sums[10], sums[8],
        sums[9], grad_w_in.T, grad_b_in, grad_w_down, sums[2], sums[0], sums[1],
        sums[3], grad_b_term,
    )


def solution(mesh):
    both = ("dp", "head")
    placed = (
        P(both, None), P(None, None, "head"), P(None, "head"), P("head", None),
        P(), P(), P(), P(), P(), P(), P(), P(), P(), P(), P(),
        P("dp"), P("dp"), P(both, None), P(both),
    )
    return jax.shard_map(
        shards,
        mesh=mesh,
        in_specs=placed,
        out_specs=(
            P(both, None), P(both), P(both, None), P(None, None, "head"), P(None, "head"),
            P("head", None), P(), P(), P(), P(None, both), P(), P(both, None),
            P(), P(), P(), P(), P(),
        ),
        check_vma=False,
    )
```

```python
import functools
import math

import jax
import jax.numpy as jnp
import numpy as np
from jax import lax
from jax.experimental import pallas as pl
from jax.experimental.pallas import tpu as pltpu
from jax.sharding import PartitionSpec as P

HEAD_DIM = 64
PLEN = 512
QLEN = 32
F32 = jnp.float32
BF16 = jnp.bfloat16
NN = (((1,), (0,)), ((), ()))
NT = (((1,), (1,)), ((), ()))
TN = (((0,), (0,)), ((), ()))
SCALE = 1.0 / math.sqrt(HEAD_DIM)
MIB = 1024 * 1024
CUT = 384
SMEM = pl.BlockSpec(memory_space=pltpu.SMEM)
VMEM = pl.BlockSpec(memory_space=pltpu.VMEM)


def mm(left, right, dims):
    return lax.dot_general(left, right, dims, preferred_element_type=F32)


def whole(shape):
    zeros = (0,) * len(shape)
    return pl.BlockSpec(shape, lambda *_: zeros)


def call(kernel, name, outs, flops, mib, grid=None, in_specs=None, out_specs=None, scratch=(), scalars=0):
    options = dict(
        out_shape=[jax.ShapeDtypeStruct(shape, dtype) for shape, dtype in outs],
        compiler_params=pltpu.CompilerParams(vmem_limit_bytes=mib * MIB),
        cost_estimate=pl.CostEstimate(flops=flops * 100, bytes_accessed=flops // 5, transcendentals=0),
        name=name,
    )
    if grid is None:
        return pl.pallas_call(
            kernel, in_specs=in_specs, out_specs=[VMEM] * len(outs), scratch_shapes=list(scratch), **options
        )
    spec = pltpu.PrefetchScalarGridSpec(
        num_scalar_prefetch=scalars, grid=grid, in_specs=in_specs, out_specs=out_specs,
        scratch_shapes=list(scratch),
    )
    return pl.pallas_call(kernel, grid_spec=spec, **options)


def masks(lengths_ref, extra):
    long_key = lax.broadcasted_iota(jnp.int32, (PLEN, PLEN), 0)
    key = lax.broadcasted_iota(jnp.int32, (extra, extra), 0)
    row = lax.broadcasted_iota(jnp.int32, (extra, extra), 1)
    short = jnp.zeros((extra, extra), jnp.bool_)
    for at in range(extra // QLEN):
        low, high = at * QLEN, (at + 1) * QLEN
        short = short | (
            (key >= low) & (key < low + lengths_ref[lengths_ref[2] + at]) & (row >= low) & (row < high)
        )
    return long_key < lengths_ref[lengths_ref[1]], short


def attend_kernel(lengths_ref, x_ref, *refs):
    pack_refs, (qkv_ref, mixed_ref, total_ref) = refs[:-3], refs[-3:]
    wide = mixed_ref.shape[1]
    pitch = wide + 16
    count = x_ref.shape[0]
    ones = jnp.ones((16, count), BF16)
    order = lengths_ref[0]
    valids = masks(lengths_ref, count - PLEN)
    total_ref[...] = jnp.zeros_like(total_ref)
    for at, pack_ref in enumerate(pack_refs):
        for member in range(3):
            begin = pl.multiple_of((member ^ order) * pitch, pitch)
            part = mm(pack_ref[pl.ds(begin, wide), :], x_ref[...], NT)
            if member != 1:
                part = part + mm(pack_ref[pl.ds(begin + wide, 16), :wide], ones, TN)
            part = part.astype(BF16)
            qkv_ref[at, member * wide : (member + 1) * wide, :] = part * BF16(SCALE) if member == 0 else part
        for head in range(wide // HEAD_DIM):
            row = head * HEAD_DIM
            for valid, low, high in ((valids[0], 0, PLEN), (valids[1], PLEN, count)):
                query = qkv_ref[at, row : row + HEAD_DIM, low:high]
                keys = qkv_ref[at, wide + row : wide + row + HEAD_DIM, low:high]
                values = qkv_ref[at, 2 * wide + row : 2 * wide + row + HEAD_DIM, low:high]
                scores = jnp.where(valid, mm(keys, query, TN), -1000000000.0)
                top = jnp.max(scores, 0, keepdims=True)
                exponent = jnp.exp(scores - top)
                total = jnp.sum(exponent, 0, keepdims=True)
                shares = (exponent * (1.0 / total)).astype(BF16)
                mixed_ref[at, row : row + HEAD_DIM, low:high] = mm(values, shares, NN).astype(BF16)
                total_ref[at, head : head + 1, low:high] = top + jnp.log(total)


def attend(lengths, x, pack, wide):
    count = x.shape[0]
    outs = [((1, 3 * wide, count), BF16), ((1, wide, count), BF16), ((1, 8, count), F32)]
    return call(attend_kernel, "attend", outs, 1_200_000_000, 44, in_specs=[SMEM] + [VMEM] * 2)(lengths, x, pack)


def attend_back_kernel(lengths_ref, da_ref, qkv_ref, total_ref, mixed_ref, vec_ref, pack_ref, grad_ref):
    wide = mixed_ref.shape[1]
    count, width = da_ref.shape
    valids = masks(lengths_ref, count - PLEN)
    begin = pl.multiple_of((3 ^ lengths_ref[0]) * (wide + 16), wide + 16)
    grad_mixed = mm(pack_ref[pl.ds(begin, wide), :], da_ref[...], NT).astype(BF16)
    grad_ref[: 3 * wide, count:] = jnp.zeros((3 * wide, width - count), BF16)
    grad_ref[3 * wide : 4 * wide, :] = mm(mixed_ref[0], da_ref[...], NN).astype(BF16)
    grad_ref[4 * wide :, :] = vec_ref[...].astype(BF16)
    for head in range(wide // HEAD_DIM):
        row = head * HEAD_DIM
        for valid, low, high in ((valids[0], 0, PLEN), (valids[1], PLEN, count)):
            query = qkv_ref[0, row : row + HEAD_DIM, low:high]
            keys = qkv_ref[0, wide + row : wide + row + HEAD_DIM, low:high]
            values = qkv_ref[0, 2 * wide + row : 2 * wide + row + HEAD_DIM, low:high]
            upper = grad_mixed[row : row + HEAD_DIM, low:high]
            scores = jnp.where(valid, mm(keys, query, TN), -1000000000.0)
            shares = jnp.exp(scores - total_ref[0, head : head + 1, low:high])
            grad_shares = mm(values, upper, TN)
            inner = jnp.sum(shares * grad_shares, 0, keepdims=True)
            grad_scores = (shares * (grad_shares - inner)).astype(BF16)
            grad_ref[2 * wide + row : 2 * wide + row + HEAD_DIM, low:high] = mm(
                upper, shares.astype(BF16), NT
            ).astype(BF16)
            grad_ref[wide + row : wide + row + HEAD_DIM, low:high] = mm(query, grad_scores, NT).astype(BF16)
            grad_ref[row : row + HEAD_DIM, low:high] = (mm(keys, grad_scores, NN) * SCALE).astype(BF16)


def attend_back(lengths, da, qkv, total, mixed, vec, pack):
    _, wide, count = mixed.shape
    width = da.shape[1]
    return call(
        attend_back_kernel, "attend_back", [((4 * wide + vec.shape[0], width), BF16)], 2_000_000_000, 36,
        in_specs=[SMEM] + [VMEM] * 6,
    )(lengths, da, qkv, total, mixed, vec, pack)[0]


def head_grads_kernel(x_ref, x_core_ref, own_ref, core_ref, vec_ref, first_ref, second_ref):
    count = x_ref.shape[0]
    sums = vec_ref.shape[0]
    rows = own_ref.shape[0] - sums
    wide = rows // 4
    cut = first_ref.shape[0]
    dtype = second_ref.dtype
    grads = jnp.concatenate([own_ref[: 3 * wide, :count], core_ref[: 3 * wide, :count]], 1)
    tokens = jnp.concatenate([x_ref[...], x_core_ref[...]], 0)
    first_ref[...] = mm(grads[:cut], tokens, NN).astype(first_ref.dtype)
    second_ref[: 3 * wide - cut, :] = mm(grads[cut:], tokens, NN).astype(dtype)
    second_ref[3 * wide - cut : rows - cut, :] = (
        own_ref[3 * wide : rows].astype(F32) + core_ref[3 * wide : rows].astype(F32)
    ).astype(dtype)
    second_ref[rows - cut :, :] = jnp.zeros((second_ref.shape[0] - rows + cut, second_ref.shape[1]), dtype)
    ones = jnp.ones((16, grads.shape[1]), BF16)
    second_ref[rows - cut : rows - cut + 16, : 3 * wide] = mm(ones, grads, NT).astype(dtype)
    second_ref[rows - cut + 16 : rows - cut + 16 + sums, :] = (
        vec_ref[...] + core_ref[rows:].astype(F32)
    ).astype(dtype)


def head_grads(x, x_core, at_core, own, core, vec, dtype):
    count, width = x.shape
    rows = own.shape[0] - vec.shape[0]
    outs = [((CUT, width), F32), ((rows - CUT + 64, width), dtype)]
    return call(
        head_grads_kernel, "head_grads", outs, 1_500_000_000, 44, grid=(1,),
        in_specs=[
            whole(x.shape), pl.BlockSpec((count, width), lambda _: (0, at_core)), whole(own.shape),
            whole(core.shape), whole(vec.shape),
        ],
        out_specs=[whole(shape) for shape, _ in outs],
    )(x, x_core, own, core, vec)


def rows_kernel(wide, orders_ref, base_ref, beside_ref, *refs):
    out_ref = refs[-1]
    parts = (len(refs) - 1) // 2
    width = base_ref.shape[1]
    total = base_ref[...]
    for part in range(parts):
        grad_ref, pack_ref = refs[part], refs[parts + part]
        high = wide + 16
        for member in range(3):
            begin = pl.multiple_of((member ^ orders_ref[part]) * high, high)
            grad = grad_ref[member * wide : (member + 1) * wide, : base_ref.shape[0]]
            total = total + mm(grad, pack_ref[pl.ds(begin, wide), :], TN)
    out_ref[:, :width] = total.astype(BF16)
    out_ref[:, width:] = beside_ref[...]


def rows_back(orders, base, beside, grads, packs):
    shape = (base.shape[0], base.shape[1] + beside.shape[1])
    return call(
        functools.partial(rows_kernel, grads[0].shape[0] // 4 // 16 * 16), "rows_back", [(shape, BF16)], 2_000_000_000, 60, in_specs=[SMEM] + [VMEM] * (2 + 2 * len(packs)),
    )(orders, base, beside, *grads, *packs)[0]


def normed(hidden):
    center = hidden - jnp.mean(hidden, -1, keepdims=True)
    inverse = lax.rsqrt(jnp.mean(center * center, -1, keepdims=True) + 1e-06)
    return center * inverse, inverse


def norm_back(grad, unit, inverse, gain):
    grad_unit = grad * gain
    return inverse * (
        grad_unit
        - jnp.mean(grad_unit, -1, keepdims=True)
        - unit * jnp.mean(grad_unit * unit, -1, keepdims=True)
    )


def column_sum(values):
    return jnp.sum(values, 0, keepdims=True)


def put_halves(values, block, core, mine_ref, other_ref):
    if values.shape[1] < 2 * block:
        mine_ref[...] = values
        return
    sides = [
        jnp.concatenate(
            [values[:, at : at + block] for at in range(side * block, values.shape[1], 2 * block)], 1
        )
        for side in (0, 1)
    ]
    mine_ref[...] = jnp.where(core == 0, sides[0], sides[1])
    other_ref[...] = jnp.where(core == 0, sides[1], sides[0])


def forward_kernel(parts, block, scalars_ref, *refs):
    x_ref, params_ref, grads_ref, bias_ref, w_in_ref, w_down_ref = refs[:6]
    mixed_refs = refs[6 : 6 + parts]
    out_refs = refs[6 + parts : 6 + 2 * parts]
    r1_ref, a1_ref, mine_ref, pass_ref, slope_ref, out_ref, db_ref, dr2_ref, vec_ref = refs[6 + 2 * parts : -2]
    first_ref, sum_ref = refs[-2:]
    half_width = pass_ref.shape[1] - 3 * x_ref.shape[1]
    step, steps = pl.program_id(0), pl.num_programs(0)
    width = x_ref.shape[1]

    def param(at):
        return params_ref[at : at + 1, :].astype(F32)

    @pl.when(step == 0)
    def _():
        total = x_ref[...].astype(F32) + param(0)
        for part in range(parts):
            total = total + mm(mixed_refs[part][0], out_refs[part][...], TN)
        r1_ref[...] = total
        unit, _ = normed(total)
        first = unit * param(1) + param(2)
        first_ref[...] = first
        a1_ref[...] = first.astype(BF16)
        pass_ref[:, half_width + width : half_width + 2 * width] = first.astype(BF16)
        pass_ref[:, half_width + 2 * width :] = x_ref[...]
        sum_ref[...] = jnp.zeros_like(sum_ref)

    inner = mm(a1_ref[...], w_in_ref[...], NN) + bias_ref[...].astype(F32)
    square = inner * inner
    factor = math.sqrt(2.0 / math.pi)
    tanh = jnp.tanh(inner * (factor + (factor * 0.044715) * square))
    half = 0.5 + 0.5 * tanh
    active = (inner * half).astype(BF16)
    share = active.shape[1] // 2
    place = pl.ds(pl.multiple_of(step * share, share), share)
    put_halves(active, block, scalars_ref[parts], mine_ref, pass_ref.at[:, place])
    slope_ref[...] = half + inner * (0.5 - 0.5 * tanh * tanh) * (factor + (3 * factor * 0.044715) * square)
    sum_ref[...] += mm(active, w_down_ref[...], NN)

    @pl.when(step == steps - 1)
    def _():
        unit, inverse = normed(first_ref[...] + sum_ref[...] + param(3))
        gain = param(4)
        second = unit * gain + param(5)
        weight = param(6)
        logit = jnp.sum(second * weight, -1, keepdims=True) + params_ref[7:8, 0:1].astype(F32)
        term = jnp.maximum(logit, 0.0) + jnp.log1p(jnp.exp(-jnp.abs(logit)))
        sigmoid = 1.0 / (1.0 + jnp.exp(-logit))
        lane = lax.broadcasted_iota(jnp.int32, (term.shape[0], 128), 1)
        high = term.astype(BF16).astype(F32)
        middle = (term - high).astype(BF16).astype(F32)
        rest = term - high - middle
        tail = jnp.where(lane == 0, high, jnp.where(lane == 1, middle, jnp.where(lane == 2, rest, 0.0)))
        out_ref[:, :width] = second.astype(BF16)
        out_ref[:, width:] = tail.astype(BF16)
        grad_term = jnp.sum(grads_ref[:, width:].astype(F32), -1, keepdims=True)
        grad_logit = grad_term * sigmoid
        grad = grads_ref[:, :width].astype(F32) + grad_logit * weight
        back = norm_back(grad, unit, inverse, gain)
        db_ref[...] = back.astype(BF16)
        pass_ref[:, half_width : half_width + width] = back.astype(BF16)
        dr2_ref[...] = back
        vec_ref[...] = jnp.zeros_like(vec_ref)
        vec_ref[0:1, :] = column_sum(grad * unit)
        vec_ref[1:2, :] = column_sum(grad)
        vec_ref[2:3, :] = column_sum(back)
        vec_ref[3:4, :] = column_sum(grad_logit * second)
        scalar = jnp.broadcast_to(column_sum(grad_logit), (1, width))
        scaled = jnp.floor(jnp.abs(scalar) * param(8))
        digit = scaled - 2.0 * jnp.floor(0.5 * scaled)
        vec_ref[4:5, :] = jnp.where(scalar < 0, -digit, digit)


def forward(scalars, x, params, grads, b_in, w_in, w_down, mixed, packs, block, chunk):
    count, width = x.shape
    hidden = w_in.shape[1]
    wide = mixed[0].shape[1]
    parts = len(packs)
    specs = [
        whole(x.shape), whole(params.shape), whole(grads.shape),
        pl.BlockSpec((1, chunk), lambda j, o: (0, j)),
        pl.BlockSpec((width, chunk), lambda j, o: (0, j)),
        pl.BlockSpec((chunk, width), lambda j, o: (j, 0)),
    ]
    mixed = [(array, at) for array in mixed for at in range(array.shape[0])]
    specs += [
        pl.BlockSpec((1, wide, count), functools.partial(lambda at, j, o: (at, 0, 0), at)) for _, at in mixed
    ]
    specs += [
        pl.BlockSpec(
            (pl.Element(wide), pl.Element(width)),
            functools.partial(lambda part, j, o: ((3 ^ o[part]) * (wide + 16), 0), part),
        )
        for part in range(parts)
    ]
    share = 2 if chunk >= 2 * block else 1
    outs = [
        ((count, width), F32), ((count, width), BF16), ((count, hidden // share), BF16),
        ((count, hidden // 2 + 3 * width), BF16), ((count, hidden), F32),
        ((count, width + 128), BF16), ((count, width), BF16), ((count, width), F32), ((8, width), F32),
    ]
    out_specs = [whole(s) for s, _ in outs]
    out_specs[2] = pl.BlockSpec((count, chunk // share), lambda j, o: (0, j))
    out_specs[4] = pl.BlockSpec((count, chunk), lambda j, o: (0, j))
    return call(
        functools.partial(forward_kernel, parts, block), "forward", outs, 6_200_000_000, 44,
        grid=(hidden // chunk,), in_specs=specs, out_specs=out_specs, scalars=1,
        scratch=[pltpu.VMEM((count, width), F32), pltpu.VMEM((count, width), F32)],
    )(scalars, x, params, grads, b_in, w_in, w_down, *[array for array, _ in mixed], *packs)


def backward_kernel(
    block, scalars_ref, db_ref, slope_ref, w_down_ref, w_in_ref, r1_ref, dr2_ref, params_ref, vec_ref,
    dr1_ref, da_ref, out_vec_ref, mine_ref, other_ref, sum_ref
):
    step, steps = pl.program_id(0), pl.num_programs(0)

    @pl.when(step == 0)
    def _():
        sum_ref[...] = dr2_ref[...]
        out_vec_ref[:8, :] = vec_ref[...]
        out_vec_ref[8:, :] = jnp.zeros_like(vec_ref)

    grad_inner = mm(db_ref[...], w_down_ref[...], NT) * slope_ref[...]
    out_vec_ref[pl.ds(11 + step, 1), :] = column_sum(grad_inner)
    low = grad_inner.astype(BF16)
    put_halves(low, block, scalars_ref[0], mine_ref, other_ref)
    sum_ref[...] += mm(low, w_in_ref[...], NT)

    @pl.when(step == steps - 1)
    def _():
        grad = sum_ref[...]
        unit, inverse = normed(r1_ref[...])
        back = norm_back(grad, unit, inverse, params_ref[1:2, :].astype(F32))
        dr1_ref[...] = back
        da_ref[...] = back.astype(BF16)
        out_vec_ref[8:9, :] = column_sum(grad * unit)
        out_vec_ref[9:10, :] = column_sum(grad)
        out_vec_ref[10:11, :] = column_sum(back)


def backward(scalars, db, slope, w_down, w_in, r1, dr2, params, vec, block):
    count, width = db.shape
    hidden = w_in.shape[1]
    chunk = width
    share = 2 if chunk >= 2 * block else 1
    outs = [
        ((count, width), F32), ((count, width), BF16), ((16, width), F32),
        ((count, hidden // share), BF16), ((count, hidden // 2), BF16),
    ]
    out_specs = [whole(s) for s, _ in outs]
    out_specs[3] = pl.BlockSpec((count, chunk // share), lambda j, o: (0, j))
    out_specs[4] = pl.BlockSpec((count, chunk // 2), lambda j, o: (0, j))
    return call(
        functools.partial(backward_kernel, block), "backward", outs, 5_500_000_000, 44, grid=(hidden // chunk,),
        in_specs=[
            whole(db.shape),
            pl.BlockSpec((count, chunk), lambda j, o: (0, j)),
            pl.BlockSpec((chunk, width), lambda j, o: (j, 0)),
            pl.BlockSpec((width, chunk), lambda j, o: (0, j)),
            whole(r1.shape), whole(dr2.shape), whole(params.shape), whole(vec.shape),
        ],
        out_specs=out_specs, scalars=1, scratch=[pltpu.VMEM((count, width), F32)],
    )(scalars, db, slope, w_down, w_in, r1, dr2, params, vec)


def owner_grads_kernel(block, x_next, me_ref, left_ref, left_core_ref, right_ref, right_core_ref, send_ref, keep_ref, tile_ref):
    tile_ref[...] = mm(
        jnp.concatenate([left_ref[...], left_core_ref[...]], 0),
        jnp.concatenate([right_ref[...], right_core_ref[...]], 0),
        TN,
    )
    low = me_ref[0] & 3
    far = me_ref[1] >> 1
    for at in range(4):
        y, z = (at ^ low) & 1, (at ^ low) >> 1
        for x in (0, 1):
            begin = pl.multiple_of(2 * block * at + block * (far ^ x), block)
            rows = tile_ref[pl.ds(begin, block), :]
            place = (x, y, 0) if x_next else (y, x, 0)

            @pl.when(z == 1)
            def _():
                send_ref[place] = rows.astype(BF16)

            @pl.when(z == 0)
            def _():
                keep_ref[place] = rows.astype(BF16)


def owner_grads(me, left, left_core, right, right_core, at_core, block, x_next):
    count, half = left.shape
    width = right.shape[1]
    n_dp = half // (2 * block)
    chunk = 8 * block
    shape = (2, 2, n_dp // 4, block, width)
    spec = pl.BlockSpec((2, 2, 1, block, width), lambda j, me: (0, 0, j, 0, 0))
    columns = pl.BlockSpec((count, chunk), lambda j, me: (0, j ^ (me[0] >> 2)))
    return call(
        functools.partial(owner_grads_kernel, block, x_next), "owner_grads", [(shape, BF16), (shape, BF16)],
        2_700_000_000, 44, grid=(half // chunk,),
        in_specs=[columns, columns, whole(right.shape), pl.BlockSpec((count, width), lambda j, me: (0, at_core))],
        out_specs=[spec, spec], scalars=1, scratch=[pltpu.VMEM((chunk, width), F32)],
    )(me, left, left_core, right, right_core)


def place_kernel(extra, me_ref, rows_ref, near_ref, *refs):
    query_refs, (grads_ref, out_ref, term_ref, all_ref) = refs[:-4], refs[-4:]
    count, width = grads_ref.shape
    passage = count - extra
    moved = near_ref.shape[0]
    all_ref[:passage, :] = rows_ref[:passage, :]
    all_ref[passage + moved :, :] = rows_ref[passage:, :]

    @pl.when(me_ref[1] == moved // extra)
    def _():
        all_ref[passage : passage + extra, :] = near_ref[:extra, :]
        for at, query_ref in enumerate(query_refs):
            begin = passage + extra * (at + 1)
            all_ref[begin : begin + extra, :] = query_ref[...]

    @pl.when(me_ref[1] != moved // extra)
    def _():
        all_ref[passage : passage + moved, :] = near_ref[...]

    rows = pl.ds(pl.multiple_of(me_ref[1] * extra, extra), count)
    grads_ref[...] = all_ref[rows, :width]
    out_ref[...] = all_ref[rows, width : 2 * width]
    term_ref[...] = mm(jnp.ones((8, 128), BF16), all_ref[rows, 2 * width :], NT)


def place_rows(me, rows, sent, extra, width):
    count = rows.shape[0]
    outs = [((count, width), BF16), ((count, width), BF16), ((8, count), F32)]
    return call(
        functools.partial(place_kernel, extra), "place_rows", outs, 1_000_000, 24,
        in_specs=[SMEM] + [VMEM] * (1 + len(sent)),
        scratch=[pltpu.VMEM((count + sent[0].shape[0], rows.shape[1]), BF16)],
    )(me, rows, *sent)


def swap(array, axis, bit, name="swap"):
    size = lax.axis_size(axis)
    with jax.named_scope(name + "_" + axis + str(bit)):
        return lax.ppermute(array, axis, [(at, at ^ bit) for at in range(size)])


def bits_of(size):
    return [1 << at for at in range(size.bit_length() - 1)]


def shift(rows, extra):
    heads = lax.axis_size("head")
    me = lax.axis_index("head")
    count = rows.shape[0]
    moved = extra * (heads - 1)
    begin = count - moved - jnp.where(me == heads - 1, extra, 0)
    return lax.dynamic_slice_in_dim(rows, begin, moved, 0)


def forth(payload):
    heads = lax.axis_size("head")
    return lax.ppermute(payload, "head", [(at, (at + 1) % heads) for at in range(heads)])


def queries_for(rows, extra, target):
    begin = rows.shape[0] - (lax.axis_size("head") - target) * extra
    return rows[begin : begin + extra]


def aligned(rows, received, sent, extra):
    me = lax.axis_index("head")
    count = rows.shape[0]
    moved = received.shape[0]
    passage = lax.dynamic_slice_in_dim(
        jnp.concatenate([received, rows], 0), moved - extra * me, count - extra, 0
    )
    query = jnp.where(
        me == 0, received[:extra], jnp.where(me == 1, sent[0], jnp.where(me == 2, sent[1], rows[count - extra :]))
    )
    return jnp.concatenate([passage, query], 0)


def back_payloads(rows, extra):
    moved = extra * (lax.axis_size("head") - 1)
    query = rows[rows.shape[0] - extra :]
    payload = jnp.where(
        lax.axis_index("head") == 0, jnp.concatenate([query, rows[: moved - extra]], 0), rows[:moved]
    )
    return payload, query


def send_back(payload):
    heads = lax.axis_size("head")
    return lax.ppermute(payload, "head", [((at + 1) % heads, at) for at in range(heads)])


def with_column(rows, values):
    high = lax.reduce_precision(values, 8, 7)
    rest = values - high
    middle = lax.reduce_precision(rest, 8, 7)
    parts = jnp.stack([high, middle, rest - middle], 1).astype(BF16)
    return jnp.concatenate([rows, jnp.pad(parts, ((0, 0), (0, 125)))], 1)


def after(value, *others):
    return lax.optimization_barrier((*others, value))[-1]


class Scatter:
    def __init__(self, send, keep, sent, names, label):
        self.names, self.label, self.current, self.away = list(names), label, keep, None
        self.received = self.swap(send, sent)

    def swap(self, away, name):
        axis, bit = ("head", 2) if name == "x" else ("dp", int(name[2:]))
        return swap(away, axis, bit, self.label)

    def prepare(self, *before):
        shape = self.current.shape[1:]
        self.received = after(self.received, *before) if before else self.received

        def side(which):
            return self.current[which].astype(F32).reshape(shape) + self.received[which].astype(F32).reshape(shape)

        self.away = side(1).astype(BF16)
        self.current = side(0)
        return self.away

    def step(self, *before):
        if self.away is None:
            self.prepare(*before)
        away = after(self.away, *before) if before else self.away
        self.received, self.away = self.swap(away, self.names.pop(0)), None
        return away

    def result(self):
        return self.current + self.received.astype(F32)


class Total:
    def __init__(self, keep, far, steps, label):
        self.label, self.keep, self.far, self.steps = label, keep, far, list(steps)
        self.received, self.kind = None, None
        dp = [name for name in steps if name != "x"]
        self.steps += dp[:-1][::-1]
        self.middle = dp[-1]
        self.backs = len(dp) - 1
        self.me = lax.axis_index("dp")

    def merged(self):
        kind, received = self.kind, self.received
        if kind == "back":
            return jnp.where(
                self.mine,
                jnp.concatenate([received, self.keep], 0),
                jnp.concatenate([self.keep, received], 0),
            )
        if kind == "both":
            rows = self.keep.shape[0]
            self.far = self.far + received[:rows].astype(F32)
            received = received[rows:]
        if kind is not None:
            return self.keep.astype(F32) + received.astype(F32)
        return self.keep

    def step(self, *before):
        name = self.steps.pop(0)
        if before:
            tied = [value for value in (self.keep, self.far, self.received) if value is not None]
            tied = list(lax.optimization_barrier((*before, *tied))[len(before) :])
            self.keep = tied.pop(0)
            if self.far is not None:
                self.far = tied.pop(0)
            if self.received is not None:
                self.received = tied.pop(0)
        block = self.merged()
        if name == "x":
            away, self.far = self.far.astype(BF16), None
            self.keep, self.kind = block, "add"
            self.received = swap(away, "head", 2, self.label)
            return away
        bit = int(name[2:])
        self.mine = (self.me & bit) != 0
        if name == self.middle:
            away = self.keep = block.astype(BF16)
            self.kind = "add"
        elif len(self.steps) < self.backs:
            away = self.keep = block.astype(BF16)
            self.kind = "back"
        else:
            half = block.shape[0] // 2
            side = self.mine.astype(jnp.int32)

            def part(array, which):
                return lax.dynamic_slice_in_dim(array, which * half, half, 0)

            away = part(block, 1 - side).astype(BF16)
            self.keep, self.kind = part(block, side), "add"
            if self.far is not None:
                away = jnp.concatenate([part(self.far, 1 - side).astype(BF16), away], 0)
                self.far, self.kind = part(self.far, side), "both"
        self.received = swap(away, "dp", bit, self.label)
        return away


TAIL = "abdiababidabpdatbisu"


def shards(
    tokens, w_qkv, b_qv, w_out, b_out, gain_one, shift_one, w_in, b_in, w_down, b_down,
    gain_two, shift_two, w_term, b_term, pass_len, query_len, grad_out, grad_term,
):
    n_dp, n_head = lax.axis_size("dp"), lax.axis_size("head")
    me, me_dp = lax.axis_index("head"), lax.axis_index("dp")
    width = tokens.shape[1]
    wide = w_qkv.shape[2]
    hidden = w_in.shape[1]
    extra = query_len.shape[0] * QLEN // n_head
    block = hidden // (n_dp * n_head)
    owners = n_head == 4 and block == 96
    chunk = 768

    shifted = shift(tokens, extra)
    weights = after(w_qkv, shifted)
    bias = jnp.zeros((4, 16, width), BF16).at[0, 0, :wide].set(b_qv[0]).at[2, 0, :wide].set(b_qv[1])
    own = jnp.concatenate([jnp.concatenate([weights.transpose(0, 2, 1), w_out[None]], 0), bias], 1)
    high = own.shape[1]
    turn = me_dp & 3
    received = forth(shifted)
    query = lax.ppermute(queries_for(tokens, extra, 1), "head", [(n_head - 1, 1)])
    pieces = [swap(lax.dynamic_index_in_dim(own, turn, 0, keepdims=False), "head", 2, "weights")]
    own = own.reshape(-1, width)
    beside = jnp.concatenate([own, queries_for(tokens, extra, 2)], 0)
    second = lax.dynamic_slice_in_dim(after(own, beside), (turn ^ 3) * high, high, 0)
    beside = swap(beside, "head", 1, "weights")
    last = swap(second, "head", 2, "weights")
    rows = aligned(tokens, received, (query, beside[4 * high :]), extra)
    packs = [own, beside]
    counts = (pass_len.shape[0], query_len.shape[0])
    near = jnp.concatenate(
        [
            jnp.stack([jnp.zeros_like(me), 3 + me, 3 + counts[0] + me * (counts[1] // n_head)]).astype(jnp.int32),
            pass_len, query_len,
        ]
    )
    distant = jnp.concatenate([turn.astype(jnp.int32)[None], near[1:]])
    core = (me & 1).astype(jnp.int32)[None]
    scalars = jnp.concatenate([jnp.zeros((2,), jnp.int32), distant[:1], distant[:1], core])
    digits = np.zeros((width,), np.float32)
    digits[:36] = 2.0 ** (np.arange(36) - 11)
    params = jnp.concatenate(
        [b_out, gain_one, shift_one, b_down, gain_two, shift_two, w_term, b_term]
        + [jnp.zeros((width - 1,), BF16), jnp.asarray(digits, BF16), jnp.zeros((7 * width,), BF16)]
    ).reshape(16, width)
    place = jnp.stack([me_dp, me]).astype(jnp.int32)

    saved = [attend(near, rows, packs[0], wide)]
    pieces = [after(pieces[0], saved[0][1])]
    pieces += [swap(pieces[0], "dp", 1, "weights"), swap(pieces[0], "dp", 2, "weights"), last]
    rows_then, packs[1] = lax.optimization_barrier((after(rows, saved[0][1]), packs[1]))
    saved.append(attend(near, rows_then, packs[1], wide))
    pieces = lax.optimization_barrier((saved[1][1], *pieces))[1:]
    packs.append(jnp.concatenate(pieces, 0))
    packs.append(swap(packs[2], "head", 1, "weights"))
    with_terms = with_column(after(grad_out, saved[0][1]), grad_term)
    with_terms = after(with_terms, saved[1][1])
    given = [forth(shift(with_terms, extra))] + [
        lax.ppermute(queries_for(with_terms, extra, target), "head", [(n_head - 1, target)]) for target in (1, 2)
    ]
    saved.append(attend(distant, rows, packs[2], wide))
    rows_then, packs[3] = lax.optimization_barrier((after(rows, saved[2][1]), packs[3]))
    saved.append(attend(distant, rows_then, packs[3], wide))
    given = lax.optimization_barrier((saved[3][1], *given))[1:]
    grads_in = aligned(with_terms, given[0], given[1:], extra)
    split = block if owners else hidden
    r1, a1, mine, given, slope, out_rows, db, dr2, vec = forward(
        scalars, rows, params, grads_in, b_in[None], w_in, w_down, [m for _, m, _ in saved], packs, split, chunk
    )
    given_core = swap(given, "head", 1, "given")
    dr1, da, vec, dz_mine, dz_other = backward(core, db, slope, w_down, w_in, r1, dr2, params, vec, split)
    names = ["dp%d" % bit for bit in bits_of(n_dp)]
    at_core = hidden // 2 // width
    if owners:
        dz_core = swap(dz_other, "head", 1, "inner")
        place, given_core = lax.optimization_barrier((after(place, da), given_core))
        send, keep = owner_grads(place, mine, given_core, db, given_core, at_core, block, True)
        down = Scatter(send, keep, names[1], ["x", names[0]] + names[2:], "down")
        da = after(da, send)
    else:
        both = ("dp", "head")
        grad_w_down = lax.psum_scatter(mm(mine, db, TN), both, scatter_dimension=0, tiled=True)
        grad_w_in = lax.psum_scatter(mm(dz_mine, a1, TN), both, scatter_dimension=0, tiled=True)

    def back(part, da):
        qkv, mixed, total = saved[part]
        return attend_back(distant if part > 1 else near, da, qkv, total, mixed, vec, packs[part])

    def heads(part, own, core, dtype):
        return head_grads(rows, given_core, at_core + 2, own, core, vec, dtype)

    grads, then = {}, da
    for part in (3, 2, 1, 0):
        grads[part] = back(part, after(da, then))
        then = grads[part]
    far_core, near_core = swap(grads[3], "head", 1, "far"), swap(grads[1], "head", 1, "near")
    far_then = grads[2]
    if owners:
        place, dz_core = lax.optimization_barrier((after(place, then), dz_core))
        send, keep = owner_grads(place, dz_mine, dz_core, a1, given_core, at_core + 1, block, False)
        inner = Scatter(send, keep, names[1], [names[0], "x"] + names[2:], "inner")
        far_then, down.received = lax.optimization_barrier((after(far_then, send), down.received))
    far_then, far_core, near_core = lax.optimization_barrier((far_then, far_core, near_core))
    far_sum = heads(2, far_then, far_core, BF16)
    near_sum = heads(0, after(grads[0], far_sum[1]), near_core, F32)
    steps = ["dp%d" % bit for bit in bits_of(n_dp)]
    totals = [
        Total(near_sum[1], far_sum[1], ["x"] + steps, "first"),
        Total(near_sum[0], far_sum[0], steps[:1] + ["x"] + steps[1:], "second"),
    ]
    totals[0].step()
    then = totals[1].step()
    combined = rows_back(scalars, after(dr1, then), out_rows, [grads[part] for part in range(n_head)], packs)
    done = [combined]

    def step(one):
        done[:] = [one.step(*done)]

    scatters = {"d": down, "i": inner} if owners else {}
    for item in TAIL:
        if item in "ab":
            total = totals["ab".index(item)]
            if total.steps:
                step(total)
        elif item == "t":
            payloads = lax.optimization_barrier((*done, *payloads))[len(done) :]
            shifted = [send_back(payloads[0])]
        elif item == "s":
            query = lax.optimization_barrier((*done, payloads[1]))[-1]
            shifted.append(lax.ppermute(query, "head", [(1, n_head - 1)]))
        elif item == "p":
            payloads = back_payloads(after(combined, *done), extra)
        elif item == "w":
            shifted = lax.optimization_barrier((*done, *shifted))[len(done) :]
            done[:] = shifted[1:2]
        elif item in "ej":
            one = scatters.get("di"["ej".index(item)])
            if one and one.names:
                done[:] = [one.prepare(*done)]
        elif item == "u":
            shifted[0] = after(shifted[0], *done)
        elif item in scatters and scatters[item].names:
            step(scatters[item])
    for total in totals:
        while total.steps:
            step(total)
    for one in scatters.values():
        while one.names:
            step(one)
    last = totals[0].merged().astype(F32)
    cut = near_sum[0].shape[0]
    grad_w_out = last[3 * wide - cut : 4 * wide - cut]
    bias_row, sums = last[4 * wide - cut], last[4 * wide - cut + 16 : 4 * wide - cut + 32]
    grad_b_qv = jnp.stack([bias_row[:wide], bias_row[2 * wide : 3 * wide]])
    grad_b_term = jnp.sum(sums[4, :36] * jnp.asarray(2.0 ** (11 - np.arange(36)), F32))[None]
    grad_b_in = sums[11:15].reshape(-1)
    done = [grad_w_out, grad_b_qv, grad_b_term, grad_b_in, sums[10]]
    shifted.append(lax.ppermute(after(payloads[1], grad_w_out), "head", [(2, n_head - 1)]))
    if owners:
        inner.received = after(inner.received, *done)
        grad_w_down, grad_w_in = down.result().reshape(block, width), inner.result().reshape(block, width)
        done = [grad_w_in]
    shifted[0] = after(shifted[0], *done)
    shifted = lax.optimization_barrier(tuple(shifted))
    grad_tokens, out, term = place_rows(place, combined, shifted, extra, width)
    totals[1].received = after(totals[1].received, grad_tokens)
    total = jnp.concatenate([totals[1].merged().astype(F32), last[: 3 * wide - cut]], 0)
    grad_w_qkv = total.reshape(3, wide, width).transpose(0, 2, 1)
    return (
        out, term[0], grad_tokens, grad_w_qkv, grad_b_qv, grad_w_out, sums[10], sums[8],
        sums[9], grad_w_in.T, grad_b_in, grad_w_down, sums[2], sums[0], sums[1],
        sums[3], grad_b_term,
    )


def solution(mesh):
    both = ("dp", "head")
    placed = (
        P(both, None), P(None, None, "head"), P(None, "head"), P("head", None),
        P(), P(), P(), P(), P(), P(), P(), P(), P(), P(), P(),
        P("dp"), P("dp"), P(both, None), P(both),
    )
    return jax.shard_map(
        shards,
        mesh=mesh,
        in_specs=placed,
        out_specs=(
            P(both, None), P(both), P(both, None), P(None, None, "head"), P(None, "head"),
            P("head", None), P(), P(), P(), P(None, both), P(), P(both, None),
            P(), P(), P(), P(), P(),
        ),
        check_vma=False,
    )
```
